128 devices in a mesh: role: 2 (over core), dp: 16 (over x, z), mp: 4 (over y).
Axes of the slice: x: 4, y: 4, z: 4, core: 2. Of those that a mesh axis runs over, the one named last changes fastest.
Arguments:
- latents: float32 [2, 16384, 16], P(None, 'dp'), may hold values from -6 to 6
- noise_draws: float32 [2, 16384, 16], P(None, 'dp'), may hold values from -6 to 6
- timesteps: int32 [2, 16384], P(None, 'dp'), may hold values from 0 to 999
- buckets: int32 [2, 16], P(None, 'dp'), may hold values from 0 to 1, as said below
- visible_index: int32 [2, 5120], P(None, 'dp'), may hold values from 0 to 1024, as said below
- patch_embed: float32 [18, 768], replicated, may hold values from -1.5 to 1.5
- patch_embed_first: float32 [18, 768], replicated, may hold values from -2.861023e-06 to 2.861023e-06
- patch_embed_second: float32 [18, 768], replicated, may hold values from 8.892634e-13 to 3.5502911e-12
- attention_in: float32 [2, 768, 12, 192], P('role', 'dp', 'mp'), may hold values from -0.21875 to 0.21875
- attention_in_first: float32 [2, 768, 12, 192], P('role', 'dp', 'mp'), may hold values from -2.861023e-06 to 2.861023e-06
- attention_in_second: float32 [2, 768, 12, 192], P('role', 'dp', 'mp'), may hold values from 8.892634e-13 to 3.5502911e-12
- attention_out: float32 [2, 768, 768], P('role', 'mp', 'dp'), may hold values from -0.625 to 0.625
- attention_out_first: float32 [2, 768, 768], P('role', 'mp', 'dp'), may hold values from -2.861023e-06 to 2.861023e-06
- attention_out_second: float32 [2, 768, 768], P('role', 'mp', 'dp'), may hold values from 8.892634e-13 to 3.5502911e-12
- feedforward_in: float32 [2, 768, 3072], P('role', 'dp', 'mp'), may hold values from -0.21875 to 0.21875
- feedforward_in_first: float32 [2, 768, 3072], P('role', 'dp', 'mp'), may hold values from -2.861023e-06 to 2.861023e-06
- feedforward_in_second: float32 [2, 768, 3072], P('role', 'dp', 'mp'), may hold values from 8.892634e-13 to 3.5502911e-12
- feedforward_out: float32 [2, 3072, 768], P('role', 'mp', 'dp'), may hold values from -0.109375 to 0.109375
- feedforward_out_first: float32 [2, 3072, 768], P('role', 'mp', 'dp'), may hold values from -2.861023e-06 to 2.861023e-06
- feedforward_out_second: float32 [2, 3072, 768], P('role', 'mp', 'dp'), may hold values from 8.892634e-13 to 3.5502911e-12
- block_affine: float32 [2, 6, 768], P('role', None, 'dp')
- block_affine_first: float32 [2, 6, 768], P('role', None, 'dp'), may hold values from -2.861023e-06 to 2.861023e-06
- block_affine_second: float32 [2, 6, 768], P('role', None, 'dp'), may hold values from 8.892634e-13 to 3.5502911e-12
- head_entry: float32 [1067, 1024], P(None, ('role', 'dp', 'mp'))
- head_entry_first: float32 [1067, 1024], P(None, ('role', 'dp', 'mp')), may hold values from -2.861023e-06 to 2.861023e-06
- head_entry_second: float32 [1067, 1024], P(None, ('role', 'dp', 'mp')), may hold values from 8.892634e-13 to 3.5502911e-12
- head_square: float32 [3, 1024, 1024], P(None, None, ('role', 'dp', 'mp')), may hold values from -0.1875 to 0.1875
- head_square_first: float32 [3, 1024, 1024], P(None, None, ('role', 'dp', 'mp')), may hold values from -2.861023e-06 to 2.861023e-06
- head_square_second: float32 [3, 1024, 1024], P(None, None, ('role', 'dp', 'mp')), may hold values from 8.892634e-13 to 3.5502911e-12
- head_modulate: float32 [1024, 5120], P(None, ('role', 'dp', 'mp')), may hold values from -0.1875 to 0.1875
- head_modulate_first: float32 [1024, 5120], P(None, ('role', 'dp', 'mp')), may hold values from -2.861023e-06 to 2.861023e-06
- head_modulate_second: float32 [1024, 5120], P(None, ('role', 'dp', 'mp')), may hold values from 8.892634e-13 to 3.5502911e-12
Outputs:
- total_loss: float32 [], replicated
- gradient_norm: float32 [], replicated
- new_patch_embed_first: float32 [18, 768], replicated
- new_patch_embed_second: float32 [18, 768], replicated
- new_patch_embed: float32 [18, 768], replicated
- new_attention_in_first: float32 [2, 768, 12, 192], P('role', 'dp', 'mp')
- new_attention_in_second: float32 [2, 768, 12, 192], P('role', 'dp', 'mp')
- new_attention_in: float32 [2, 768, 12, 192], P('role', 'dp', 'mp')
- new_attention_out_first: float32 [2, 768, 768], P('role', 'mp', 'dp')
- new_attention_out_second: float32 [2, 768, 768], P('role', 'mp', 'dp')
- new_attention_out: float32 [2, 768, 768], P('role', 'mp', 'dp')
- new_feedforward_in_first: float32 [2, 768, 3072], P('role', 'dp', 'mp')
- new_feedforward_in_second: float32 [2, 768, 3072], P('role', 'dp', 'mp')
- new_feedforward_in: float32 [2, 768, 3072], P('role', 'dp', 'mp')
- new_feedforward_out_first: float32 [2, 3072, 768], P('role', 'mp', 'dp')
- new_feedforward_out_second: float32 [2, 3072, 768], P('role', 'mp', 'dp')
- new_feedforward_out: float32 [2, 3072, 768], P('role', 'mp', 'dp')
- new_block_affine_first: float32 [2, 6, 768], P('role', None, 'dp')
- new_block_affine_second: float32 [2, 6, 768], P('role', None, 'dp')
- new_block_affine: float32 [2, 6, 768], P('role', None, 'dp')
- new_head_entry_first: float32 [1067, 1024], P(None, ('role', 'dp', 'mp'))
- new_head_entry_second: float32 [1067, 1024], P(None, ('role', 'dp', 'mp'))
- new_head_entry: float32 [1067, 1024], P(None, ('role', 'dp', 'mp'))
- new_head_square_first: float32 [3, 1024, 1024], P(None, None, ('role', 'dp', 'mp'))
- new_head_square_second: float32 [3, 1024, 1024], P(None, None, ('role', 'dp', 'mp'))
- new_head_square: float32 [3, 1024, 1024], P(None, None, ('role', 'dp', 'mp'))
- new_head_modulate_first: float32 [1024, 5120], P(None, ('role', 'dp', 'mp'))
- new_head_modulate_second: float32 [1024, 5120], P(None, ('role', 'dp', 'mp'))
- new_head_modulate: float32 [1024, 5120], P(None, ('role', 'dp', 'mp'))
The draws below stay inside these ranges and needn't reach their ends.
Inputs may be any that keep to these rules, and one draw needn't show every extreme that they name: `buckets`: 0 is a slot of four images, 1 a slot of one image; both values occur in every draw. `visible_index`: for each slot, 320 entries: its visible positions in increasing order, then 1024 as padding. A bucket-1 slot has 160 to 320 visible positions; each image of a bucket-0 slot has 40 to 80. Some slot has exactly 320 visible positions, and some bucket-1 slot exactly 160.
All inputs are finite; a program needn't handle non-finite values.
Results may differ from the reference program's by a relative error of at most 0.0024.
The reference program's roundings to bfloat16 on the way count: a program that leaves them out, or rounds other values in their place, can miss the bound.
Values may be sent and summed in bfloat16 or wider, within the bound.
A program may use at most 256 MiB of HBM per device.

```python
import math
import jax
import jax.numpy as jnp
from jax import lax

D = 768
HEADS = 12
HD = 64
FF = 3072
W = 1024
C = 16
FREQ = 256
GRID = 32
MICRO = 2
STEP = 5
SEQ = 1024
VCAP = 320
MCAP = 864
HE = 1067
PTOT = 23660032
N_DP = 16


def slot_plan(key):
    slot_total = MICRO * N_DP
    split_keys = jax.random.split(key, 5)
    slot_index = jnp.arange(slot_total)
    wide_flags = jax.random.randint(split_keys[0], (slot_total,), 0, 2)
    anchor = jax.random.randint(split_keys[1], (), 0, slot_total)
    wide_flags = jnp.where(slot_index == anchor, 1, wide_flags)
    wide_flags = jnp.where(slot_index == (anchor + 1) % slot_total, 1, wide_flags)
    wide_flags = jnp.where(slot_index == (anchor + 2) % slot_total, 0, wide_flags)
    wide_counts = jax.random.randint(split_keys[2], (slot_total,), VCAP // 2, VCAP + 1)
    wide_counts = jnp.where(slot_index == anchor, VCAP, wide_counts)
    wide_counts = jnp.where(slot_index == (anchor + 1) % slot_total, VCAP // 2, wide_counts)
    small_counts = jax.random.randint(split_keys[3], (slot_total, 4), VCAP // 8, VCAP // 4 + 1)
    quarter = SEQ // 4
    places = jnp.arange(SEQ)
    slot_keys = jax.random.split(split_keys[4], slot_total)

    def one_slot(slot_key, is_wide, wide_count, image_counts):
        whole_key, piece_key = jax.random.split(slot_key)
        whole_rank = jax.random.permutation(whole_key, SEQ)
        piece_rank = jax.vmap(lambda image_key: jax.random.permutation(image_key, quarter))(jax.random.split(piece_key, 4)).reshape(SEQ)
        image_limit = image_counts[places // quarter]
        drawn = jnp.where(is_wide == 1, whole_rank < wide_count, piece_rank < image_limit)
        drawn_flag = drawn.astype(jnp.int32)
        running_rank = jnp.cumsum(drawn_flag) - 1
        drawn_total = jnp.sum(drawn_flag)
        target = jnp.arange(VCAP)
        hit_table = (running_rank[None, :] == target[:, None]) & (drawn_flag[None, :] == 1)
        picked = jnp.sum(jnp.where(hit_table, places[None, :], 0), axis=1)
        return jnp.where(target < drawn_total, picked, SEQ).astype(jnp.int32)
    lists = jax.vmap(one_slot)(slot_keys, wide_flags, wide_counts, small_counts)
    return (wide_flags.astype(jnp.int32), lists)


def draw_buckets(key, part):
    wide_flags, lists = slot_plan(key)
    return wide_flags.reshape(MICRO, N_DP)


def draw_visible_index(key, part):
    wide_flags, lists = slot_plan(key)
    return lists.reshape(MICRO, N_DP * VCAP)


def draw_block_affine(key, part):
    key = jax.random.fold_in(key, 11)
    gain_key, bias_key = jax.random.split(key)
    gains = 1.0 + jax.random.uniform(gain_key, (2, 6, D), jnp.float32, -0.4, 0.4)
    biases = 0.3 * jax.random.normal(bias_key, (2, 6, D), jnp.float32)
    row_index = jnp.arange(6)[None, :, None]
    return jnp.where((row_index == 0) | (row_index == 2), gains, biases)


def draw_head_entry(key, part):
    key = jax.random.fold_in(key, 23)
    row_index = jnp.arange(HE)[:, None]
    row_scale = jnp.where(row_index < D, D ** (-0.5), jnp.where(row_index < D + FREQ, FREQ ** (-0.5), jnp.where(row_index < D + FREQ + C, C ** (-0.5), jnp.where(row_index < D + FREQ + 2 * C, W ** (-0.5), 0.3))))
    return row_scale * jax.random.normal(key, (HE, W), jnp.float32)


def with_ends(values, rng, smallest, high):
    longest = values.shape.index(max(values.shape))
    spots = []
    for shift in (0, 1):
        where = [jax.random.randint(jax.random.fold_in(rng, axis), (), 0, length) for axis, length in enumerate(values.shape)]
        where[longest] = (where[longest] + shift) % values.shape[longest]
        spots.append(tuple(where))
    return values.at[spots[0]].set(smallest).at[spots[1]].set(high)


def block_levels(key, extent, cuts, low, high):
    gain, own = 1.0, jax.random.fold_in(key, 6)
    for axis_at, blocks in cuts:
        heights = jnp.exp(jax.random.uniform(jax.random.fold_in(own, axis_at), (blocks,), jnp.float32, low / len(cuts), high / len(cuts)))
        gain = gain * jnp.repeat(heights, extent[axis_at] // blocks).reshape([-1 if axis == axis_at else 1 for axis in range(len(extent))])
    return gain


def noise(stream_key, extent, width, bound, shards=(), kind=jnp.bfloat16):
    level = block_levels(stream_key, extent, shards, -0.22, 0.18) if shards else 1.0
    result = jax.random.normal(stream_key, extent, jnp.float32) * width * level
    return jnp.minimum(jnp.maximum(result, -bound), bound).astype(kind)


def setup_inputs(seed: int = 0) -> dict:
    key_of = jax.random.split(jax.random.key(seed), 33)
    latents = noise(key_of[0], (MICRO, N_DP * SEQ, C), 1.0, 6.0, ((1, 16),), jnp.float32)
    noise_draws = noise(key_of[1], (MICRO, N_DP * SEQ, C), 1.0, 6.0, ((1, 16),), jnp.float32)
    timesteps = with_ends(jax.random.randint(key_of[2], (MICRO, N_DP * SEQ), 0, 1000), jax.random.fold_in(key_of[2], 1), 0, 999).astype(jnp.int32)
    buckets = draw_buckets(jax.random.fold_in(key_of[32], 71), 0)
    visible_index = draw_visible_index(jax.random.fold_in(key_of[32], 71), 0)
    patch_embed = noise(key_of[5], (C + 2, D), C ** -0.5, 1.5, (), jnp.float32)
    patch_embed_first = noise(key_of[6], (C + 2, D), (0.111 * 0.02 / PTOT ** 0.5), 2.86102294921875e-06, (), jnp.float32)
    patch_embed_second = jnp.clip(jnp.exp(jax.random.uniform(key_of[7], (C + 2, D), jnp.float32, math.log(8.892633808141315e-13), math.log(3.5502911374662993e-12))), 8.892633808141315e-13, 3.5502911374662993e-12)
    attention_in = noise(key_of[8], (2, D, HEADS, 3 * HD), D ** -0.5, 0.21875, ((0, 2), (1, 16), (2, 4)), jnp.float32)
    attention_in_first = noise(key_of[9], (2, D, HEADS, 3 * HD), (0.111 * 0.02 / PTOT ** 0.5), 2.86102294921875e-06, ((0, 2), (1, 16), (2, 4)), jnp.float32)
    attention_in_second = jnp.clip(jnp.exp(math.log(3.5502911374662993e-12) - 1.3843914 * jax.random.uniform(key_of[10], (2, D, HEADS, 3 * HD), jnp.float32) ** block_levels(key_of[10], (2, D, HEADS, 3 * HD), ((0, 2), (1, 16), (2, 4)), -0.2, 0.2)), 8.892633808141315e-13, 3.5502911374662993e-12)
    attention_out = noise(key_of[11], (2, D, D), (D // 8) ** -0.5, 0.625, ((0, 2), (1, 4), (2, 16)), jnp.float32)
    attention_out_first = noise(key_of[12], (2, D, D), (0.111 * 0.02 / PTOT ** 0.5), 2.86102294921875e-06, ((0, 2), (1, 4), (2, 16)), jnp.float32)
    attention_out_second = jnp.clip(jnp.exp(math.log(3.5502911374662993e-12) - 1.3843914 * jax.random.uniform(key_of[13], (2, D, D), jnp.float32) ** block_levels(key_of[13], (2, D, D), ((0, 2), (1, 4), (2, 16)), -0.2, 0.2)), 8.892633808141315e-13, 3.5502911374662993e-12)
    feedforward_in = noise(key_of[14], (2, D, FF), D ** -0.5, 0.21875, ((0, 2), (1, 16), (2, 4)), jnp.float32)
    feedforward_in_first = noise(key_of[15], (2, D, FF), (0.111 * 0.02 / PTOT ** 0.5), 2.86102294921875e-06, ((0, 2), (1, 16), (2, 4)), jnp.float32)
    feedforward_in_second = jnp.clip(jnp.exp(math.log(3.5502911374662993e-12) - 1.3843914 * jax.random.uniform(key_of[16], (2, D, FF), jnp.float32) ** block_levels(key_of[16], (2, D, FF), ((0, 2), (1, 16), (2, 4)), -0.2, 0.2)), 8.892633808141315e-13, 3.5502911374662993e-12)
    feedforward_out = noise(key_of[17], (2, FF, D), FF ** -0.5, 0.109375, ((0, 2), (1, 4), (2, 16)), jnp.float32)
    feedforward_out_first = noise(key_of[18], (2, FF, D), (0.111 * 0.02 / PTOT ** 0.5), 2.86102294921875e-06, ((0, 2), (1, 4), (2, 16)), jnp.float32)
    feedforward_out_second = jnp.clip(jnp.exp(math.log(3.5502911374662993e-12) - 1.3843914 * jax.random.uniform(key_of[19], (2, FF, D), jnp.float32) ** block_levels(key_of[19], (2, FF, D), ((0, 2), (1, 4), (2, 16)), -0.2, 0.2)), 8.892633808141315e-13, 3.5502911374662993e-12)
    block_affine = draw_block_affine(jax.random.fold_in(key_of[32], 71), 0)
    block_affine_first = noise(key_of[21], (2, 6, D), (0.111 * 0.02 / PTOT ** 0.5), 2.86102294921875e-06, ((0, 2), (2, 16)), jnp.float32)
    block_affine_second = jnp.clip(jnp.exp(math.log(3.5502911374662993e-12) - 1.3843914 * jax.random.uniform(key_of[22], (2, 6, D), jnp.float32) ** block_levels(key_of[22], (2, 6, D), ((0, 2), (2, 16)), -0.2, 0.2)), 8.892633808141315e-13, 3.5502911374662993e-12)
    head_entry = draw_head_entry(jax.random.fold_in(key_of[32], 71), 0)
    head_entry_first = noise(key_of[24], (HE, W), (0.111 * 0.02 / PTOT ** 0.5), 2.86102294921875e-06, ((1, 128),), jnp.float32)
    head_entry_second = jnp.clip(jnp.exp(math.log(3.5502911374662993e-12) - 1.3843914 * jax.random.uniform(key_of[25], (HE, W), jnp.float32) ** block_levels(key_of[25], (HE, W), ((1, 128),), -0.2, 0.2)), 8.892633808141315e-13, 3.5502911374662993e-12)
    head_square = noise(key_of[26], (3, W, W), W ** -0.5, 0.1875, ((2, 128),), jnp.float32)
    head_square_first = noise(key_of[27], (3, W, W), (0.111 * 0.02 / PTOT ** 0.5), 2.86102294921875e-06, ((2, 128),), jnp.float32)
    head_square_second = jnp.clip(jnp.exp(math.log(3.5502911374662993e-12) - 1.3843914 * jax.random.uniform(key_of[28], (3, W, W), jnp.float32) ** block_levels(key_of[28], (3, W, W), ((2, 128),), -0.2, 0.2)), 8.892633808141315e-13, 3.5502911374662993e-12)
    head_modulate = noise(key_of[29], (W, 5 * W), W ** -0.5, 0.1875, ((1, 128),), jnp.float32)
    head_modulate_first = noise(key_of[30], (W, 5 * W), (0.111 * 0.02 / PTOT ** 0.5), 2.86102294921875e-06, ((1, 128),), jnp.float32)
    head_modulate_second = jnp.clip(jnp.exp(math.log(3.5502911374662993e-12) - 1.3843914 * jax.random.uniform(key_of[31], (W, 5 * W), jnp.float32) ** block_levels(key_of[31], (W, 5 * W), ((1, 128),), -0.2, 0.2)), 8.892633808141315e-13, 3.5502911374662993e-12)
    return dict(latents=latents, noise_draws=noise_draws, timesteps=timesteps, buckets=buckets, visible_index=visible_index, patch_embed=patch_embed, patch_embed_first=patch_embed_first, patch_embed_second=patch_embed_second, attention_in=attention_in, attention_in_first=attention_in_first, attention_in_second=attention_in_second, attention_out=attention_out, attention_out_first=attention_out_first, attention_out_second=attention_out_second, feedforward_in=feedforward_in, feedforward_in_first=feedforward_in_first, feedforward_in_second=feedforward_in_second, feedforward_out=feedforward_out, feedforward_out_first=feedforward_out_first, feedforward_out_second=feedforward_out_second, block_affine=block_affine, block_affine_first=block_affine_first, block_affine_second=block_affine_second, head_entry=head_entry, head_entry_first=head_entry_first, head_entry_second=head_entry_second, head_square=head_square, head_square_first=head_square_first, head_square_second=head_square_second, head_modulate=head_modulate, head_modulate_first=head_modulate_first, head_modulate_second=head_modulate_second)


@jax.custom_vjp
def low(v):
    return lax.optimization_barrier(v.astype(jnp.bfloat16)).astype(jnp.float32)

@jax.custom_vjp
def low_back(v):
    return v

def low_keep(v):
    return (low(v), None)

def low_pass(kept, grad):
    return (grad,)

def back_keep(v):
    return (v, None)

def back_low(kept, grad):
    return (low(grad),)
low.defvjp(low_keep, low_pass)
low_back.defvjp(back_keep, back_low)
LN_EPS = 1e-06
BETA_ONE = 0.9
BETA_TWO = 0.95
ADAM_EPS = 1e-08
DECAY = 0.02
RATE = 0.02
CLIP_NORM = 0.02
BUCKET_SHARE = (0.6, 0.4)
COSINE_OFFSET = 0.008
HORIZON = 1000.0
HIGHEST = lax.Precision.HIGHEST

def matmul_high(left_side, right_side):
    return jnp.dot(left_side, right_side, precision=HIGHEST)

def layer_norm(values, gain_row, offset):
    centered = values - lax.optimization_barrier(jnp.mean(values, axis=-1, keepdims=True))
    spread = lax.optimization_barrier(jnp.mean(centered * centered, axis=-1, keepdims=True))
    return centered * lax.rsqrt(spread + LN_EPS) * gain_row + offset

def plain_norm(values):
    centered = values - lax.optimization_barrier(jnp.mean(values, axis=-1, keepdims=True))
    spread = lax.optimization_barrier(jnp.mean(centered * centered, axis=-1, keepdims=True))
    return centered * lax.rsqrt(spread + LN_EPS)

def positions(places, wide_image):
    local_place = jnp.where(wide_image, places, places % (SEQ // 4))
    grid_side = jnp.where(wide_image, GRID, GRID // 2)
    row_pos = (local_place // grid_side).astype(jnp.float32)
    col_pos = (local_place % grid_side).astype(jnp.float32)
    frequency = 1.0 / 10000.0 ** (jnp.arange(D // 4, dtype=jnp.float32) / (D // 4))
    row_angle = row_pos[:, None] * frequency[None, :]
    col_angle = col_pos[:, None] * frequency[None, :]
    return jnp.concatenate([jnp.sin(row_angle), jnp.cos(row_angle), jnp.sin(col_angle), jnp.cos(col_angle)], axis=1)

def image_ids(places, wide_image):
    return jnp.where(wide_image, 0, places // (SEQ // 4)).astype(jnp.int32)

def masked_list(visible):
    places = jnp.arange(SEQ, dtype=jnp.int32)
    shown = jnp.any(visible[:, None] == places[None, :], axis=0)
    masked_flag = jnp.logical_not(shown).astype(jnp.int32)
    running_rank = jnp.cumsum(masked_flag) - 1
    slot_index = jnp.arange(MCAP, dtype=jnp.int32)
    hit_table = (running_rank[None, :] == slot_index[:, None]) & (masked_flag[None, :] == 1)
    masked_total = jnp.sum(masked_flag)
    picked = lax.optimization_barrier(jnp.sum(jnp.where(hit_table, places[None, :], 0), axis=1))
    return jnp.where(slot_index < masked_total, picked, SEQ).astype(jnp.int32)

def attend(queries, key_rows, values, query_images, key_images, key_valid):
    raw = jnp.einsum('qhd,khd->hqk', queries, key_rows, precision=HIGHEST) * HD ** (-0.5)
    allowed = (query_images[:, None] == key_images[None, :]) & key_valid[None, :]
    scores = low_back(jnp.where(allowed[None], raw, -1e+30))
    probability = low(jax.nn.softmax(scores, axis=-1))
    attended = jnp.einsum('hqk,khd->qhd', probability, values, precision=HIGHEST)
    return attended.reshape(attended.shape[0], -1)

def block_forward(embedded, query_count, row_images, key_valid, weights, affine):
    w_in, w_out, w_up, w_down = weights
    normed = low(layer_norm(embedded, affine[0], affine[1]))
    joint_proj = jnp.einsum('rd,dhe->rhe', normed, w_in, precision=HIGHEST)
    queries = low(low_back(joint_proj[:query_count, :, :HD]))
    key_rows = low(low_back(joint_proj[:, :, HD:2 * HD]))
    values = low(low_back(joint_proj[:, :, 2 * HD:]))
    merged = low(low_back(attend(queries, key_rows, values, row_images[:query_count], row_images, key_valid)))
    branch = low_back(matmul_high(merged, w_out))
    first_res = embedded[:query_count] + branch + affine[4]
    normed_two = low(layer_norm(first_res, affine[2], affine[3]))
    before = low_back(matmul_high(normed_two, w_up))
    active = low(jax.nn.gelu(before, approximate=False))
    down_branch = low_back(matmul_high(active, w_down))
    return first_res + down_branch + affine[5]

def head_loss(condition, clean, noise_rows, slot_times, entry, square, modulate):
    times_f = (slot_times + 1).astype(jnp.float32)
    half_turn = math.pi / 2
    angle_now = (times_f / HORIZON + COSINE_OFFSET) / (1.0 + COSINE_OFFSET) * half_turn
    start_cos = math.cos(COSINE_OFFSET / (1.0 + COSINE_OFFSET) * half_turn)
    signal_kept = (jnp.cos(angle_now) / start_cos) ** 2
    noisy_input = low(jnp.sqrt(signal_kept)[:, None] * clean + jnp.sqrt(1.0 - signal_kept)[:, None] * noise_rows)
    half_width = FREQ // 2
    frequency = jnp.exp(-math.log(10000.0) * jnp.arange(half_width, dtype=jnp.float32) / half_width)
    angles = times_f[:, None] * frequency[None, :]
    features = low(jnp.concatenate([jnp.cos(angles), jnp.sin(angles)], axis=1))
    at_time = D
    at_input = D + FREQ
    at_output = at_input + C
    at_bias = at_output + C
    biases = entry[at_bias:]
    time_pre = low_back(matmul_high(features, entry[at_time:at_input]) + biases[1])
    time_act = low(jax.nn.silu(time_pre))
    time_vec = matmul_high(time_act, square[0]) + biases[2]
    cond_pre = low_back(matmul_high(condition, entry[:D]) + biases[0] + time_vec)
    cond_act = low(jax.nn.silu(cond_pre))
    modulation = low_back(matmul_high(cond_act, modulate) + biases[6:11].reshape(-1))
    shift_in, scale_in, gate_in, shift_out, scale_out = jnp.split(modulation, 5, axis=1)
    entry_x = low_back(matmul_high(noisy_input, entry[at_input:at_output]) + biases[3])
    mod_in = low(plain_norm(entry_x) * (1.0 + scale_in) + shift_in)
    hidden_one = low_back(matmul_high(mod_in, square[1]) + biases[4])
    hidden_act = low(jax.nn.silu(hidden_one))
    hidden_two = low_back(matmul_high(hidden_act, square[2]) + biases[5])
    leaving = entry_x + gate_in * hidden_two
    mod_out = low(plain_norm(leaving) * (1.0 + scale_out) + shift_out)
    predicted = low_back(matmul_high(mod_out, entry[at_output:at_bias].T))
    return lax.optimization_barrier(jnp.mean((predicted - noise_rows) ** 2, axis=1))

def slot_loss(params, slot_latent, slot_noise, slot_times, wide_flag, visible, shares):
    patch_embed, attention_in, attention_out, feed_in, feed_out, affine, entry, square, modulate = params
    wide_image = wide_flag == 1
    visible_c = jnp.minimum(visible, SEQ - 1)
    visible_ok = visible < SEQ
    masked = masked_list(visible)
    masked_c = jnp.minimum(masked, SEQ - 1)
    masked_ok = masked < SEQ
    ids_visible = image_ids(visible_c, wide_image)
    ids_masked = image_ids(masked_c, wide_image)
    table_visible = positions(visible_c, wide_image)
    table_masked = positions(masked_c, wide_image)

    def weights_of(which):
        return (low(attention_in[which]), low(attention_out[which]), low(feed_in[which]), low(feed_out[which]))
    embedded = matmul_high(slot_latent[visible_c], patch_embed[:C]) + patch_embed[C] + table_visible
    encoded = block_forward(embedded, VCAP, ids_visible, visible_ok, weights_of(0), low(affine[0]))
    sent = low(low_back(encoded))
    dec_rows = jnp.concatenate([patch_embed[C + 1] + table_masked, sent + table_visible], axis=0)
    dec_ids = jnp.concatenate([ids_masked, ids_visible])
    dec_ok = jnp.concatenate([masked_ok, visible_ok])
    decoded = block_forward(dec_rows, MCAP, dec_ids, dec_ok, weights_of(1), low(affine[1]))
    condition = low(low_back(decoded))
    per_row = head_loss(condition, slot_latent[masked_c], slot_noise[masked_c], slot_times[masked_c], low(entry), low(square), low(modulate))
    row_weight = jnp.where(masked_ok, shares[wide_flag], 0.0)
    return jnp.sum(row_weight * per_row)

def adam_update(weight_now, first_now, second_now, grad_now):
    first_new = BETA_ONE * first_now + (1.0 - BETA_ONE) * grad_now
    second_new = BETA_TWO * second_now + (1.0 - BETA_TWO) * grad_now * grad_now
    first_hat = first_new / (1.0 - BETA_ONE ** STEP)
    second_hat = second_new / (1.0 - BETA_TWO ** STEP)
    weight_new = weight_now - RATE * (first_hat / (jnp.sqrt(second_hat) + ADAM_EPS) + DECAY * weight_now)
    return (first_new, second_new, weight_new)

def reference(latents, noise_draws, timesteps, buckets, visible_index, patch_embed, patch_embed_first, patch_embed_second, attention_in, attention_in_first, attention_in_second, attention_out, attention_out_first, attention_out_second, feedforward_in, feedforward_in_first, feedforward_in_second, feedforward_out, feedforward_out_first, feedforward_out_second, block_affine, block_affine_first, block_affine_second, head_entry, head_entry_first, head_entry_second, head_square, head_square_first, head_square_second, head_modulate, head_modulate_first, head_modulate_second):
    params = (patch_embed, attention_in, attention_out, feedforward_in, feedforward_out, block_affine, head_entry, head_square, head_modulate)
    firsts = (patch_embed_first, attention_in_first, attention_out_first, feedforward_in_first, feedforward_out_first, block_affine_first, head_entry_first, head_square_first, head_modulate_first)
    seconds = (patch_embed_second, attention_in_second, attention_out_second, feedforward_in_second, feedforward_out_second, block_affine_second, head_entry_second, head_square_second, head_modulate_second)
    slot_count = MICRO * N_DP
    latent_slots = latents.reshape(slot_count, SEQ, C)
    noise_slots = noise_draws.reshape(slot_count, SEQ, C)
    time_slots = timesteps.reshape(slot_count, SEQ)
    wide_slots = buckets.reshape(slot_count)
    visible_slots = visible_index.reshape(slot_count, VCAP)
    masked_counts = SEQ - lax.optimization_barrier(jnp.sum((visible_slots < SEQ).astype(jnp.int32), axis=1))
    counts = jnp.stack([jnp.sum(jnp.where(wide_slots == 0, masked_counts, 0)), jnp.sum(jnp.where(wide_slots == 1, masked_counts, 0))]).astype(jnp.float32)
    shares = jnp.array(BUCKET_SHARE, dtype=jnp.float32) / counts

    def one_slot(carry, slot_data):
        slot_latent, slot_noise, slot_times, wide_flag, visible = slot_data
        slot_value, pullback = jax.vjp(lambda weights: slot_loss(weights, slot_latent, slot_noise, slot_times, wide_flag, visible, shares), params)
        gradients = pullback(jnp.ones_like(slot_value))[0]
        loss_sum, grad_sums = carry
        return ((loss_sum + slot_value, jax.tree.map(jnp.add, grad_sums, gradients)), None)
    initial = (jnp.zeros((), jnp.float32), jax.tree.map(jnp.zeros_like, params))
    (loss_total, gradients), ignored = lax.scan(one_slot, initial, (latent_slots, noise_slots, time_slots, wide_slots, visible_slots))
    square_total = sum((jnp.sum(item * item) for item in gradients))
    grad_norm = jnp.sqrt(square_total)
    factor = jnp.minimum(1.0, CLIP_NORM / (grad_norm + 1e-06))
    news = []
    for weight_now, first_now, second_now, grad_now in zip(params, firsts, seconds, gradients):
        news.extend(adam_update(weight_now, first_now, second_now, factor * grad_now))
    return (loss_total, grad_norm, news[0], news[1], news[2], news[3], news[4], news[5], news[6], news[7], news[8], news[9], news[10], news[11], news[12], news[13], news[14], news[15], news[16], news[17], news[18], news[19], news[20], news[21], news[22], news[23], news[24], news[25], news[26])
```

```python
import math

import jax
import jax.numpy as jnp
from jax import lax
from jax.experimental import pallas as pl
from jax.experimental.pallas import tpu as pltpu
from jax.sharding import PartitionSpec as P

D = 768
HD = 64
C = 16
FREQ = 256
GRID = 32
STEP = 5
SEQ = 1024
VCAP = 320
MCAP = 864


LN_EPS = 1e-06
BETA_ONE = 0.9
BETA_TWO = 0.95
ADAM_EPS = 1e-08
DECAY = 0.02
RATE = 0.02
CLIP_NORM = 0.02
BUCKET_SHARE = (0.6, 0.4)
COSINE_OFFSET = 0.008
HORIZON = 1000.0
LOW_TYPE = jnp.bfloat16
WIDE_TYPE = jnp.float32


def matmul_low(left_side, right_side):
    return jnp.dot(left_side, right_side, preferred_element_type=WIDE_TYPE)


def matmul_high(left_side, right_side):
    return jnp.dot(left_side, right_side, precision=lax.Precision.HIGHEST)


def inner_rows(left_side, right_side):
    return lax.dot_general(
        left_side, right_side, (((0,), (0,)), ((), ())), preferred_element_type=WIDE_TYPE
    )


def outer_rows(left_side, right_side):
    return lax.dot_general(
        left_side, right_side, (((1,), (1,)), ((), ())), preferred_element_type=WIDE_TYPE
    )


def plain_forward(values):
    centered = values - jnp.mean(values, axis=-1, keepdims=True)
    spread = jnp.mean(centered * centered, axis=-1, keepdims=True)
    inverse = lax.rsqrt(spread + LN_EPS)
    scaled = centered * inverse
    return (scaled, (scaled, inverse))


def plain_backward(upstream, saved_norm):
    scaled, inverse = saved_norm
    return inverse * (
        upstream
        - jnp.mean(upstream, axis=-1, keepdims=True)
        - scaled * jnp.mean(upstream * scaled, axis=-1, keepdims=True)
    )


def silu_slope(values):
    sigmoid = jax.nn.sigmoid(values)
    return sigmoid * (1.0 + values * (1.0 - sigmoid))


def adam_update(weight_now, first_now, second_now, grad_now):
    first_new = BETA_ONE * first_now + (1.0 - BETA_ONE) * grad_now
    second_new = BETA_TWO * second_now + (1.0 - BETA_TWO) * grad_now * grad_now
    first_hat = first_new / (1.0 - BETA_ONE**STEP)
    second_hat = second_new / (1.0 - BETA_TWO**STEP)
    weight_new = weight_now - RATE * (
        first_hat / (jnp.sqrt(second_hat) + ADAM_EPS) + DECAY * weight_now
    )
    return (first_new, second_new, weight_new)


QUARTER = 4
MQ = MCAP // QUARTER
VQ = VCAP // QUARTER
HEADS = 12
FF = 3072
W = 1024
ALL = ("role", "dp", "mp")
SCALE = HD ** (-0.5)


def device_order():
    return [(r, x, z, y) for r in range(2) for x in range(4) for z in range(4) for y in range(4)]


def flat_index(r, x, z, y):
    return r * 64 + x * 16 + z * 4 + y


def ring_pairs(axis):
    pairs = []
    for place in device_order():
        target = list(place)
        target[axis] = (target[axis] + (1 if place[0] == 0 else -1)) % 4
        pairs.append((flat_index(*place), flat_index(*target)))
    return pairs


def partner_pairs():
    return [(flat_index(r, x, z, y), flat_index(1 - r, x, z, y)) for r, x, z, y in device_order()]


def neighbour_pairs():
    return [(flat_index(r, x, z, y), flat_index(r, x, z, y ^ 1)) for r, x, z, y in device_order()]


def send(value, pairs):
    return lax.ppermute(value, ALL, pairs)


def pick(value, index, dim):
    return lax.dynamic_index_in_dim(value, index, dim, keepdims=False)


def ring_sum(parts, dim, axis, place, step, wire):
    def chunk(index):
        return pick(parts, lax.rem(place - index * step + 8, 4), dim)

    total = chunk(1)
    for hop in (1, 2, 3):
        total = send(total.astype(wire), ring_pairs(axis)).astype(WIDE_TYPE) + chunk(hop + 1)
    return total


def torus_sum(parts, order, places, step, first_wire=LOW_TYPE):
    left = [1, 2, 3]
    for count, axis in enumerate(order):
        dim = left.index(axis)
        wire = first_wire if count == 0 else WIDE_TYPE
        parts = ring_sum(parts, dim, axis, places[axis], step, wire)
        left.remove(axis)
    return parts


ORDERS = ((1, 2, 3), (2, 3, 1), (3, 1, 2))


BLOCK_COLS = 2432
PIECES = (
    ((0, 0, 0, BLOCK_COLS, 1280), (3, None, 0, 640, 384)),
    ((0, 16, 0, BLOCK_COLS, 1280), (3, None, 640, 384, 256), (2, None, 0, 1024, 512), (4, None, 0, 128, 128)),
    ((0, 32, 0, BLOCK_COLS, 1280), (1, None, 0, 1024, 512)),
)
GATHER_COPIES = 8 + 3 * 8 * 8


def mesh_place():
    dp_index = lax.axis_index("dp")
    role, mp_index = lax.axis_index("role"), lax.axis_index("mp")
    return (role, dp_index // 4, lax.rem(dp_index, 4), mp_index)


def mesh_device(place):
    return (place[0], place[1] * 4 + place[2], place[3])


def moved(place, axis, steps):
    target = list(place)
    count = 2 if axis == 0 else 4
    target[axis] = lax.rem(target[axis] + steps + count, count)
    return tuple(target)


def greet(place, moves):
    barrier = pltpu.get_barrier_semaphore()
    for axis, steps in moves:
        pl.semaphore_signal(
            barrier,
            inc=1,
            device_id=mesh_device(moved(place, axis, steps)),
            device_id_type=pl.DeviceIdType.MESH,
        )
    pl.semaphore_wait(barrier, len(moves))


RING_MOVES = ((0, 1), (1, 1), (1, -1), (2, 1), (2, -1), (3, 1), (3, -1))


def gather_kernel(*refs):
    ins, outs, (send_sems, recv_sems, local_sems) = refs[:5], refs[5:10], refs[10:]
    place = mesh_place()
    used = [0]

    def region(piece, spans, half):
        kind, row, column, width, cut = piece
        if half is not None:
            column, width = (column, cut) if half == 0 else (column + cut, width - cut)
        r = spans[0]
        x, z, y = (slice(None) if spans[axis] is None else spans[axis] for axis in (1, 2, 3))
        columns = pl.ds(column, width)
        if kind == 0:
            return outs[0].at[r, y, x, z, pl.ds(row, 16), columns]
        if kind == 1:
            return outs[1].at[:, r, x, z, y, :, columns]
        return outs[kind].at[r, x, z, y, :, columns]

    def start(third, spans, half, axis, steps):
        copies = []
        for piece in PIECES[third]:
            if half == 1 and piece[3] == piece[4]:
                continue
            ref = region(piece, spans, half)
            slot = used[0]
            used[0] += 1
            copy = pltpu.make_async_remote_copy(
                src_ref=ref,
                dst_ref=ref,
                send_sem=send_sems.at[slot],
                recv_sem=recv_sems.at[slot],
                device_id=mesh_device(moved(place, axis, steps)),
                device_id_type=pl.DeviceIdType.MESH,
            )
            copy.start()
            copies.append(copy)
        return copies

    r, x, z, y = place
    own = {0: r, 1: x, 2: z, 3: y}
    targets = (
        outs[0].at[r, y, x, z], outs[1].at[:, r, x, z, y], outs[2].at[r, x, z, y],
        outs[3].at[r, x, z, y], outs[4].at[r, x, z, y],
    )
    placed = [
        pltpu.make_async_copy(source, target, local_sems.at[index])
        for index, (source, target) in enumerate(zip(ins, targets))
    ]
    for copy in placed:
        copy.start()
    greet(place, RING_MOVES)
    for copy in placed:
        copy.wait()
    pending = []
    spans = [dict(own) for _ in range(3)]
    for third in range(3):
        pending += start(third, spans[third], None, 0, 1)
    for stage in range(3):
        first = []
        for third in range(3):
            axis = ORDERS[third][stage]
            first.append([start(third, spans[third], None, axis, steps) for steps in (1, -1)])
        second = []
        for third in range(3):
            axis = ORDERS[third][stage]
            batch = []
            for which, steps in ((0, 1), (1, -1)):
                came = dict(spans[third])
                came[axis] = lax.rem(own[axis] - steps + 4, 4)
                for copy in first[third][which]:
                    copy.wait_recv()
                batch.append(start(third, came, which, axis, steps))
                pending += start(third, came, None, 0, 1)
            second.append(batch)
        for third in range(3):
            axis = ORDERS[third][stage]
            came = dict(spans[third])
            came[axis] = lax.rem(own[axis] + 2, 4)
            for which in (0, 1):
                for copy in second[third][which]:
                    copy.wait_recv()
                pending += start(third, came, which, 0, 1)
            for batch in (first[third], second[third]):
                for copies in batch:
                    for copy in copies:
                        copy.wait_send()
            spans[third][axis] = None
    for copy in pending:
        copy.wait()


def gather_weights(shards):
    whole_torus = (2, 4, 4, 4)
    return pl.pallas_call(
        gather_kernel,
        out_shape=(
            jax.ShapeDtypeStruct(whole_torus + (48, BLOCK_COLS), LOW_TYPE),
            jax.ShapeDtypeStruct((3,) + whole_torus + (8, W), LOW_TYPE),
            jax.ShapeDtypeStruct(whole_torus + (8, W), LOW_TYPE),
            jax.ShapeDtypeStruct(whole_torus + (40, W), LOW_TYPE),
            jax.ShapeDtypeStruct(whole_torus + (8, 128), LOW_TYPE),
        ),
        in_specs=[pl.BlockSpec(memory_space=pl.ANY)] * 5,
        out_specs=(pl.BlockSpec(memory_space=pl.ANY),) * 5,
        scratch_shapes=[
            pltpu.SemaphoreType.DMA((GATHER_COPIES,)),
            pltpu.SemaphoreType.DMA((GATHER_COPIES,)),
            pltpu.SemaphoreType.DMA((5,)),
        ],
        compiler_params=pltpu.CompilerParams(collective_id=0, has_side_effects=True),
    )(*shards)


SUM_MOVES = ((0, 1),) + tuple((axis, steps) for axis in (1, 2, 3) for steps in (1, 2, 3))


def sum_kernel(value_in, value_out, held, slots, send_sems, recv_sems):
    place = mesh_place()
    greet(place, SUM_MOVES)
    held[...] = value_in[...]
    for stage, axis in enumerate((0, 3, 1, 2)):
        count = 2 if axis == 0 else 4
        copies = []
        for steps in range(1, count):
            copy = pltpu.make_async_remote_copy(
                src_ref=held,
                dst_ref=slots.at[stage, place[axis]],
                send_sem=send_sems.at[stage, steps - 1],
                recv_sem=recv_sems.at[stage, steps - 1],
                device_id=mesh_device(moved(place, axis, steps)),
                device_id_type=pl.DeviceIdType.MESH,
            )
            copy.start()
            copies.append(copy)
        slots[stage, place[axis]] = held[...]
        for copy in copies:
            copy.wait()
        total = slots[stage, 0]
        for index in range(1, count):
            total = total + slots[stage, index]
        held[...] = total
    value_out[...] = held[...]


def sum_everywhere(value, collective):
    shape = value.shape
    return pl.pallas_call(
        sum_kernel,
        out_shape=jax.ShapeDtypeStruct(shape, WIDE_TYPE),
        in_specs=[pl.BlockSpec(memory_space=pltpu.VMEM)],
        out_specs=pl.BlockSpec(memory_space=pltpu.VMEM),
        scratch_shapes=[
            pltpu.VMEM(shape, WIDE_TYPE),
            pltpu.VMEM((4, 4) + shape, WIDE_TYPE),
            pltpu.SemaphoreType.DMA((4, 3)),
            pltpu.SemaphoreType.DMA((4, 3)),
        ],
        compiler_params=pltpu.CompilerParams(collective_id=collective, has_side_effects=True),
    )(value)


def position_table():
    frequency = 1.0 / 10000.0 ** (jnp.arange(D // 4, dtype=WIDE_TYPE) / (D // 4))
    angle = jnp.arange(GRID, dtype=WIDE_TYPE)[:, None] * frequency[None, :]
    return jnp.concatenate([jnp.sin(angle), jnp.cos(angle)], axis=1)


def one_hot(index, count):
    return (index[:, None] == jnp.arange(count, dtype=jnp.int32)[None, :]).astype(WIDE_TYPE)


def positions(places, wide_image, table):
    local_place = jnp.where(wide_image, places, places % (SEQ // 4))
    grid_side = jnp.where(wide_image, GRID, GRID // 2)
    rows = one_hot(local_place // grid_side, GRID)
    cols = one_hot(local_place % grid_side, GRID)
    return jnp.concatenate([matmul_high(rows, table), matmul_high(cols, table)], axis=1)


def image_ids(places, wide_image):
    return jnp.where(wide_image, 0, places // (SEQ // 4))


def masked_places(visible):
    places = jnp.arange(SEQ, dtype=jnp.int32)
    shown = jnp.any(visible[:, None] == places[None, :], axis=0)
    masked_flag = jnp.logical_not(shown).astype(jnp.int32)
    running_rank = jnp.cumsum(masked_flag) - 1
    slot_index = jnp.arange(MCAP, dtype=jnp.int32)
    hit_table = (running_rank[None, :] == slot_index[:, None]) & (masked_flag[None, :] == 1)
    picked = jnp.sum(jnp.where(hit_table, places[None, :], 0), axis=1)
    return jnp.where(slot_index < jnp.sum(masked_flag), picked, SEQ)


def half_of(values, groups, index):
    rows, columns = values.shape
    split = values.reshape(rows, groups, 2, columns // groups // 2)
    return pick(split, index, 2).reshape(rows, columns // 2)


def split_grad(left, right, groups, role, left_halved):
    def part(index):
        if left_halved:
            return inner_rows(half_of(left, groups, index), right)
        return inner_rows(left, half_of(right, groups, index))

    theirs = send(part(1 - role).astype(LOW_TYPE), partner_pairs())
    return part(role) + theirs.astype(WIDE_TYPE)


MQP = 224
VMEM_BYTES = 60 * 1024 * 1024


def normed_rows(values, gain, offset):
    centered = values - jnp.mean(values, axis=-1, keepdims=True)
    inverse = lax.rsqrt(jnp.mean(centered * centered, axis=-1, keepdims=True) + LN_EPS)
    scaled = centered * inverse
    return scaled * gain + offset, scaled, inverse


def norm_pull(upstream, scaled, inverse, gain):
    inner = upstream * gain
    return inverse * (
        inner
        - jnp.mean(inner, axis=-1, keepdims=True)
        - scaled * jnp.mean(inner * scaled, axis=-1, keepdims=True)
    )


def row_sum(values):
    return jnp.sum(values, axis=0, keepdims=True)


def attention_forward_kernel(
    all_ref, own_ref, keys_ref, own_ids_ref, affine_ref, w_ref,
    first_ref, low_all_ref, low_own_ref, joint_ref, query_ref, mass_ref, merged_ref,
    total,
):
    head_set = pl.program_id(0)

    @pl.when(head_set == 0)
    def _():
        gain, offset = affine_ref[0:1], affine_ref[1:2]
        low_all_ref[...] = normed_rows(all_ref[...], gain, offset)[0].astype(LOW_TYPE)
        low_own_ref[...] = normed_rows(own_ref[...], gain, offset)[0].astype(LOW_TYPE)
        total[...] = own_ref[...] + affine_ref[4:5]

    weights = w_ref[0, 0]
    joint = matmul_low(low_all_ref[...], weights[:, :384]).astype(LOW_TYPE)
    query = matmul_low(low_own_ref[...], weights[:, 384:])[:, :192].astype(LOW_TYPE)
    joint_ref[0] = joint
    query_ref[0] = query
    allowed = keys_ref[...] == own_ids_ref[...]
    parts = []
    for head in range(3):
        key = joint[:, HD * head : HD * (head + 1)]
        value = joint[:, 192 + HD * head : 192 + HD * (head + 1)]
        scores = outer_rows(key, query[:, HD * head : HD * (head + 1)]) * SCALE
        scores = jnp.where(allowed, scores, -1e30)
        peak = jnp.max(scores, axis=0, keepdims=True)
        exponent = jnp.exp(scores - peak)
        mass = row_sum(exponent)
        probability = (exponent * (1.0 / mass)).astype(LOW_TYPE)
        mass_ref[0, head : head + 1] = peak + jnp.log(mass)
        parts.append(inner_rows(value, probability))
    merged = jnp.concatenate(parts, axis=0).T.astype(LOW_TYPE)
    merged_ref[0] = merged
    total[...] += outer_rows(merged, weights[:, 576:])

    @pl.when(head_set == 3)
    def _():
        first_ref[...] = total[...]


def attention_backward_kernel(
    role_ref, grad_ref, all_ref, own_ref, keys_ref, own_ids_ref, affine_ref, w_ref,
    low_all_ref, low_own_ref, joint_ref, query_ref, mass_ref, merged_ref,
    mine_ref, theirs_ref, all_grad_ref, own_grad_ref, affine_grad_ref,
    branch, all_sum, own_sum,
):
    head_set = pl.program_id(0)

    @pl.when(head_set == 0)
    def _():
        branch[...] = grad_ref[...].astype(LOW_TYPE)
        all_sum[...] = jnp.zeros_like(all_sum)
        own_sum[...] = jnp.zeros_like(own_sum)

    weights = w_ref[0, 0]
    joint = joint_ref[0]
    query = query_ref[0]
    branch_grad = branch[...]
    merged_grad = matmul_low(branch_grad, weights[:, 576:]).astype(LOW_TYPE)
    grad_out = inner_rows(branch_grad, merged_ref[0])
    allowed = keys_ref[...] == own_ids_ref[...]
    key_grads, value_grads, query_grads = [], [], []
    for head in range(3):
        key = joint[:, HD * head : HD * (head + 1)]
        value = joint[:, 192 + HD * head : 192 + HD * (head + 1)]
        one_query = query[:, HD * head : HD * (head + 1)]
        one_merged = merged_grad[:, HD * head : HD * (head + 1)]
        scores = jnp.where(allowed, outer_rows(key, one_query) * SCALE, -1e30)
        probability = jnp.exp(scores - mass_ref[0, head : head + 1])
        value_grads.append(matmul_low(probability.astype(LOW_TYPE), one_merged))
        weighted = probability * outer_rows(value, one_merged)
        score_grad = (weighted - probability * row_sum(weighted)).astype(LOW_TYPE)
        key_grads.append(matmul_low(score_grad, one_query) * SCALE)
        query_grads.append(inner_rows(key, score_grad) * SCALE)
    joint_grad = jnp.concatenate(key_grads + value_grads, axis=1).astype(LOW_TYPE)
    query_grad = jnp.concatenate(query_grads, axis=0).T.astype(LOW_TYPE)
    all_sum[...] += outer_rows(joint_grad, weights[:, :384])
    own_sum[...] += outer_rows(query_grad, weights[:, 384:576])
    grad_joint = inner_rows(low_all_ref[...], joint_grad)
    grad_rest = jnp.concatenate([inner_rows(low_own_ref[...], query_grad), grad_out], axis=1)
    first_core = role_ref[0] == 0
    mine_ref[:, 0] = jnp.where(first_core, grad_joint, grad_rest).reshape(16, 48, 384)
    theirs = jnp.where(first_core, grad_rest, grad_joint).astype(LOW_TYPE)
    theirs_ref[:, 0] = theirs.reshape(16, 48, 384)

    @pl.when(head_set == 3)
    def _():
        gain = affine_ref[0:1]
        _, scaled, inverse = normed_rows(all_ref[...], gain, gain)
        all_grad_ref[...] = norm_pull(all_sum[...], scaled, inverse, gain)
        gain_grad = row_sum(all_sum[...] * scaled)
        offset_grad = row_sum(all_sum[...])
        _, scaled, inverse = normed_rows(own_ref[...], gain, gain)
        own_grad_ref[...] = norm_pull(own_sum[...], scaled, inverse, gain) + grad_ref[...]
        gain_grad += row_sum(own_sum[...] * scaled)
        offset_grad += row_sum(own_sum[...])
        affine_grad_ref[0:1] = gain_grad
        affine_grad_ref[1:2] = offset_grad
        affine_grad_ref[2:3] = row_sum(grad_ref[...])
        affine_grad_ref[3:8] = jnp.zeros((5, D), WIDE_TYPE)


def feed_forward_kernel(first_ref, affine_ref, up_ref, down_ref, out_ref, low_ref, before_ref, total):
    part = pl.program_id(0)

    @pl.when(part == 0)
    def _():
        first = first_ref[...]
        low_ref[...] = normed_rows(first, affine_ref[2:3], affine_ref[3:4])[0].astype(LOW_TYPE)
        total[...] = first + affine_ref[5:6]

    before = matmul_low(low_ref[...], up_ref[0, 0])
    before_ref[0] = before
    acted = before * (0.5 * (1.0 + lax.erf(before * (1.0 / math.sqrt(2.0)))))
    total[...] += outer_rows(acted.astype(LOW_TYPE), down_ref[0, 0])

    @pl.when(part == 3)
    def _():
        out_ref[...] = total[...]


def feed_backward_kernel(
    role_ref, grad_ref, first_ref, low_ref, before_ref, affine_ref, up_ref, down_ref,
    up_mine_ref, up_theirs_ref, down_mine_ref, down_theirs_ref, first_grad_ref, affine_grad_ref,
    down_grad, total,
):
    part = pl.program_id(0)

    @pl.when(part == 0)
    def _():
        down_grad[...] = grad_ref[...].astype(LOW_TYPE)
        total[...] = jnp.zeros_like(total)

    first_core = role_ref[0] == 0

    def give(values, mine_ref, theirs_ref):
        lower, upper = values[:, :384], values[:, 384:]
        mine_ref[:, 0] = jnp.where(first_core, lower, upper).reshape(16, 48, 384)
        theirs = jnp.where(first_core, upper, lower).astype(LOW_TYPE)
        theirs_ref[:, 0] = theirs.reshape(16, 48, 384)

    before = before_ref[0]
    half = 0.5 * (1.0 + lax.erf(before * (1.0 / math.sqrt(2.0))))
    acted = (before * half).astype(LOW_TYPE)
    give(inner_rows(down_grad[...], acted), down_mine_ref, down_theirs_ref)
    slope = half + before * jnp.exp(-0.5 * before * before) * (1.0 / math.sqrt(2.0 * math.pi))
    before_grad = (matmul_low(down_grad[...], down_ref[0, 0]) * slope).astype(LOW_TYPE)
    give(inner_rows(low_ref[...], before_grad), up_mine_ref, up_theirs_ref)
    total[...] += outer_rows(before_grad, up_ref[0, 0])

    @pl.when(part == 3)
    def _():
        gain = affine_ref[2:3]
        _, scaled, inverse = normed_rows(first_ref[...], gain, gain)
        first_grad_ref[...] = grad_ref[...] + norm_pull(total[...], scaled, inverse, gain)
        affine_grad_ref[0:1] = row_sum(total[...] * scaled)
        affine_grad_ref[1:2] = row_sum(total[...])
        affine_grad_ref[2:3] = row_sum(grad_ref[...])
        affine_grad_ref[3:8] = jnp.zeros((5, D), WIDE_TYPE)


def whole(shape):
    return pl.BlockSpec(shape, lambda part: (0,) * len(shape))


def weight_spec(which, column):
    return pl.BlockSpec((1, 1, D, D), lambda part: (which, part, 0, column))


def part_spec(*shape):
    return pl.BlockSpec((1,) + shape, lambda part: (part,) + (0,) * len(shape))


GRAD_SPEC = pl.BlockSpec((16, 1, 48, 384), lambda part: (0, part, 0, 0))
GRAD_WIDE = jax.ShapeDtypeStruct((16, 4, 48, 384), WIDE_TYPE)
GRAD_LOW = jax.ShapeDtypeStruct((16, 4, 48, 384), LOW_TYPE)
ROLE_SPEC = pl.BlockSpec(memory_space=pltpu.SMEM)


def cost(flops, moved_bytes):
    return pl.CostEstimate(flops=flops, bytes_accessed=moved_bytes, transcendentals=0)


def wide(*shape):
    return jax.ShapeDtypeStruct(shape, WIDE_TYPE)


def narrow(*shape):
    return jax.ShapeDtypeStruct(shape, LOW_TYPE)


def grid_call(kernel, in_specs, out_specs, out_shape, scratch, price, name):
    return pl.pallas_call(
        kernel,
        grid=(4,),
        in_specs=in_specs,
        out_specs=out_specs,
        out_shape=out_shape,
        scratch_shapes=scratch,
        compiler_params=pltpu.CompilerParams(
            dimension_semantics=("arbitrary",), vmem_limit_bytes=VMEM_BYTES
        ),
        cost_estimate=price,
        name=name,
    )


def block_forward(rows_all, rows_own, keys, own_ids, blocks, which, affine):
    total, count = rows_all.shape[0], rows_own.shape[0]
    saved_specs = (
        whole((total, D)), whole((count, D)), part_spec(total, 384), part_spec(count, 192),
        part_spec(3, count), part_spec(count, 192),
    )
    first, *saved = grid_call(
        attention_forward_kernel,
        [
            whole((total, D)), whole((count, D)), whole((total, 1)), whole((1, count)),
            whole((8, D)), weight_spec(which, 0),
        ],
        (whole((count, D)),) + saved_specs,
        (
            wide(count, D), narrow(total, D), narrow(count, D), narrow(4, total, 384),
            narrow(4, count, 192), wide(4, 3, count), narrow(4, count, 192),
        ),
        [pltpu.VMEM((count, D), WIDE_TYPE)],
        cost(2 * total * D * 2 * D + 24 * total * count * 256, 20 * total * D),
        "attention_forward",
    )(rows_all, rows_own, keys, own_ids, affine, blocks)
    result, low_two, before = grid_call(
        feed_forward_kernel,
        [whole((count, D)), whole((8, D)), weight_spec(which, 1), weight_spec(which, 2)],
        (whole((count, D)), whole((count, D)), part_spec(count, D)),
        (wide(count, D), narrow(count, D), wide(4, count, D)),
        [pltpu.VMEM((count, D), WIDE_TYPE)],
        cost(4 * count * D * FF, 4 * D * FF),
        "feed_forward",
    )(first, affine, blocks, blocks)
    return result, (rows_all, rows_own, keys, own_ids, saved, first, low_two, before)


def block_backward(upstream, kept, blocks, which, affine, role_array):
    rows_all, rows_own, keys, own_ids, saved, first, low_two, before = kept
    total, count = rows_all.shape[0], rows_own.shape[0]
    up_mine, up_theirs, down_mine, down_theirs, first_grad, affine_two = grid_call(
        feed_backward_kernel,
        [
            ROLE_SPEC, whole((count, D)), whole((count, D)), whole((count, D)),
            part_spec(count, D), whole((8, D)), weight_spec(which, 1), weight_spec(which, 2),
        ],
        (GRAD_SPEC,) * 4 + (whole((count, D)), whole((8, D))),
        (GRAD_WIDE, GRAD_LOW, GRAD_WIDE, GRAD_LOW, wide(count, D), wide(8, D)),
        [pltpu.VMEM((count, D), LOW_TYPE), pltpu.VMEM((count, D), WIDE_TYPE)],
        cost(8 * count * D * FF, 16 * D * FF),
        "feed_backward",
    )(role_array, upstream, first, low_two, before, affine, blocks, blocks)
    mine, theirs, all_grad, own_grad, affine_one = grid_call(
        attention_backward_kernel,
        [
            ROLE_SPEC, whole((count, D)), whole((total, D)), whole((count, D)),
            whole((total, 1)), whole((1, count)), whole((8, D)), weight_spec(which, 0),
            whole((total, D)), whole((count, D)), part_spec(total, 384), part_spec(count, 192),
            part_spec(3, count), part_spec(count, 192),
        ],
        (GRAD_SPEC, GRAD_SPEC, whole((total, D)), whole((count, D)), whole((8, D))),
        (GRAD_WIDE, GRAD_LOW, wide(total, D), wide(count, D), wide(8, D)),
        [
            pltpu.VMEM((count, D), LOW_TYPE),
            pltpu.VMEM((total, D), WIDE_TYPE),
            pltpu.VMEM((count, D), WIDE_TYPE),
        ],
        cost(4 * total * D * 2 * D + 24 * total * count * 640, 30 * total * D),
        "attention_backward",
    )(
        role_array, first_grad, rows_all, rows_own, keys, own_ids, affine, blocks, *saved
    )
    affine_grad = jnp.stack(
        [
            affine_one[0], affine_one[1], affine_two[0], affine_two[1],
            affine_one[2], affine_two[2],
        ]
    )
    grads = ((mine, theirs), (up_mine, up_theirs), (down_mine, down_theirs))
    return all_grad, own_grad, grads, affine_grad


def block_reduce(grads, places, step):
    sums = []
    for (mine, theirs), order in zip(grads, ORDERS):
        both = mine + send(theirs, partner_pairs()).astype(WIDE_TYPE)
        sums.append(torus_sum(both.reshape(4, 4, 4, 48, 384), order, places, step))
    return jnp.stack(sums)


def head_step(condition, clean, noise_rows, times_f, row_weight, tables, extras, role):
    w_entry, w_time_two, w_one, w_two, modulate = tables
    table_in, table_out = (extras[:, :C], extras[:, C : 2 * C])
    biases = extras[:, 2 * C : 2 * C + 11].astype(WIDE_TYPE).T
    w_cond, w_time = (w_entry[:, :D], w_entry[:, D:])
    half_turn = math.pi / 2
    angle_now = (times_f / HORIZON + COSINE_OFFSET) / (1.0 + COSINE_OFFSET) * half_turn
    start_cos = math.cos(COSINE_OFFSET / (1.0 + COSINE_OFFSET) * half_turn)
    signal_kept = (jnp.cos(angle_now) / start_cos) ** 2
    noisy_input = (
        jnp.sqrt(signal_kept)[:, None] * clean + jnp.sqrt(1.0 - signal_kept)[:, None] * noise_rows
    ).astype(LOW_TYPE)
    half_width = FREQ // 2
    frequency = jnp.exp(-math.log(10000.0) * jnp.arange(half_width, dtype=WIDE_TYPE) / half_width)
    angles = times_f[:, None] * frequency[None, :]
    features = jnp.concatenate([jnp.cos(angles), jnp.sin(angles)], axis=1).astype(LOW_TYPE)
    time_pre = outer_rows(features, w_time) + biases[1]
    time_act = jax.nn.silu(time_pre).astype(LOW_TYPE)
    time_vec = outer_rows(time_act, w_time_two) + biases[2]
    cond_pre = outer_rows(condition, w_cond) + biases[0] + time_vec
    cond_act = jax.nn.silu(cond_pre).astype(LOW_TYPE)
    modulation = outer_rows(cond_act, modulate) + biases[6:11].reshape(-1)
    shift_in, scale_in, gate_in, shift_out, scale_out = jnp.split(modulation, 5, axis=1)
    entry_x = outer_rows(noisy_input, table_in) + biases[3]
    normed_in, saved_in = plain_forward(entry_x)
    mod_in = (normed_in * (1.0 + scale_in) + shift_in).astype(LOW_TYPE)
    hidden_one = outer_rows(mod_in, w_one) + biases[4]
    hidden_act = jax.nn.silu(hidden_one).astype(LOW_TYPE)
    hidden_two = outer_rows(hidden_act, w_two) + biases[5]
    leaving = entry_x + gate_in * hidden_two
    normed_out, saved_out = plain_forward(leaving)
    mod_out = (normed_out * (1.0 + scale_out) + shift_out).astype(LOW_TYPE)
    predicted = matmul_low(mod_out, table_out)
    error = predicted - noise_rows
    loss_part = jnp.sum(row_weight * jnp.mean(error * error, axis=1))
    pred_grad = (row_weight[:, None] * (2.0 / C) * error).astype(LOW_TYPE)
    grad_table = inner_rows(pred_grad, mod_out)
    mod_out_grad = outer_rows(pred_grad, table_out)
    leaving_grad = plain_backward(mod_out_grad * (1.0 + scale_out), saved_out)
    two_grad = (leaving_grad * gate_in).astype(LOW_TYPE)
    one_grad = (matmul_low(two_grad, w_two) * silu_slope(hidden_one)).astype(LOW_TYPE)
    mod_in_grad = matmul_low(one_grad, w_one)
    entry_x_grad = (plain_backward(mod_in_grad * (1.0 + scale_in), saved_in) + leaving_grad).astype(
        LOW_TYPE
    )
    grad_input = inner_rows(noisy_input, entry_x_grad)
    modulation_grad = jnp.concatenate(
        [
            mod_in_grad,
            mod_in_grad * normed_in,
            leaving_grad * hidden_two,
            mod_out_grad,
            mod_out_grad * normed_out,
        ],
        axis=1,
    ).astype(LOW_TYPE)
    cond_grad = (matmul_low(modulation_grad, modulate) * silu_slope(cond_pre)).astype(LOW_TYPE)
    condition_grad = matmul_low(cond_grad, w_cond).astype(LOW_TYPE)
    time_grad = (matmul_low(cond_grad, w_time_two) * silu_slope(time_pre)).astype(LOW_TYPE)

    def shard(left, right):
        return split_grad(left, right, 1, role, True).reshape(4, 4, 4, -1, right.shape[1])

    square_grad = (
        shard(cond_grad, time_act),
        shard(one_grad, mod_in),
        shard(two_grad, hidden_act),
    )
    entry_grad = jnp.concatenate([shard(cond_grad, condition), shard(time_grad, features)], axis=4)
    modulate_grad = shard(modulation_grad, cond_act)
    grads = (
        jnp.concatenate(square_grad, axis=3),
        modulate_grad[:, :, :, :24],
        jnp.concatenate([modulate_grad[:, :, :, 24:], entry_grad], axis=3),
    )

    def column_sum(values):
        return jnp.sum(values.astype(WIDE_TYPE), axis=0)

    cond_bias = column_sum(cond_grad)
    rows = [cond_bias, column_sum(time_grad), cond_bias, column_sum(entry_x_grad)]
    rows = jnp.stack(rows + [column_sum(one_grad), column_sum(two_grad)])
    extra_grad = jnp.concatenate(
        [grad_input, grad_table, rows, column_sum(modulation_grad).reshape(5, -1)], axis=0
    )
    return loss_part, grads, extra_grad, condition_grad


def head_reduce(grads, places, step):
    return [torus_sum(part, order, places, step) for part, order in zip(grads, ORDERS)]


def per_device(
    latents,
    noise_draws,
    timesteps,
    buckets,
    visible_index,
    patch_embed,
    patch_embed_first,
    patch_embed_second,
    attention_in,
    attention_in_first,
    attention_in_second,
    attention_out,
    attention_out_first,
    attention_out_second,
    feedforward_in,
    feedforward_in_first,
    feedforward_in_second,
    feedforward_out,
    feedforward_out_first,
    feedforward_out_second,
    block_affine,
    block_affine_first,
    block_affine_second,
    head_entry,
    head_entry_first,
    head_entry_second,
    head_square,
    head_square_first,
    head_square_second,
    head_modulate,
    head_modulate_first,
    head_modulate_second,
):
    role = lax.axis_index("role")
    dp_index = lax.axis_index("dp")
    mp_index = lax.axis_index("mp")
    places = (role, dp_index // 4, dp_index % 4, mp_index)
    step = 1 - 2 * role
    slot = mp_index // 2
    quarter = (mp_index % 2) * 2 + role

    masked_counts = SEQ - jnp.sum((visible_index < SEQ).astype(jnp.int32), axis=1)
    wide_flags = buckets[:, 0]
    count_codes = jnp.stack([masked_counts // 32, masked_counts % 32, wide_flags]).astype(WIDE_TYPE)
    block_shard = jnp.concatenate(
        [
            attention_in[0].reshape(48, 3, 3, HD).transpose(0, 2, 1, 3)[:, (1, 2, 0)].reshape(48, 576),
            attention_out[0].T,
            feedforward_in[0],
            feedforward_out[0].T,
            jnp.pad(block_affine[0].T, ((0, 0), (0, 122))),
        ],
        axis=1,
    ).astype(LOW_TYPE)
    square_shard = head_square.transpose(0, 2, 1).astype(LOW_TYPE)
    entry_shard = head_entry[:SEQ].T.astype(LOW_TYPE)
    modulate_shard = head_modulate.T.astype(LOW_TYPE)
    extra_shard = jnp.concatenate(
        [
            jnp.pad(head_entry[SEQ:].T, ((0, 0), (0, 21))),
            jnp.pad(count_codes.reshape(1, 6), ((0, 7), (0, 58))),
        ],
        axis=1,
    ).astype(LOW_TYPE)
    blocks, squares_all, entry_all, modulate_all, extras = gather_weights(
        (block_shard, square_shard, entry_shard, modulate_shard, extra_shard)
    )
    blocks = blocks.reshape(2, 4, D, BLOCK_COLS)
    affine_all = blocks[:, 0, :, 2304:2312].transpose(0, 2, 1).astype(WIDE_TYPE)
    squares_all = squares_all.reshape(3, W, W)
    tables = (
        entry_all.reshape(W, SEQ),
        squares_all[0],
        squares_all[1],
        squares_all[2],
        modulate_all.reshape(5 * W, W),
    )
    codes = extras[0, :, :, 0, 0, 64:70].astype(WIDE_TYPE).reshape(16, 3, 2)
    counts = codes[:, 0] * 32.0 + codes[:, 1]
    wide_count = jnp.sum(counts * codes[:, 2])
    global_counts = jnp.stack([jnp.sum(counts) - wide_count, wide_count])
    shares = jnp.array(BUCKET_SHARE, dtype=WIDE_TYPE) / global_counts
    extras = extras.reshape(W, 128)
    role_array = jnp.reshape(role, (1,)).astype(jnp.int32)

    slot_latent = pick(latents, slot, 0)
    slot_noise = pick(noise_draws, slot, 0)
    slot_times = pick(timesteps, slot, 0)
    wide_flag = pick(wide_flags, slot, 0)
    visible = pick(visible_index, slot, 0)
    wide_image = wide_flag == 1
    visible_c = jnp.minimum(visible, SEQ - 1)
    visible_ok = visible < SEQ
    masked = masked_places(visible)
    masked_c = jnp.minimum(masked, SEQ - 1)
    masked_ok = masked < SEQ
    ids_visible = image_ids(visible_c, wide_image)
    ids_masked = image_ids(masked_c, wide_image)
    table = position_table()
    table_visible = positions(visible_c, wide_image, table)
    table_masked = positions(masked_c, wide_image, table)
    picked_latent = matmul_high(one_hot(visible_c, SEQ), slot_latent)

    def own(values, count):
        return lax.dynamic_slice_in_dim(values, quarter * count, count, 0)

    def key_column(ids, valid):
        return jnp.where(valid, ids, -1).astype(WIDE_TYPE)[:, None]

    def padded(values, fill):
        pads = ((0, MQP - MQ),) + ((0, 0),) * (values.ndim - 1)
        return jnp.pad(values, pads, constant_values=fill)

    embedded = matmul_high(picked_latent, patch_embed[:C]) + patch_embed[C] + table_visible
    encoded, enc_kept = block_forward(
        embedded,
        own(embedded, VQ),
        key_column(ids_visible, visible_ok),
        own(ids_visible, VQ).astype(WIDE_TYPE)[None],
        blocks,
        0,
        affine_all[0],
    )
    encoded = encoded.astype(LOW_TYPE)
    across = send(encoded, partner_pairs())
    pair = jnp.where(role == 0, jnp.stack([encoded, across]), jnp.stack([across, encoded]))
    pair = pair.reshape(2 * VQ, D)
    other = send(pair, neighbour_pairs())
    even = mp_index % 2 == 0
    received = jnp.where(even, jnp.stack([pair, other]), jnp.stack([other, pair]))
    received = received.reshape(VCAP, D).astype(WIDE_TYPE)

    dec_rows = jnp.concatenate(
        [patch_embed[C + 1] + table_masked, received + table_visible], axis=0
    )
    dec_ids = jnp.concatenate([ids_masked, ids_visible])
    dec_ok = jnp.concatenate([masked_ok, visible_ok])
    decoded, dec_kept = block_forward(
        dec_rows,
        padded(own(dec_rows, MQ), 0.0),
        key_column(dec_ids, dec_ok),
        padded(own(dec_ids, MQ), -2).astype(WIDE_TYPE)[None],
        blocks,
        1,
        affine_all[1],
    )
    condition = decoded.astype(LOW_TYPE)
    head_places = padded(own(masked, MQ), SEQ)
    chosen = one_hot(jnp.minimum(head_places, SEQ - 1), SEQ)
    facts = jnp.concatenate(
        [slot_latent, slot_noise, (slot_times + 1).astype(WIDE_TYPE)[:, None]], axis=1
    )
    facts = matmul_high(chosen, facts)
    row_weight = jnp.where(head_places < SEQ, shares[wide_flag], 0.0)
    loss_local, head_grads, extra_grad, condition_grad = head_step(
        condition,
        facts[:, :C],
        facts[:, C : 2 * C],
        facts[:, 2 * C],
        row_weight,
        tables,
        extras,
        role,
    )
    head_sums = head_reduce(head_grads, places, step)
    extra_half = half_of(extra_grad, 1, 1 - role)
    extra_half = half_of(extra_grad, 1, role) + send(extra_half, partner_pairs())
    extra_half = jnp.pad(extra_half.T, ((0, 0), (0, 85))).reshape(4, 4, 4, 8, 128)
    extra_sum = torus_sum(extra_half, ORDERS[0], places, step, WIDE_TYPE)
    dec_all_grad, dec_own_grad, dec_grads, dec_affine = block_backward(
        condition_grad.astype(WIDE_TYPE), dec_kept, blocks, 1, affine_all[1], role_array
    )
    dec_sum = block_reduce(dec_grads, places, step)
    mask_grad = jnp.sum(dec_all_grad[:MCAP], axis=0) + jnp.sum(dec_own_grad, axis=0)
    visible_grad = dec_all_grad[MCAP:].reshape(2, 2, VQ, D)
    mine = pick(visible_grad, mp_index % 2, 0)
    mine = mine + send(pick(visible_grad, 1 - mp_index % 2, 0), neighbour_pairs())
    returned = pick(mine, role, 0) + send(pick(mine, 1 - role, 0), partner_pairs())
    returned = returned.astype(LOW_TYPE).astype(WIDE_TYPE)
    enc_all_grad, enc_own_grad, enc_grads, enc_affine = block_backward(
        returned, enc_kept, blocks, 0, affine_all[0], role_array
    )
    enc_sum = block_reduce(enc_grads, places, step)
    picked_own = own(picked_latent, VQ)
    weight_grad = lax.dot_general(
        picked_latent, enc_all_grad, (((0,), (0,)), ((), ())), precision=lax.Precision.HIGHEST
    ) + lax.dot_general(
        picked_own, enc_own_grad, (((0,), (0,)), ((), ())), precision=lax.Precision.HIGHEST
    )
    bias_grad = jnp.sum(enc_all_grad, axis=0) + jnp.sum(enc_own_grad, axis=0)
    small = jnp.concatenate(
        [
            weight_grad,
            bias_grad[None],
            mask_grad[None],
            enc_affine,
            dec_affine,
            jnp.full((2, D), loss_local),
        ],
        axis=0,
    )
    small = sum_everywhere(small, 1)
    loss_total = small[30, 0]
    patch_total = small[: C + 2]
    affine_total = small[C + 2 : 30].reshape(2, 6, D)

    kept_sum = jnp.where(role == 0, enc_sum, dec_sum)
    given_sum = jnp.where(role == 0, dec_sum, enc_sum)
    taken_sum = send(given_sum, partner_pairs())
    lower = jnp.where(role == 0, kept_sum, taken_sum)
    upper = jnp.where(role == 0, taken_sum, kept_sum)

    attention_in_grad = jnp.stack(
        [
            upper[0, :, :192].reshape(48, 3, HD),
            lower[0, :, :192].reshape(48, 3, HD),
            lower[0, :, 192:].reshape(48, 3, HD),
        ],
        axis=2,
    ).reshape(1, 48, 3, 3 * HD)
    block_reduced = (
        attention_in_grad,
        upper[0, :, 192:].T[None],
        jnp.concatenate([lower[1], upper[1]], axis=1)[None],
        jnp.concatenate([lower[2], upper[2]], axis=1).T[None],
        lax.dynamic_slice(affine_total, (role, 0, dp_index * 48), (1, 6, 48)),
    )
    head_reduced = (
        jnp.concatenate([head_sums[2][16:].T, extra_sum[:, :43].T], axis=0),
        head_sums[0].reshape(3, 8, W).transpose(0, 2, 1),
        jnp.concatenate([head_sums[1], head_sums[2][:16]], axis=0).T,
    )
    squares = (
        sum((jnp.sum(item * item) for item in block_reduced[:4]))
        + jnp.sum(block_reduced[4] * block_reduced[4]) / 4
    )
    squares = (
        squares
        + sum((jnp.sum(item * item) for item in head_reduced))
        + jnp.sum(patch_total * patch_total) / 128
    )
    square_total = sum_everywhere(jnp.full((8, 128), squares), 2)[0, 0]
    grad_norm = jnp.sqrt(square_total)
    factor = jnp.minimum(1.0, CLIP_NORM / (grad_norm + 1e-06))
    params = (
        patch_embed,
        attention_in,
        attention_out,
        feedforward_in,
        feedforward_out,
        block_affine,
        head_entry,
        head_square,
        head_modulate,
    )
    firsts = (
        patch_embed_first,
        attention_in_first,
        attention_out_first,
        feedforward_in_first,
        feedforward_out_first,
        block_affine_first,
        head_entry_first,
        head_square_first,
        head_modulate_first,
    )
    seconds = (
        patch_embed_second,
        attention_in_second,
        attention_out_second,
        feedforward_in_second,
        feedforward_out_second,
        block_affine_second,
        head_entry_second,
        head_square_second,
        head_modulate_second,
    )
    gradients = (patch_total,) + tuple(block_reduced) + tuple(head_reduced)
    news = []
    for weight_now, first_now, second_now, grad_now in zip(params, firsts, seconds, gradients):
        news.extend(adam_update(weight_now, first_now, second_now, factor * grad_now))
    return (
        loss_total,
        grad_norm,
        news[0],
        news[1],
        news[2],
        news[3],
        news[4],
        news[5],
        news[6],
        news[7],
        news[8],
        news[9],
        news[10],
        news[11],
        news[12],
        news[13],
        news[14],
        news[15],
        news[16],
        news[17],
        news[18],
        news[19],
        news[20],
        news[21],
        news[22],
        news[23],
        news[24],
        news[25],
        news[26],
    )


def solution(mesh):
    placed = (
        P(None, "dp", None),
        P(None, "dp", None),
        P(None, "dp"),
        P(None, "dp"),
        P(None, "dp"),
        P(),
        P(),
        P(),
        P("role", "dp", "mp", None),
        P("role", "dp", "mp", None),
        P("role", "dp", "mp", None),
        P("role", "mp", "dp"),
        P("role", "mp", "dp"),
        P("role", "mp", "dp"),
        P("role", "dp", "mp"),
        P("role", "dp", "mp"),
        P("role", "dp", "mp"),
        P("role", "mp", "dp"),
        P("role", "mp", "dp"),
        P("role", "mp", "dp"),
        P("role", None, "dp"),
        P("role", None, "dp"),
        P("role", None, "dp"),
        P(None, ("role", "dp", "mp")),
        P(None, ("role", "dp", "mp")),
        P(None, ("role", "dp", "mp")),
        P(None, None, ("role", "dp", "mp")),
        P(None, None, ("role", "dp", "mp")),
        P(None, None, ("role", "dp", "mp")),
        P(None, ("role", "dp", "mp")),
        P(None, ("role", "dp", "mp")),
        P(None, ("role", "dp", "mp")),
    )
    return jax.shard_map(
        per_device,
        mesh=mesh,
        in_specs=placed,
        out_specs=(
            P(),
            P(),
            P(),
            P(),
            P(),
            P("role", "dp", "mp", None),
            P("role", "dp", "mp", None),
            P("role", "dp", "mp", None),
            P("role", "mp", "dp"),
            P("role", "mp", "dp"),
            P("role", "mp", "dp"),
            P("role", "dp", "mp"),
            P("role", "dp", "mp"),
            P("role", "dp", "mp"),
            P("role", "mp", "dp"),
            P("role", "mp", "dp"),
            P("role", "mp", "dp"),
            P("role", None, "dp"),
            P("role", None, "dp"),
            P("role", None, "dp"),
            P(None, ("role", "dp", "mp")),
            P(None, ("role", "dp", "mp")),
            P(None, ("role", "dp", "mp")),
            P(None, None, ("role", "dp", "mp")),
            P(None, None, ("role", "dp", "mp")),
            P(None, None, ("role", "dp", "mp")),
            P(None, ("role", "dp", "mp")),
            P(None, ("role", "dp", "mp")),
            P(None, ("role", "dp", "mp")),
        ),
        check_vma=False,
    )
```

```python
import math

import jax
import jax.numpy as jnp
from jax import lax
from jax.experimental import pallas as pl
from jax.experimental.pallas import tpu as pltpu
from jax.sharding import PartitionSpec as P

D = 768
HD = 64
C = 16
FREQ = 256
GRID = 32
STEP = 5
SEQ = 1024
VCAP = 320
MCAP = 864


LN_EPS = 1e-06
BETA_ONE = 0.9
BETA_TWO = 0.95
ADAM_EPS = 1e-08
DECAY = 0.02
RATE = 0.02
CLIP_NORM = 0.02
BUCKET_SHARE = (0.6, 0.4)
COSINE_OFFSET = 0.008
HORIZON = 1000.0
LOW_TYPE = jnp.bfloat16
WIDE_TYPE = jnp.float32


def matmul_low(left_side, right_side):
    return jnp.dot(left_side, right_side, preferred_element_type=WIDE_TYPE)


def matmul_high(left_side, right_side):
    return jnp.dot(left_side, right_side, precision=lax.Precision.HIGHEST)


def inner_rows(left_side, right_side):
    return lax.dot_general(
        left_side, right_side, (((0,), (0,)), ((), ())), preferred_element_type=WIDE_TYPE
    )


def outer_rows(left_side, right_side):
    return lax.dot_general(
        left_side, right_side, (((1,), (1,)), ((), ())), preferred_element_type=WIDE_TYPE
    )


def plain_forward(values):
    centered = values - jnp.mean(values, axis=-1, keepdims=True)
    spread = jnp.mean(centered * centered, axis=-1, keepdims=True)
    inverse = lax.rsqrt(spread + LN_EPS)
    scaled = centered * inverse
    return (scaled, (scaled, inverse))


def plain_backward(upstream, saved_norm):
    scaled, inverse = saved_norm
    return inverse * (
        upstream
        - jnp.mean(upstream, axis=-1, keepdims=True)
        - scaled * jnp.mean(upstream * scaled, axis=-1, keepdims=True)
    )


def silu_slope(values):
    sigmoid = jax.nn.sigmoid(values)
    return sigmoid * (1.0 + values * (1.0 - sigmoid))


QUARTER = 4
HE = 1067
MQ = MCAP // QUARTER
VQ = VCAP // QUARTER
HEADS = 12
FF = 3072
W = 1024
ALL = ("role", "dp", "mp")
SCALE = HD ** (-0.5)


def device_order():
    return [(r, x, z, y) for r in range(2) for x in range(4) for z in range(4) for y in range(4)]


def flat_index(r, x, z, y):
    return r * 64 + x * 16 + z * 4 + y


def partner_pairs():
    return [(flat_index(r, x, z, y), flat_index(1 - r, x, z, y)) for r, x, z, y in device_order()]


def neighbour_pairs():
    return [(flat_index(r, x, z, y), flat_index(r, x, z, y ^ 1)) for r, x, z, y in device_order()]


def send(value, pairs):
    return lax.ppermute(value, ALL, pairs)


def pick(value, index, dim):
    return lax.dynamic_index_in_dim(value, index, dim, keepdims=False)


ORDERS = ((1, 2, 3), (2, 3, 1), (3, 1, 2))


def block_position(places, wide_image, table):
    local = jnp.where(wide_image, places, places & 255)
    shift = jnp.where(wide_image, 5, 4)
    rows = lax.shift_right_logical(local, jnp.broadcast_to(shift, local.shape))
    cols = local & jnp.where(wide_image, 31, 15)
    grid = lax.broadcasted_iota(jnp.int32, (places.shape[0], GRID), 1)
    pair = [(side == grid).astype(WIDE_TYPE) for side in (rows, cols)]
    return jnp.concatenate([matmul_high(side, table) for side in pair], axis=1)


def as_row(column):
    return jnp.broadcast_to(column, (column.shape[0], 128)).T[0:1]


def pack_shards(ins, packed):
    joint, branch, up, down, affine, square, entry, modulate = ins
    block, squares, entry_out, modulate_out, extra = packed
    heads = [joint[head] for head in range(3)]

    def kind(index):
        return [head[:, HD * index : HD * (index + 1)] for head in heads]

    block[:, :768] = jnp.concatenate(kind(1) + kind(2) + kind(0) + [branch[...]], axis=1).astype(
        LOW_TYPE
    )
    block[:, 768:1536] = up[...].astype(LOW_TYPE)
    block[:, 1536:2304] = down[...].astype(LOW_TYPE)
    affine_rows = jnp.concatenate([affine[...], jnp.zeros((122, 48), WIDE_TYPE)], axis=0)
    block[:, 2304:] = affine_rows.T.astype(LOW_TYPE)
    squares[...] = square[...].astype(LOW_TYPE)
    entry_out[...] = entry[:, :SEQ].astype(LOW_TYPE)
    modulate_out[...] = modulate[...].astype(LOW_TYPE)
    tail = jnp.concatenate([entry[:, SEQ:], jnp.zeros((8, 85), WIDE_TYPE)], axis=1)
    return tail


def count_codes(buckets, visible):
    lane = lax.broadcasted_iota(jnp.int32, (1, 128), 1)
    row = jnp.zeros((1, 128), WIDE_TYPE)
    for slot in range(2):
        shown = jnp.sum((visible[slot] < SEQ).astype(WIDE_TYPE), axis=0, keepdims=True)
        masked = SEQ - shown
        high = jnp.floor(masked * (1.0 / 32.0))
        bucket = buckets[slot : slot + 1].astype(WIDE_TYPE)
        for index, value in enumerate((high, masked - 32.0 * high, bucket)):
            row = row + jnp.where(lane == 64 + 2 * index + slot, value, 0.0)
    return row


def prepare_rows(ins, outs):
    patch, facts, buckets, visible, table, trig = ins
    (
        embedded_out, embedded_own_out, enc_keys_out, enc_ids_out, rows_out, rows_own_out,
        dec_keys_out, dec_ids_out, noisy_out, features_out, noise_out, valid_out, left_out,
        left_own_out,
    ) = outs
    role, mp_index = lax.axis_index("role"), lax.axis_index("mp")
    slot = lax.div(mp_index, 2)
    quarter = lax.rem(mp_index, 2) * 2 + role
    wide_image = buckets[pl.ds(slot, 1)] == 1
    table = table[...]
    slot_facts = facts[slot]
    shown_col = visible[slot]
    lanes = lax.broadcasted_iota(jnp.int32, (1, SEQ), 1)

    def ids_of(places):
        return jnp.where(wide_image, 0, lax.shift_right_logical(places, jnp.full_like(places, 8)))

    def encoder_rows(column):
        places = jnp.minimum(column, SEQ - 1)
        chosen = (places == lanes).astype(WIDE_TYPE)
        picked = lax.dot_general(
            chosen, slot_facts, (((1,), (1,)), ((), ())), precision=lax.Precision.HIGHEST
        )
        place = block_position(places, wide_image, table)
        rows = matmul_high(picked[:, :C], patch[0:C]) + patch[C : C + 1] + place
        ones = jnp.ones((column.shape[0], 1), WIDE_TYPE)
        zeros = jnp.zeros((column.shape[0], 7), WIDE_TYPE)
        return rows, place, ids_of(places), jnp.concatenate([picked[:, :C], ones, zeros], axis=1)

    rows, place, ids, left = encoder_rows(shown_col)
    embedded_out[...] = rows
    left_out[...] = left
    visible_keys = jnp.where(shown_col < SEQ, ids, -1).astype(WIDE_TYPE)
    enc_keys_out[...] = visible_keys
    own_col = visible[slot, pl.ds(pl.multiple_of(quarter * VQ, 8), VQ)]
    rows, _, ids, left = encoder_rows(own_col)
    embedded_own_out[...] = rows
    left_own_out[...] = left
    enc_ids_out[...] = as_row(ids.astype(WIDE_TYPE))

    shown = jnp.max((shown_col == lanes).astype(WIDE_TYPE), axis=0, keepdims=True)
    masked = 1.0 - shown
    low = lax.broadcasted_iota(jnp.int32, (SEQ, SEQ), 0)
    high = lax.broadcasted_iota(jnp.int32, (SEQ, SEQ), 1)
    before = (low <= high).astype(LOW_TYPE)
    rank = matmul_low(jnp.broadcast_to(masked, (16, SEQ)).astype(LOW_TYPE), before)[0:1] - 1.0
    rank = jnp.where(masked > 0.0, rank, -1.0)
    total = jnp.sum(masked, axis=1, keepdims=True)

    def masked_rows(index):
        valid = index < total
        wanted = jnp.where(valid, index, -2.0)
        hit = jnp.where(valid, (rank == wanted).astype(WIDE_TYPE), (lanes == SEQ - 1).astype(WIDE_TYPE))
        places = jnp.sum(hit * lanes.astype(WIDE_TYPE), axis=1, keepdims=True).astype(jnp.int32)
        return hit, valid, places, patch[C + 1 : C + 2] + block_position(places, wide_image, table)

    index = lax.broadcasted_iota(jnp.int32, (MCAP, 1), 0).astype(WIDE_TYPE)
    _, valid, places, rows = masked_rows(index)
    rows_out[0:MCAP] = rows
    rows_out[MCAP:] = place
    dec_keys_out[0:MCAP] = jnp.where(valid, ids_of(places), -1).astype(WIDE_TYPE)
    dec_keys_out[MCAP:] = visible_keys
    inner = lax.broadcasted_iota(jnp.int32, (MQP, 1), 0)
    index = jnp.where(inner < MQ, inner + quarter * MQ, MCAP).astype(WIDE_TYPE)
    hit, valid, places, rows = masked_rows(index)
    rows_own_out[...] = rows
    ids = jnp.where(inner < MQ, ids_of(places), -2).astype(WIDE_TYPE)
    dec_ids_out[...] = as_row(ids)
    valid_out[...] = valid.astype(WIDE_TYPE)
    picked = lax.dot_general(
        hit, slot_facts, (((1,), (1,)), ((), ())), precision=lax.Precision.HIGHEST
    )
    noise_rows = picked[:, C : 2 * C]
    noise_out[...] = noise_rows
    noisy_out[...] = (picked[:, 33:34] * picked[:, :C] + picked[:, 34:35] * noise_rows).astype(
        LOW_TYPE
    )
    time = picked[:, 32:33].astype(jnp.int32)
    grid = lax.broadcasted_iota(jnp.int32, (MQP, GRID), 1)
    coarse = (lax.shift_right_logical(time, jnp.full_like(time, 5)) == grid).astype(WIDE_TYPE)
    fine = ((time & 31) == grid).astype(WIDE_TYPE)
    coarse = matmul_high(coarse, trig[:, :256])
    fine = matmul_high(fine, trig[:, 256:])
    cos_a, sin_a, cos_b, sin_b = coarse[:, :128], coarse[:, 128:], fine[:, :128], fine[:, 128:]
    features_out[:, :128] = (cos_a * cos_b - sin_a * sin_b).astype(LOW_TYPE)
    features_out[:, 128:] = (sin_a * cos_b + cos_a * sin_b).astype(LOW_TYPE)


BLOCK_COLS = 2432
PIECES = (
    ((0, 0, 0, BLOCK_COLS, 1280), (3, None, 0, 640, 384)),
    ((0, 16, 0, BLOCK_COLS, 1280), (3, None, 640, 384, 256), (2, None, 0, 1024, 512), (4, None, 0, 128, 128)),
    ((0, 32, 0, BLOCK_COLS, 1280), (1, None, 0, 1024, 512)),
)
GATHER_COPIES = 8 + 3 * 8 * 8


def mesh_place():
    dp_index = lax.axis_index("dp")
    role, mp_index = lax.axis_index("role"), lax.axis_index("mp")
    return (role, dp_index // 4, lax.rem(dp_index, 4), mp_index)


def mesh_device(place):
    return (place[0], place[1] * 4 + place[2], place[3])


def moved(place, axis, steps):
    target = list(place)
    count = 2 if axis == 0 else 4
    target[axis] = lax.rem(target[axis] + steps + count, count)
    return tuple(target)


def greet(place, moves):
    barrier = pltpu.get_barrier_semaphore()
    for axis, steps in moves:
        pl.semaphore_signal(
            barrier,
            inc=1,
            device_id=mesh_device(moved(place, axis, steps)),
            device_id_type=pl.DeviceIdType.MESH,
        )
    pl.semaphore_wait(barrier, len(moves))


RING_MOVES = ((0, 1), (1, 1), (1, -1), (2, 1), (2, -1), (3, 1), (3, -1))


def gather_kernel(*refs):
    shard_ins, row_ins, outs, row_outs = refs[:8], refs[8:14], refs[14:19], refs[19:33]
    packed, (send_sems, recv_sems, local_sems) = refs[33:38], refs[38:]
    ins = packed
    extra_row = count_codes(row_ins[2], row_ins[3])
    first_row = lax.broadcasted_iota(jnp.int32, (8, 128), 0) == 0
    tail = pack_shards(shard_ins, packed)
    packed[4][...] = (tail + jnp.where(first_row, extra_row, 0.0)).astype(LOW_TYPE)
    place = mesh_place()
    used = [0]

    def region(piece, spans, half):
        kind, row, column, width, cut = piece
        if half is not None:
            column, width = (column, cut) if half == 0 else (column + cut, width - cut)
        r = spans[0]
        x, z, y = (slice(None) if spans[axis] is None else spans[axis] for axis in (1, 2, 3))
        columns = pl.ds(column, width)
        if kind == 0:
            return outs[0].at[r, y, x, z, pl.ds(row, 16), columns]
        if kind == 1:
            return outs[1].at[:, r, x, z, y, :, columns]
        return outs[kind].at[r, x, z, y, :, columns]

    def start(unit, spans, half, axis, steps):
        copies = []
        for piece in PIECES[unit[0]]:
            if (piece[0] > 0) != unit[1] or (half == 1 and piece[3] == piece[4]):
                continue
            ref = region(piece, spans, half)
            slot = used[0]
            used[0] += 1
            copy = pltpu.make_async_remote_copy(
                src_ref=ref,
                dst_ref=ref,
                send_sem=send_sems.at[slot],
                recv_sem=recv_sems.at[slot],
                device_id=mesh_device(moved(place, axis, steps)),
                device_id_type=pl.DeviceIdType.MESH,
            )
            copy.start()
            copies.append(copy)
        return copies

    r, x, z, y = place
    own = {0: r, 1: x, 2: z, 3: y}
    targets = (
        outs[0].at[r, y, x, z], outs[1].at[:, r, x, z, y], outs[2].at[r, x, z, y],
        outs[3].at[r, x, z, y], outs[4].at[r, x, z, y],
    )
    placed = [
        pltpu.make_async_copy(source, target, local_sems.at[index])
        for index, (source, target) in enumerate(zip(ins, targets))
    ]
    for copy in placed:
        copy.start()
    greet(place, RING_MOVES)
    for copy in placed:
        copy.wait()
    pending, leaving = [], []
    units = [(third, stream) for stream in (0, 1) for third in range(3)]
    spans = {unit: dict(own) for unit in units}
    first, second = {}, {}

    def step_one(unit, stage):
        axis = ORDERS[unit[0]][stage]
        first[unit] = [start(unit, spans[unit], None, axis, steps) for steps in (1, -1)]

    for unit in units:
        step_one(unit, 0)
    for unit in units:
        pending += start(unit, spans[unit], None, 0, 1)
    for stage in range(3):
        if stage == 2:
            prepare_rows(row_ins, row_outs)
        for unit in units:
            axis = ORDERS[unit[0]][stage]
            batch = []
            for which, steps in ((0, 1), (1, -1)):
                came = dict(spans[unit])
                came[axis] = lax.rem(own[axis] - steps + 4, 4)
                for copy in first[unit][which]:
                    copy.wait_recv()
                batch.append(start(unit, came, which, axis, steps))
                pending += start(unit, came, None, 0, 1)
            second[unit] = batch
        for unit in units:
            axis = ORDERS[unit[0]][stage]
            came = dict(spans[unit])
            came[axis] = lax.rem(own[axis] + 2, 4)
            for which in (0, 1):
                for copy in second[unit][which]:
                    copy.wait_recv()
                pending += start(unit, came, which, 0, 1)
            for copies in first[unit] + second[unit]:
                leaving += copies
            spans[unit][axis] = None
            if stage < 2:
                step_one(unit, stage + 1)
    for copy in leaving:
        copy.wait_send()
    for copy in pending:
        copy.wait()


def gather_weights(shards, rows):
    whole_torus = (2, 4, 4, 4)
    held = pl.BlockSpec(memory_space=pltpu.VMEM)
    return pl.pallas_call(
        gather_kernel,
        out_shape=(
            narrow(*whole_torus, 48, BLOCK_COLS),
            narrow(3, *whole_torus, 8, W),
            narrow(*whole_torus, 8, W),
            narrow(*whole_torus, 40, W),
            narrow(*whole_torus, 8, 128),
            wide(VCAP, D), wide(VQ, D), wide(VCAP, 1), wide(1, VQ),
            wide(MCAP + VCAP, D), wide(MQP, D), wide(MCAP + VCAP, 1), wide(1, MQP),
            narrow(MQP, C), narrow(MQP, FREQ), wide(MQP, C), wide(MQP, 1),
            wide(VCAP, 24), wide(VQ, 24),
        ),
        in_specs=[held] * 14,
        out_specs=(pl.BlockSpec(memory_space=pl.ANY),) * 5 + (held,) * 14,
        scratch_shapes=[
            pltpu.VMEM((48, BLOCK_COLS), LOW_TYPE),
            pltpu.VMEM((3, 8, W), LOW_TYPE),
            pltpu.VMEM((8, W), LOW_TYPE),
            pltpu.VMEM((40, W), LOW_TYPE),
            pltpu.VMEM((8, 128), LOW_TYPE),
            pltpu.SemaphoreType.DMA((GATHER_COPIES,)),
            pltpu.SemaphoreType.DMA((GATHER_COPIES,)),
            pltpu.SemaphoreType.DMA((5,)),
        ],
        compiler_params=pltpu.CompilerParams(
            collective_id=0, has_side_effects=True, vmem_limit_bytes=VMEM_BYTES
        ),
        name="gather_weights",
    )(*shards, *rows)


SUM_MOVES = ((0, 1),) + tuple((axis, steps) for axis in (1, 2, 3) for steps in (1, 2, 3))


def position_table():
    frequency = 1.0 / 10000.0 ** (jnp.arange(D // 4, dtype=WIDE_TYPE) / (D // 4))
    angle = jnp.arange(GRID, dtype=WIDE_TYPE)[:, None] * frequency[None, :]
    return jnp.concatenate([jnp.sin(angle), jnp.cos(angle)], axis=1)


def time_tables():
    half_width = FREQ // 2
    frequency = jnp.exp(-math.log(10000.0) * jnp.arange(half_width, dtype=WIDE_TYPE) / half_width)
    fine = jnp.arange(32, dtype=WIDE_TYPE)[:, None] * frequency[None, :]
    angles = (32.0 * fine, fine)
    return jnp.concatenate([part(angle) for angle in angles for part in (jnp.cos, jnp.sin)], axis=1)


def kept_signal(timesteps):
    times_f = (timesteps + 1).astype(WIDE_TYPE)
    half_turn = math.pi / 2
    angle_now = (times_f / HORIZON + COSINE_OFFSET) / (1.0 + COSINE_OFFSET) * half_turn
    start_cos = math.cos(COSINE_OFFSET / (1.0 + COSINE_OFFSET) * half_turn)
    signal_kept = (jnp.cos(angle_now) / start_cos) ** 2
    return jnp.stack([times_f, jnp.sqrt(signal_kept), jnp.sqrt(1.0 - signal_kept)], axis=1)


def block_position(places, wide_image, table):
    local = jnp.where(wide_image, places, places & 255)
    shift = jnp.where(wide_image, 5, 4)
    rows = lax.shift_right_logical(local, jnp.broadcast_to(shift, local.shape))
    cols = local & jnp.where(wide_image, 31, 15)
    grid = lax.broadcasted_iota(jnp.int32, (places.shape[0], GRID), 1)
    pair = [(side == grid).astype(WIDE_TYPE) for side in (rows, cols)]
    return jnp.concatenate([matmul_high(side, table) for side in pair], axis=1)


def as_row(column):
    return jnp.broadcast_to(column, (column.shape[0], 128)).T[0:1]


def pack_shards(ins, packed):
    joint, branch, up, down, affine, square, entry, modulate = ins
    block, squares, entry_out, modulate_out, extra = packed
    heads = [joint[head] for head in range(3)]

    def kind(index):
        return [head[:, HD * index : HD * (index + 1)] for head in heads]

    block[:, :768] = jnp.concatenate(kind(1) + kind(2) + kind(0) + [branch[...]], axis=1).astype(
        LOW_TYPE
    )
    block[:, 768:1536] = up[...].astype(LOW_TYPE)
    block[:, 1536:2304] = down[...].astype(LOW_TYPE)
    affine_rows = jnp.concatenate([affine[...], jnp.zeros((122, 48), WIDE_TYPE)], axis=0)
    block[:, 2304:] = affine_rows.T.astype(LOW_TYPE)
    squares[...] = square[...].astype(LOW_TYPE)
    entry_out[...] = entry[:, :SEQ].astype(LOW_TYPE)
    modulate_out[...] = modulate[...].astype(LOW_TYPE)
    tail = jnp.concatenate([entry[:, SEQ:], jnp.zeros((8, 85), WIDE_TYPE)], axis=1)
    return tail


def count_codes(buckets, visible):
    lane = lax.broadcasted_iota(jnp.int32, (1, 128), 1)
    row = jnp.zeros((1, 128), WIDE_TYPE)
    for slot in range(2):
        shown = jnp.sum((visible[slot] < SEQ).astype(WIDE_TYPE), axis=0, keepdims=True)
        masked = SEQ - shown
        high = jnp.floor(masked * (1.0 / 32.0))
        bucket = buckets[slot : slot + 1].astype(WIDE_TYPE)
        for index, value in enumerate((high, masked - 32.0 * high, bucket)):
            row = row + jnp.where(lane == 64 + 2 * index + slot, value, 0.0)
    return row


def prepare_rows(ins, outs):
    patch, facts, buckets, visible, table, trig = ins
    (
        embedded_out, embedded_own_out, enc_keys_out, enc_ids_out, rows_out, rows_own_out,
        dec_keys_out, dec_ids_out, noisy_out, features_out, noise_out, valid_out, left_out,
        left_own_out,
    ) = outs
    role, mp_index = lax.axis_index("role"), lax.axis_index("mp")
    slot = lax.div(mp_index, 2)
    quarter = lax.rem(mp_index, 2) * 2 + role
    wide_image = buckets[pl.ds(slot, 1)] == 1
    table = table[...]
    slot_facts = facts[slot]
    shown_col = visible[slot]
    lanes = lax.broadcasted_iota(jnp.int32, (1, SEQ), 1)

    def ids_of(places):
        return jnp.where(wide_image, 0, lax.shift_right_logical(places, jnp.full_like(places, 8)))

    def encoder_rows(column):
        places = jnp.minimum(column, SEQ - 1)
        chosen = (places == lanes).astype(WIDE_TYPE)
        picked = lax.dot_general(
            chosen, slot_facts, (((1,), (1,)), ((), ())), precision=lax.Precision.HIGHEST
        )
        place = block_position(places, wide_image, table)
        rows = matmul_high(picked[:, :C], patch[0:C]) + patch[C : C + 1] + place
        ones = jnp.ones((column.shape[0], 1), WIDE_TYPE)
        zeros = jnp.zeros((column.shape[0], 7), WIDE_TYPE)
        return rows, place, ids_of(places), jnp.concatenate([picked[:, :C], ones, zeros], axis=1)

    rows, place, ids, left = encoder_rows(shown_col)
    embedded_out[...] = rows
    left_out[...] = left
    visible_keys = jnp.where(shown_col < SEQ, ids, -1).astype(WIDE_TYPE)
    enc_keys_out[...] = visible_keys
    own_col = visible[slot, pl.ds(pl.multiple_of(quarter * VQ, 8), VQ)]
    rows, _, ids, left = encoder_rows(own_col)
    embedded_own_out[...] = rows
    left_own_out[...] = left
    enc_ids_out[...] = as_row(ids.astype(WIDE_TYPE))

    shown = jnp.max((shown_col == lanes).astype(WIDE_TYPE), axis=0, keepdims=True)
    masked = 1.0 - shown
    low = lax.broadcasted_iota(jnp.int32, (SEQ, SEQ), 0)
    high = lax.broadcasted_iota(jnp.int32, (SEQ, SEQ), 1)
    before = (low <= high).astype(LOW_TYPE)
    rank = matmul_low(jnp.broadcast_to(masked, (16, SEQ)).astype(LOW_TYPE), before)[0:1] - 1.0
    rank = jnp.where(masked > 0.0, rank, -1.0)
    total = jnp.sum(masked, axis=1, keepdims=True)

    def masked_rows(index):
        valid = index < total
        wanted = jnp.where(valid, index, -2.0)
        hit = jnp.where(valid, (rank == wanted).astype(WIDE_TYPE), (lanes == SEQ - 1).astype(WIDE_TYPE))
        places = jnp.sum(hit * lanes.astype(WIDE_TYPE), axis=1, keepdims=True).astype(jnp.int32)
        return hit, valid, places, patch[C + 1 : C + 2] + block_position(places, wide_image, table)

    index = lax.broadcasted_iota(jnp.int32, (MCAP, 1), 0).astype(WIDE_TYPE)
    _, valid, places, rows = masked_rows(index)
    rows_out[0:MCAP] = rows
    rows_out[MCAP:] = place
    dec_keys_out[0:MCAP] = jnp.where(valid, ids_of(places), -1).astype(WIDE_TYPE)
    dec_keys_out[MCAP:] = visible_keys
    inner = lax.broadcasted_iota(jnp.int32, (MQP, 1), 0)
    index = jnp.where(inner < MQ, inner + quarter * MQ, MCAP).astype(WIDE_TYPE)
    hit, valid, places, rows = masked_rows(index)
    rows_own_out[...] = rows
    ids = jnp.where(inner < MQ, ids_of(places), -2).astype(WIDE_TYPE)
    dec_ids_out[...] = as_row(ids)
    valid_out[...] = valid.astype(WIDE_TYPE)
    picked = lax.dot_general(
        hit, slot_facts, (((1,), (1,)), ((), ())), precision=lax.Precision.HIGHEST
    )
    noise_rows = picked[:, C : 2 * C]
    noise_out[...] = noise_rows
    noisy_out[...] = (picked[:, 33:34] * picked[:, :C] + picked[:, 34:35] * noise_rows).astype(
        LOW_TYPE
    )
    time = picked[:, 32:33].astype(jnp.int32)
    grid = lax.broadcasted_iota(jnp.int32, (MQP, GRID), 1)
    coarse = (lax.shift_right_logical(time, jnp.full_like(time, 5)) == grid).astype(WIDE_TYPE)
    fine = ((time & 31) == grid).astype(WIDE_TYPE)
    coarse = matmul_high(coarse, trig[:, :256])
    fine = matmul_high(fine, trig[:, 256:])
    cos_a, sin_a, cos_b, sin_b = coarse[:, :128], coarse[:, 128:], fine[:, :128], fine[:, 128:]
    features_out[:, :128] = (cos_a * cos_b - sin_a * sin_b).astype(LOW_TYPE)
    features_out[:, 128:] = (sin_a * cos_b + cos_a * sin_b).astype(LOW_TYPE)


BLOCK_COLS = 2432
PIECES = (
    ((0, 0, 0, BLOCK_COLS, 1280), (3, None, 0, 640, 384)),
    ((0, 16, 0, BLOCK_COLS, 1280), (3, None, 640, 384, 256), (2, None, 0, 1024, 512), (4, None, 0, 128, 128)),
    ((0, 32, 0, BLOCK_COLS, 1280), (1, None, 0, 1024, 512)),
)
GATHER_COPIES = 8 + 3 * 8 * 8


def mesh_place():
    dp_index = lax.axis_index("dp")
    role, mp_index = lax.axis_index("role"), lax.axis_index("mp")
    return (role, dp_index // 4, lax.rem(dp_index, 4), mp_index)


def mesh_device(place):
    return (place[0], place[1] * 4 + place[2], place[3])


def moved(place, axis, steps):
    target = list(place)
    count = 2 if axis == 0 else 4
    target[axis] = lax.rem(target[axis] + steps + count, count)
    return tuple(target)


def greet(place, moves):
    barrier = pltpu.get_barrier_semaphore()
    for axis, steps in moves:
        pl.semaphore_signal(
            barrier,
            inc=1,
            device_id=mesh_device(moved(place, axis, steps)),
            device_id_type=pl.DeviceIdType.MESH,
        )
    pl.semaphore_wait(barrier, len(moves))


RING_MOVES = ((0, 1), (1, 1), (1, -1), (2, 1), (2, -1), (3, 1), (3, -1))


def gather_kernel(*refs):
    shard_ins, row_ins, outs, row_outs = refs[:8], refs[8:14], refs[14:19], refs[19:33]
    packed, (send_sems, recv_sems, local_sems) = refs[33:38], refs[38:]
    ins = packed
    extra_row = count_codes(row_ins[2], row_ins[3])
    first_row = lax.broadcasted_iota(jnp.int32, (8, 128), 0) == 0
    tail = pack_shards(shard_ins, packed)
    packed[4][...] = (tail + jnp.where(first_row, extra_row, 0.0)).astype(LOW_TYPE)
    place = mesh_place()
    used = [0]

    def region(piece, spans, half):
        kind, row, column, width, cut = piece
        if half is not None:
            column, width = (column, cut) if half == 0 else (column + cut, width - cut)
        r = spans[0]
        x, z, y = (slice(None) if spans[axis] is None else spans[axis] for axis in (1, 2, 3))
        columns = pl.ds(column, width)
        if kind == 0:
            return outs[0].at[r, y, x, z, pl.ds(row, 16), columns]
        if kind == 1:
            return outs[1].at[:, r, x, z, y, :, columns]
        return outs[kind].at[r, x, z, y, :, columns]

    def start(unit, spans, half, axis, steps):
        copies = []
        for piece in PIECES[unit[0]]:
            if (piece[0] > 0) != unit[1] or (half == 1 and piece[3] == piece[4]):
                continue
            ref = region(piece, spans, half)
            slot = used[0]
            used[0] += 1
            copy = pltpu.make_async_remote_copy(
                src_ref=ref,
                dst_ref=ref,
                send_sem=send_sems.at[slot],
                recv_sem=recv_sems.at[slot],
                device_id=mesh_device(moved(place, axis, steps)),
                device_id_type=pl.DeviceIdType.MESH,
            )
            copy.start()
            copies.append(copy)
        return copies

    r, x, z, y = place
    own = {0: r, 1: x, 2: z, 3: y}
    targets = (
        outs[0].at[r, y, x, z], outs[1].at[:, r, x, z, y], outs[2].at[r, x, z, y],
        outs[3].at[r, x, z, y], outs[4].at[r, x, z, y],
    )
    placed = [
        pltpu.make_async_copy(source, target, local_sems.at[index])
        for index, (source, target) in enumerate(zip(ins, targets))
    ]
    for copy in placed:
        copy.start()
    greet(place, RING_MOVES)
    for copy in placed:
        copy.wait()
    pending, leaving = [], []
    units = [(third, stream) for stream in (0, 1) for third in range(3)]
    spans = {unit: dict(own) for unit in units}
    first, second = {}, {}

    def step_one(unit, stage):
        axis = ORDERS[unit[0]][stage]
        first[unit] = [start(unit, spans[unit], None, axis, steps) for steps in (1, -1)]

    for unit in units:
        step_one(unit, 0)
    for unit in units:
        pending += start(unit, spans[unit], None, 0, 1)
    for stage in range(3):
        if stage == 2:
            prepare_rows(row_ins, row_outs)
        for unit in units:
            axis = ORDERS[unit[0]][stage]
            batch = []
            for which, steps in ((0, 1), (1, -1)):
                came = dict(spans[unit])
                came[axis] = lax.rem(own[axis] - steps + 4, 4)
                for copy in first[unit][which]:
                    copy.wait_recv()
                batch.append(start(unit, came, which, axis, steps))
                pending += start(unit, came, None, 0, 1)
            second[unit] = batch
        for unit in units:
            axis = ORDERS[unit[0]][stage]
            came = dict(spans[unit])
            came[axis] = lax.rem(own[axis] + 2, 4)
            for which in (0, 1):
                for copy in second[unit][which]:
                    copy.wait_recv()
                pending += start(unit, came, which, 0, 1)
            for copies in first[unit] + second[unit]:
                leaving += copies
            spans[unit][axis] = None
            if stage < 2:
                step_one(unit, stage + 1)
    for copy in leaving:
        copy.wait_send()
    for copy in pending:
        copy.wait()


def gather_weights(shards, rows):
    whole_torus = (2, 4, 4, 4)
    held = pl.BlockSpec(memory_space=pltpu.VMEM)
    return pl.pallas_call(
        gather_kernel,
        out_shape=(
            narrow(*whole_torus, 48, BLOCK_COLS),
            narrow(3, *whole_torus, 8, W),
            narrow(*whole_torus, 8, W),
            narrow(*whole_torus, 40, W),
            narrow(*whole_torus, 8, 128),
            wide(VCAP, D), wide(VQ, D), wide(VCAP, 1), wide(1, VQ),
            wide(MCAP + VCAP, D), wide(MQP, D), wide(MCAP + VCAP, 1), wide(1, MQP),
            narrow(MQP, C), narrow(MQP, FREQ), wide(MQP, C), wide(MQP, 1),
            wide(VCAP, 24), wide(VQ, 24),
        ),
        in_specs=[held] * 14,
        out_specs=(pl.BlockSpec(memory_space=pl.ANY),) * 5 + (held,) * 14,
        scratch_shapes=[
            pltpu.VMEM((48, BLOCK_COLS), LOW_TYPE),
            pltpu.VMEM((3, 8, W), LOW_TYPE),
            pltpu.VMEM((8, W), LOW_TYPE),
            pltpu.VMEM((40, W), LOW_TYPE),
            pltpu.VMEM((8, 128), LOW_TYPE),
            pltpu.SemaphoreType.DMA((GATHER_COPIES,)),
            pltpu.SemaphoreType.DMA((GATHER_COPIES,)),
            pltpu.SemaphoreType.DMA((5,)),
        ],
        compiler_params=pltpu.CompilerParams(
            collective_id=0, has_side_effects=True, vmem_limit_bytes=VMEM_BYTES
        ),
        name="gather_weights",
    )(*shards, *rows)


SUM_MOVES = ((0, 1),) + tuple((axis, steps) for axis in (1, 2, 3) for steps in (1, 2, 3))


MQP = 224
VMEM_BYTES = 60 * 1024 * 1024


def normed_rows(values, gain, offset):
    centered = values - jnp.mean(values, axis=-1, keepdims=True)
    inverse = lax.rsqrt(jnp.mean(centered * centered, axis=-1, keepdims=True) + LN_EPS)
    scaled = centered * inverse
    return scaled * gain + offset, scaled, inverse


def affine_rows(ref):
    return ref[0, 0].astype(WIDE_TYPE).T[0:8]


def norm_pull(upstream, scaled, inverse, gain):
    inner = upstream * gain
    return inverse * (
        inner
        - jnp.mean(inner, axis=-1, keepdims=True)
        - scaled * jnp.mean(inner * scaled, axis=-1, keepdims=True)
    )


def inner_high(left_side, right_side):
    dims = (((0,), (0,)), ((), ()))
    return lax.dot_general(left_side, right_side, dims, precision=lax.Precision.HIGHEST)


def row_sum(values):
    return jnp.sum(values, axis=0, keepdims=True)


def attention_forward_kernel(
    all_ref, own_ref, keys_ref, own_ids_ref, affine_ref, w_ref,
    first_ref, low_all_ref, low_own_ref, joint_ref, query_ref, mass_ref, merged_ref,
    total,
):
    head_set = pl.program_id(0)

    @pl.when(head_set == 0)
    def _():
        affine = affine_rows(affine_ref)
        gain, offset = affine[0:1], affine[1:2]
        low_all_ref[...] = normed_rows(all_ref[...], gain, offset)[0].astype(LOW_TYPE)
        low_own_ref[...] = normed_rows(own_ref[...], gain, offset)[0].astype(LOW_TYPE)
        total[...] = own_ref[...] + affine[4:5]

    weights = w_ref[0, 0]
    joint = matmul_low(low_all_ref[...], weights[:, :384]).astype(LOW_TYPE)
    query = matmul_low(low_own_ref[...], weights[:, 384:])[:, :192].astype(LOW_TYPE)
    joint_ref[0] = joint
    query_ref[0] = query
    allowed = keys_ref[...] == own_ids_ref[...]
    parts = []
    for head in range(3):
        key = joint[:, HD * head : HD * (head + 1)]
        value = joint[:, 192 + HD * head : 192 + HD * (head + 1)]
        scores = outer_rows(key, query[:, HD * head : HD * (head + 1)]) * SCALE
        scores = jnp.where(allowed, scores, -1e30)
        peak = jnp.max(scores, axis=0, keepdims=True)
        exponent = jnp.exp(scores - peak)
        mass = row_sum(exponent)
        probability = (exponent * (1.0 / mass)).astype(LOW_TYPE)
        mass_ref[0, head : head + 1] = peak + jnp.log(mass)
        parts.append(inner_rows(value, probability))
    merged = jnp.concatenate(parts, axis=0).T.astype(LOW_TYPE)
    merged_ref[0] = merged
    total[...] += outer_rows(merged, weights[:, 576:])

    @pl.when(head_set == 3)
    def _():
        first_ref[...] = total[...]


def attention_backward_kernel(
    role_ref, grad_ref, all_ref, own_ref, keys_ref, own_ids_ref, affine_ref, w_ref,
    low_all_ref, low_own_ref, joint_ref, query_ref, mass_ref, merged_ref, affine_two_ref,
    left_all_ref, left_own_ref,
    mine_ref, theirs_ref, tail_grad_ref, small_ref,
    branch, all_sum, own_sum,
):
    head_set = pl.program_id(0)

    @pl.when(head_set == 0)
    def _():
        branch[...] = grad_ref[...].astype(LOW_TYPE)
        all_sum[...] = jnp.zeros_like(all_sum)
        own_sum[...] = jnp.zeros_like(own_sum)

    weights = w_ref[0, 0]
    joint = joint_ref[0]
    query = query_ref[0]
    branch_grad = branch[...]
    merged_grad = matmul_low(branch_grad, weights[:, 576:]).astype(LOW_TYPE)
    grad_out = inner_rows(branch_grad, merged_ref[0])
    allowed = keys_ref[...] == own_ids_ref[...]
    key_grads, value_grads, query_grads = [], [], []
    for head in range(3):
        key = joint[:, HD * head : HD * (head + 1)]
        value = joint[:, 192 + HD * head : 192 + HD * (head + 1)]
        one_query = query[:, HD * head : HD * (head + 1)]
        one_merged = merged_grad[:, HD * head : HD * (head + 1)]
        scores = jnp.where(allowed, outer_rows(key, one_query) * SCALE, -1e30)
        probability = jnp.exp(scores - mass_ref[0, head : head + 1])
        value_grads.append(matmul_low(probability.astype(LOW_TYPE), one_merged))
        weighted = probability * outer_rows(value, one_merged)
        score_grad = (weighted - probability * row_sum(weighted)).astype(LOW_TYPE)
        key_grads.append(matmul_low(score_grad, one_query) * SCALE)
        query_grads.append(inner_rows(key, score_grad) * SCALE)
    joint_grad = jnp.concatenate(key_grads + value_grads, axis=1).astype(LOW_TYPE)
    query_grad = jnp.concatenate(query_grads, axis=0).T.astype(LOW_TYPE)
    all_sum[...] += outer_rows(joint_grad, weights[:, :384])
    own_sum[...] += outer_rows(query_grad, weights[:, 384:576])
    grad_joint = inner_rows(low_all_ref[...], joint_grad)
    grad_rest = jnp.concatenate([inner_rows(low_own_ref[...], query_grad), grad_out], axis=1)
    first_core = role_ref[0] == 0
    mine_ref[:, :, 0] = jnp.where(first_core, grad_joint, grad_rest).reshape(4, 4, 48, 384)
    theirs = jnp.where(first_core, grad_rest, grad_joint).astype(LOW_TYPE)
    theirs_ref[:, :, 0] = theirs.reshape(4, 4, 48, 384)

    @pl.when(head_set == 3)
    def _():
        gain = affine_rows(affine_ref)[0:1]
        _, scaled, inverse = normed_rows(all_ref[...], gain, gain)
        all_grad = norm_pull(all_sum[...], scaled, inverse, gain)
        skipped = all_ref.shape[0] - VCAP
        tail_grad_ref[...] = all_grad[skipped:]
        gain_grad = row_sum(all_sum[...] * scaled)
        offset_grad = row_sum(all_sum[...])
        _, scaled, inverse = normed_rows(own_ref[...], gain, gain)
        own_grad = norm_pull(own_sum[...], scaled, inverse, gain) + grad_ref[...]
        small_ref[...] = inner_high(left_all_ref[...], all_grad) + inner_high(
            left_own_ref[...], own_grad
        )
        small_ref[18:19] = gain_grad + row_sum(own_sum[...] * scaled)
        small_ref[19:20] = offset_grad + row_sum(own_sum[...])
        small_ref[20:22] = affine_two_ref[0:2]
        small_ref[22:23] = row_sum(grad_ref[...])
        small_ref[23:24] = affine_two_ref[2:3]


def feed_forward_kernel(first_ref, affine_ref, up_ref, down_ref, out_ref, low_ref, before_ref, total):
    part = pl.program_id(0)

    @pl.when(part == 0)
    def _():
        first = first_ref[...]
        affine = affine_rows(affine_ref)
        low_ref[...] = normed_rows(first, affine[2:3], affine[3:4])[0].astype(LOW_TYPE)
        total[...] = first + affine[5:6]

    before = matmul_low(low_ref[...], up_ref[0, 0])
    before_ref[0] = before
    acted = before * (0.5 * (1.0 + lax.erf(before * (1.0 / math.sqrt(2.0)))))
    total[...] += outer_rows(acted.astype(LOW_TYPE), down_ref[0, 0])

    @pl.when(part == 3)
    def _():
        out_ref[...] = total[...].astype(LOW_TYPE)


def feed_backward_kernel(
    role_ref, grad_ref, first_ref, low_ref, before_ref, affine_ref, up_ref, down_ref,
    up_mine_ref, up_theirs_ref, down_mine_ref, down_theirs_ref, first_grad_ref, affine_grad_ref,
    down_grad, total,
):
    part = pl.program_id(0)

    @pl.when(part == 0)
    def _():
        down_grad[...] = grad_ref[...].astype(LOW_TYPE)
        total[...] = jnp.zeros_like(total)

    first_core = role_ref[0] == 0

    def give(values, mine_ref, theirs_ref):
        lower, upper = values[:, :384], values[:, 384:]
        mine_ref[:, :, 0] = jnp.where(first_core, lower, upper).reshape(4, 4, 48, 384)
        theirs = jnp.where(first_core, upper, lower).astype(LOW_TYPE)
        theirs_ref[:, :, 0] = theirs.reshape(4, 4, 48, 384)

    before = before_ref[0]
    half = 0.5 * (1.0 + lax.erf(before * (1.0 / math.sqrt(2.0))))
    acted = (before * half).astype(LOW_TYPE)
    give(inner_rows(down_grad[...], acted), down_mine_ref, down_theirs_ref)
    slope = half + before * jnp.exp(-0.5 * before * before) * (1.0 / math.sqrt(2.0 * math.pi))
    before_grad = (matmul_low(down_grad[...], down_ref[0, 0]) * slope).astype(LOW_TYPE)
    give(inner_rows(low_ref[...], before_grad), up_mine_ref, up_theirs_ref)
    total[...] += outer_rows(before_grad, up_ref[0, 0])

    @pl.when(part == 3)
    def _():
        gain = affine_rows(affine_ref)[2:3]
        _, scaled, inverse = normed_rows(first_ref[...], gain, gain)
        first_grad_ref[...] = grad_ref[...] + norm_pull(total[...], scaled, inverse, gain)
        affine_grad_ref[0:1] = row_sum(total[...] * scaled)
        affine_grad_ref[1:2] = row_sum(total[...])
        affine_grad_ref[2:3] = row_sum(grad_ref[...])
        affine_grad_ref[3:8] = jnp.zeros((5, D), WIDE_TYPE)


def whole(shape):
    return pl.BlockSpec(shape, lambda part: (0,) * len(shape))


def weight_spec(which, column):
    return pl.BlockSpec((1, 1, D, D), lambda part: (which, part, 0, column))


def affine_spec(which):
    return pl.BlockSpec((1, 1, D, 128), lambda part: (which, 0, 0, 18))


def part_spec(*shape):
    return pl.BlockSpec((1,) + shape, lambda part: (part,) + (0,) * len(shape))


GRAD_SPEC = pl.BlockSpec((4, 4, 1, 48, 384), lambda part: (0, 0, part, 0, 0))
GRAD_WIDE = jax.ShapeDtypeStruct((4, 4, 4, 48, 384), WIDE_TYPE)
GRAD_LOW = jax.ShapeDtypeStruct((4, 4, 4, 48, 384), LOW_TYPE)
ROLE_SPEC = pl.BlockSpec(memory_space=pltpu.SMEM)


def cost(flops, moved_bytes):
    return pl.CostEstimate(flops=flops, bytes_accessed=moved_bytes, transcendentals=0)


def wide(*shape):
    return jax.ShapeDtypeStruct(shape, WIDE_TYPE)


def narrow(*shape):
    return jax.ShapeDtypeStruct(shape, LOW_TYPE)


def grid_call(kernel, in_specs, out_specs, out_shape, scratch, price, name):
    return pl.pallas_call(
        kernel,
        grid=(4,),
        in_specs=in_specs,
        out_specs=out_specs,
        out_shape=out_shape,
        scratch_shapes=scratch,
        compiler_params=pltpu.CompilerParams(
            dimension_semantics=("arbitrary",), vmem_limit_bytes=VMEM_BYTES
        ),
        cost_estimate=price,
        name=name,
    )


def block_forward(rows_all, rows_own, keys, own_ids, blocks, which):
    total, count = rows_all.shape[0], rows_own.shape[0]
    saved_specs = (
        whole((total, D)), whole((count, D)), part_spec(total, 384), part_spec(count, 192),
        part_spec(3, count), part_spec(count, 192),
    )
    first, *saved = grid_call(
        attention_forward_kernel,
        [
            whole((total, D)), whole((count, D)), whole((total, 1)), whole((1, count)),
            affine_spec(which), weight_spec(which, 0),
        ],
        (whole((count, D)),) + saved_specs,
        (
            wide(count, D), narrow(total, D), narrow(count, D), narrow(4, total, 384),
            narrow(4, count, 192), wide(4, 3, count), narrow(4, count, 192),
        ),
        [pltpu.VMEM((count, D), WIDE_TYPE)],
        cost(2 * total * D * 2 * D + 24 * total * count * 256, 20 * total * D),
        "attention_forward",
    )(rows_all, rows_own, keys, own_ids, blocks, blocks)
    result, low_two, before = grid_call(
        feed_forward_kernel,
        [whole((count, D)), affine_spec(which), weight_spec(which, 1), weight_spec(which, 2)],
        (whole((count, D)), whole((count, D)), part_spec(count, D)),
        (narrow(count, D), narrow(count, D), wide(4, count, D)),
        [pltpu.VMEM((count, D), WIDE_TYPE)],
        cost(4 * count * D * FF, 4 * D * FF),
        "feed_forward",
    )(first, blocks, blocks, blocks)
    return result, (rows_all, rows_own, keys, own_ids, saved, first, low_two, before)


def block_backward(upstream, kept, blocks, which, role_array, left_all, left_own):
    rows_all, rows_own, keys, own_ids, saved, first, low_two, before = kept
    total, count = rows_all.shape[0], rows_own.shape[0]
    up_mine, up_theirs, down_mine, down_theirs, first_grad, affine_two = grid_call(
        feed_backward_kernel,
        [
            ROLE_SPEC, whole((count, D)), whole((count, D)), whole((count, D)),
            part_spec(count, D), affine_spec(which), weight_spec(which, 1), weight_spec(which, 2),
        ],
        (GRAD_SPEC,) * 4 + (whole((count, D)), whole((8, D))),
        (GRAD_WIDE, GRAD_LOW, GRAD_WIDE, GRAD_LOW, wide(count, D), wide(8, D)),
        [pltpu.VMEM((count, D), LOW_TYPE), pltpu.VMEM((count, D), WIDE_TYPE)],
        cost(8 * count * D * FF, 16 * D * FF),
        "feed_backward",
    )(role_array, upstream, first, low_two, before, blocks, blocks, blocks)
    mine, theirs, tail_grad, small = grid_call(
        attention_backward_kernel,
        [
            ROLE_SPEC, whole((count, D)), whole((total, D)), whole((count, D)),
            whole((total, 1)), whole((1, count)), affine_spec(which), weight_spec(which, 0),
            whole((total, D)), whole((count, D)), part_spec(total, 384), part_spec(count, 192),
            part_spec(3, count), part_spec(count, 192), whole((8, D)), whole((total, 24)),
            whole((count, 24)),
        ],
        (GRAD_SPEC, GRAD_SPEC, whole((VCAP, D)), whole((24, D))),
        (GRAD_WIDE, GRAD_LOW, wide(VCAP, D), wide(24, D)),
        [
            pltpu.VMEM((count, D), LOW_TYPE),
            pltpu.VMEM((total, D), WIDE_TYPE),
            pltpu.VMEM((count, D), WIDE_TYPE),
        ],
        cost(4 * total * D * 2 * D + 24 * total * count * 640, 30 * total * D),
        "attention_backward",
    )(
        role_array, first_grad, rows_all, rows_own, keys, own_ids, blocks, blocks, *saved,
        affine_two, left_all, left_own,
    )
    mine_all = (mine, up_mine, down_mine)
    theirs_all = (theirs, up_theirs, down_theirs)
    grads = list(zip(mine_all, theirs_all))
    return tail_grad, grads, small


B_FIRST = (True, False, True)
FAMILIES = (("blk", "head"), ("blk", "head"), ("blk", "head", "ext"))
UNITS = tuple((third, stream) for stream in (0, 1) for third in range(3))
NAMES = {
    unit: [name for name in FAMILIES[unit[0]] if (name == "blk") == (unit[1] == 1)] for unit in UNITS
}
TAILS = {"blk": (2, 48, 384), "head": (24, 1024), "ext": (8, 128)}
REDUCE_COPIES = 384
SMALL_ROWS = 32


def reduce_kernel(*refs):
    mine, theirs, ext = refs[0:9], refs[9:18], refs[18]
    enc_small, dec_small, loss = refs[19:22]
    kept_out, taken_out, head_out, ext_out, small_out, norm_out = refs[22:28]
    crossed = refs[28:38]
    scratch = list(refs[38:])
    third_refs = [dict() for _ in range(3)]
    for third in range(3):
        for name in FAMILIES[third]:
            third_refs[third][name] = {
                key: scratch.pop(0)
                for key in ("pool", "give", "rest", "come", "last", "b_come", "b_last", "c_come", "c_last")
            }
    pool_low = [{name: scratch.pop(0) for name in FAMILIES[third]} for third in range(3)]
    hand, small_held, small_slots, norm_held, norm_slots = scratch[:5]
    send_sems, recv_sems, load_sems = scratch[5:]
    place = mesh_place()
    used = [0, 0]
    flying = []

    def push(source, target, axis, steps):
        slot = used[0]
        used[0] += 1
        copy = pltpu.make_async_remote_copy(
            src_ref=source,
            dst_ref=target,
            send_sem=send_sems.at[slot],
            recv_sem=recv_sems.at[slot],
            device_id=mesh_device(moved(place, axis, steps)),
            device_id_type=pl.DeviceIdType.MESH,
        )
        copy.start()
        flying.append(copy)
        return copy

    def sent(copies):
        for copy in copies:
            copy.wait_send()
            flying[:] = [other for other in flying if other is not copy]

    def load(source, target):
        copy = pltpu.make_async_copy(source, target, load_sems.at[used[1]])
        used[1] += 1
        copy.start()
        return copy

    def half_spans(third, steps, half):
        first, second, _ = ORDERS[third]
        spans = [slice(None)] * 3
        spans[first - 1] = lax.rem(place[first] + steps + 4, 4)
        spans[second - 1] = pl.ds(2 * half, 2)
        return spans

    def arrays(unit):
        third, stream = unit
        group, low = third_refs[third], pool_low[third]
        if stream == 1:
            for block in range(2):
                index = 3 * block + third
                pools = group["blk"]["pool"].at[:, :, block], low["blk"].at[:, :, block]
                yield mine[index], theirs[index], crossed[index], *pools
            return
        index = 6 + third
        yield mine[index], theirs[index], crossed[index], group["head"]["pool"], low["head"]
        if third == 2:
            given = ext.at[1 - place[0]]
            yield ext.at[place[0]], given, crossed[9], group["ext"]["pool"], low["ext"]

    def cross(unit, steps, half):
        spans = half_spans(unit[0], steps, half)
        crossing[unit, steps, half] = [
            push(given.at[*spans], landed.at[*spans], 0, 1)
            for _, given, landed, _, _ in arrays(unit)
        ]

    def fetch(unit, steps, half):
        spans = half_spans(unit[0], steps, half)
        spot = lead(unit[0], pl.ds(2 * half, 2), slice(None))
        copies = []
        for crossed_copy, (kept, _, landed, pool, low) in zip(
            crossing[unit, steps, half], arrays(unit)
        ):
            copies.append(load(kept.at[*spans], pool.at[*spot]))
            crossed_copy.wait_recv()
            copies.append(load(landed.at[*spans], low.at[*spot]))
        return copies

    def lead(third, b, c):
        return (b, c) if B_FIRST[third] else (c, b)

    def values(third, name, b, c):
        spot = lead(third, b, c)
        total = third_refs[third][name]["pool"][spot]
        return total + pool_low[third][name][spot].astype(WIDE_TYPE)

    def halves(unit, half, body):
        def step(count, carry):
            inner, c = lax.div(count, 4), lax.rem(count, 4)
            for name in NAMES[unit]:
                body(name, inner, c, 2 * half + inner)
            return carry

        lax.fori_loop(0, 8, step, 0)

    def small_stage(held, slots, stage):
        axis = (0, 3, 1, 2)[stage]
        count = 2 if axis == 0 else 4
        copies = [
            push(held.at[stage], slots.at[stage, place[axis]], axis, steps)
            for steps in range(1, count)
        ]
        slots[stage, place[axis]] = held[stage]

        def finish():
            for copy in copies:
                copy.wait_recv()
            total = slots[stage, 0]
            for index in range(1, count):
                total = total + slots[stage, index]
            held[stage + 1] = total

        return finish

    def arrive(copies):
        for copy in copies:
            copy.wait()

    def received(copies):
        for copy in copies:
            copy.wait_recv()

    def both(unit, *steps):
        return [fetch(unit, step, half) for half, step in enumerate(steps)]

    greet(place, SUM_MOVES)
    crossing = {}
    for pair in ((2, 2), (-1, 1), (1, -1), (0, 0)):
        for unit in UNITS:
            for half in (0, 1):
                cross(unit, pair[half], half)
    loads = {unit: both(unit, 2, 2) for unit in UNITS}
    small_held[0, 0:24] = enc_small[...]
    small_held[0, 0:18] += dec_small[0:18]
    small_held[0, 24:30] = dec_small[18:24]
    small_held[0, 30:32] = jnp.concatenate([loss[0:2]] * 6, axis=1)
    small = small_stage(small_held, small_slots, 0)

    first, last = ({unit: [] for unit in UNITS} for _ in range(2))
    for unit in UNITS:
        third = unit[0]
        group = third_refs[third]
        for half in (0, 1):
            arrive(loads[unit][half])

            def give(name, inner, c, b, half=half, third=third, unit=unit, group=group):
                total = values(third, name, b, c).astype(LOW_TYPE)
                group[name]["give"][half, inner, c] = total

            halves(unit, half, give)
            first[unit].append(
                [
                    push(
                        group[name]["give"].at[half],
                        group[name]["come"].at[half],
                        ORDERS[third][0],
                        1 - 2 * half,
                    )
                    for name in NAMES[unit]
                ]
            )
        loads[unit] = both(unit, -1, 1)
    small()
    small = small_stage(small_held, small_slots, 1)

    for unit in UNITS:
        third = unit[0]
        group = third_refs[third]
        for way in (1, 0):
            arrive(loads[unit][1 - way])

            def keep(name, inner, c, b, way=way, third=third, unit=unit, group=group):
                group[name]["rest"][way, inner, c] = values(third, name, b, c).astype(LOW_TYPE)

            halves(unit, 1 - way, keep)
            for name in NAMES[unit]:
                refs_of = group[name]
                source, target = refs_of["rest"].at[way], refs_of["last"].at[way, 1 - way]
                last[unit].append(push(source, target, ORDERS[third][0], 1 - 2 * way))
        loads[unit] = both(unit, 1, -1)
    small()
    small = small_stage(small_held, small_slots, 2)
    for unit in UNITS:
        third = unit[0]
        group = third_refs[third]
        for way in (0, 1):
            arrive(loads[unit][way])
            received(first[unit][way])

            def join(name, inner, c, b, way=way, third=third, unit=unit, group=group):
                total = values(third, name, b, c)
                total = total + group[name]["come"][way, inner, c].astype(WIDE_TYPE)
                group[name]["come"][way, inner, c] = total.astype(LOW_TYPE)

            halves(unit, way, join)
            for name in NAMES[unit]:
                refs_of = group[name]
                source, target = refs_of["come"].at[way], refs_of["last"].at[way, way]
                last[unit].append(push(source, target, ORDERS[third][0], 1 - 2 * way))
        loads[unit] = both(unit, 0, 0)
    small()
    small = small_stage(small_held, small_slots, 3)

    second, ready = ({unit: [] for unit in UNITS} for _ in range(2))
    for unit in UNITS:
        third = unit[0]
        axis = ORDERS[third][1]
        group = third_refs[third]
        received(last[unit])
        for half in (0, 1):
            arrive(loads[unit][half])

            def total_up(name, inner, c, b, half=half, third=third, unit=unit, group=group):
                total = values(third, name, b, c)
                for way in (0, 1):
                    total = total + group[name]["last"][way, half, inner, c].astype(WIDE_TYPE)
                group[name]["pool"][lead(third, b, c)] = total

            halves(unit, half, total_up)
            sent(first[unit][half])

        def pack(b, spot, start, third=third, unit=unit, group=group):
            for name in NAMES[unit]:
                refs_of = group[name]
                for c in (start, start + 1):
                    total = refs_of["pool"][lead(third, b, c)]
                    refs_of["give"][(*spot, c)] = total.astype(LOW_TYPE)

        opposite = lax.rem(place[axis] + 2, 4)
        for way in (0, 1):
            pack(opposite, (0, 0), 2 * way)
            second[unit].append(
                [
                    push(
                        group[name]["give"].at[0, 0, pl.ds(2 * way, 2)],
                        group[name]["b_come"].at[way],
                        axis,
                        1 - 2 * way,
                    )
                    for name in NAMES[unit]
                ]
            )
        for way, spot in ((0, (0, 1)), (1, (1, 0))):
            steps = 1 - 2 * way
            pack(lax.rem(place[axis] + steps + 4, 4), spot, 2 - 2 * way)
            part = pl.ds(2 - 2 * way, 2)
            for name in NAMES[unit]:
                refs_of = group[name]
                source, target = refs_of["give"].at[*spot, part], refs_of["b_last"].at[way, part]
                ready[unit].append(push(source, target, axis, steps))
    small()
    small_out[...] = small_held[4]
    for unit in UNITS:
        third = unit[0]
        axis = ORDERS[third][1]
        group = third_refs[third]
        for way, spot in ((0, (0, 1)), (1, (1, 0))):
            steps = 1 - 2 * way
            b = lax.rem(place[axis] + steps + 4, 4)
            received(second[unit][way])
            part = pl.ds(2 * way, 2)
            for name in NAMES[unit]:
                refs_of = group[name]
                for inner in range(2):
                    c = 2 * way + inner
                    total = refs_of["pool"][lead(third, b, c)]
                    total = total + refs_of["b_come"][way, inner].astype(WIDE_TYPE)
                    refs_of["give"][(*spot, c)] = total.astype(LOW_TYPE)
                source, target = refs_of["give"].at[*spot, part], refs_of["b_last"].at[way, part]
                ready[unit].append(push(source, target, axis, steps))

    second, last = ({unit: [] for unit in UNITS} for _ in range(2))
    for unit in UNITS:
        third = unit[0]
        axis = ORDERS[third][2]
        own_b = place[ORDERS[third][1]]
        group = third_refs[third]
        received(ready[unit])
        for name in NAMES[unit]:
            refs_of = group[name]
            for c in range(4):
                total = refs_of["pool"][lead(third, own_b, c)]
                for way in (0, 1):
                    total = total + refs_of["b_last"][way, c].astype(WIDE_TYPE)
                refs_of["pool"][lead(third, own_b, c)] = total
        pieces = c_pieces(unit)
        spot = lead(third, own_b, lax.rem(place[axis] + 2, 4))
        for way in (0, 1):
            second[unit].append(
                [
                    push(
                        group[name]["pool"].at[(*spot, *piece)],
                        group[name]["c_come"].at[piece],
                        axis,
                        1 - 2 * way,
                    )
                    for name, piece in pieces[way]
                ]
            )
        for way in (0, 1):
            steps = 1 - 2 * way
            spot = lead(third, own_b, lax.rem(place[axis] + steps + 4, 4))
            for name, piece in pieces[1 - way]:
                source = group[name]["pool"].at[(*spot, *piece)]
                target = group[name]["c_last"].at[(way, *piece)]
                last[unit].append(push(source, target, axis, steps))
    for unit in UNITS:
        third = unit[0]
        axis = ORDERS[third][2]
        own_b = place[ORDERS[third][1]]
        group = third_refs[third]
        pieces = c_pieces(unit)
        for way in (0, 1):
            steps = 1 - 2 * way
            spot = lead(third, own_b, lax.rem(place[axis] + steps + 4, 4))
            received(second[unit][way])
            for name, piece in pieces[way]:
                refs_of = group[name]
                refs_of["pool"][(*spot, *piece)] += refs_of["c_come"][piece]
                source = refs_of["pool"].at[(*spot, *piece)]
                target = refs_of["c_last"].at[(way, *piece)]
                last[unit].append(push(source, target, axis, steps))
    squares_sum = jnp.zeros((), WIDE_TYPE)
    handed = []
    for unit in UNITS:
        third = unit[0]
        axis = ORDERS[third][2]
        spot = lead(third, place[ORDERS[third][1]], place[axis])
        for copy in last[unit]:
            copy.wait_recv()
        for name in NAMES[unit]:
            refs_of = third_refs[third][name]
            total = refs_of["pool"][spot] + (refs_of["c_last"][0] + refs_of["c_last"][1])
            refs_of["pool"][spot] = total
            squares_sum += jnp.sum(total * total)
            if name == "head":
                head_out[third] = total
            if name == "ext":
                ext_out[...] = total
        if unit[1] == 0:
            continue
        blk = third_refs[third]["blk"]["pool"]
        handed.append(push(blk.at[(*spot, 1 - place[0])], hand.at[third], 0, 1))
        kept_out[third] = blk[(*spot, place[0])]
    small_total = small_held[4, 0:30]
    squares_sum += jnp.sum(small_total * small_total) * (1.0 / 128.0)
    norm_held[0] = jnp.full((8, 128), squares_sum)
    for stage in range(4):
        small_stage(norm_held, norm_slots, stage)()
    norm_out[...] = norm_held[4]
    for copy in handed:
        copy.wait_recv()
    taken_out[...] = hand[...]
    for copy in list(flying):
        copy.wait_send()


def c_pieces(unit):
    everything = slice(None)
    if unit[1] == 1:
        return [("blk", (0,))], [("blk", (1,))]
    lower = [("head", (everything, pl.ds(0, 512)))]
    upper = [("head", (everything, pl.ds(512, 512)))]
    if unit[0] == 2:
        lower.append(("ext", (everything, everything)))
    return lower, upper


def reduce_gradients(mine, theirs, ext, enc_small, dec_small, loss):
    scratch = []
    for third in range(3):
        for name in FAMILIES[third]:
            tail = TAILS[name]
            scratch += [
                pltpu.VMEM((4, 4) + tail, WIDE_TYPE),
                pltpu.VMEM((2, 2, 4) + tail, LOW_TYPE),
                pltpu.VMEM((2, 2, 4) + tail, LOW_TYPE),
                pltpu.VMEM((2, 2, 4) + tail, LOW_TYPE),
                pltpu.VMEM((2, 2, 2, 4) + tail, LOW_TYPE),
                pltpu.VMEM((2, 2) + tail, LOW_TYPE),
                pltpu.VMEM((2, 4) + tail, LOW_TYPE),
                pltpu.VMEM(tail, WIDE_TYPE),
                pltpu.VMEM((2,) + tail, WIDE_TYPE),
            ]
    for third in range(3):
        for name in FAMILIES[third]:
            kind = WIDE_TYPE if name == "ext" else LOW_TYPE
            scratch.append(pltpu.VMEM((4, 4) + TAILS[name], kind))
    scratch += [
        pltpu.VMEM((3, 48, 384), WIDE_TYPE),
        pltpu.VMEM((5, SMALL_ROWS, D), WIDE_TYPE),
        pltpu.VMEM((4, 4, SMALL_ROWS, D), WIDE_TYPE),
        pltpu.VMEM((5, 8, 128), WIDE_TYPE),
        pltpu.VMEM((4, 4, 8, 128), WIDE_TYPE),
        pltpu.SemaphoreType.DMA((REDUCE_COPIES,)),
        pltpu.SemaphoreType.DMA((REDUCE_COPIES,)),
        pltpu.SemaphoreType.DMA((256,)),
    ]
    held = pl.BlockSpec(memory_space=pltpu.VMEM)
    return pl.pallas_call(
        reduce_kernel,
        out_shape=(
            wide(3, 48, 384),
            wide(3, 48, 384),
            wide(3, 24, 1024),
            wide(8, 128),
            wide(SMALL_ROWS, D),
            wide(8, 128),
        )
        + (narrow(4, 4, 4, 48, 384),) * 6
        + (narrow(4, 4, 4, 24, W),) * 3
        + (wide(4, 4, 4, 8, 128),),
        in_specs=[pl.BlockSpec(memory_space=pl.ANY)] * 19 + [held] * 3,
        out_specs=(held,) * 6 + (pl.BlockSpec(memory_space=pl.ANY),) * 10,
        scratch_shapes=scratch,
        compiler_params=pltpu.CompilerParams(
            collective_id=1, has_side_effects=True, vmem_limit_bytes=REDUCE_VMEM
        ),
        name="reduce_gradients",
    )(*mine, *theirs, ext, enc_small, dec_small, loss)[:6]


REDUCE_VMEM = 63 * 1024 * 1024


def silu_pair(values):
    gate = lax.logistic(values)
    return (values * gate).astype(LOW_TYPE), gate * (1.0 + values * (1.0 - gate))


def plain_rows(values):
    centered = values - jnp.mean(values, axis=-1, keepdims=True)
    inverse = lax.rsqrt(jnp.mean(centered * centered, axis=-1, keepdims=True) + LN_EPS)
    return centered * inverse, inverse


def plain_pull(upstream, scaled, inverse):
    return inverse * (
        upstream
        - jnp.mean(upstream, axis=-1, keepdims=True)
        - scaled * jnp.mean(upstream * scaled, axis=-1, keepdims=True)
    )


def slot_share(tables):
    lane = lax.broadcasted_iota(jnp.int32, (1, W), 1)
    one_each = ((lane & 31) == 0) & (lane < W // 2)
    counts = [0.0, 0.0]
    for slot in range(2):
        masked = jnp.where(
            one_each, 32.0 * tables[64 + slot : 65 + slot] + tables[66 + slot : 67 + slot], 0.0
        )
        bucket = tables[68 + slot : 69 + slot]
        counts[0] += jnp.sum(masked * (1.0 - bucket), axis=1, keepdims=True)
        counts[1] += jnp.sum(masked * bucket, axis=1, keepdims=True)
    own = lane == lax.axis_index("dp") * 32
    first = lax.axis_index("mp") < 2
    bucket = jnp.sum(
        jnp.where(own, jnp.where(first, tables[68:69], tables[69:70]), 0.0), axis=1, keepdims=True
    )
    return jnp.where(bucket == 1.0, BUCKET_SHARE[1] / counts[1], BUCKET_SHARE[0] / counts[0])


def head_kernel(
    condition_ref, noisy_ref, features_ref, noise_ref, valid_ref, entry_ref, square_ref,
    modulate_ref, extra_ref,
    cond_grad_ref, time_grad_ref, one_grad_ref, two_grad_ref, mod_grad_ref,
    time_act_ref, mod_in_ref, hidden_act_ref, cond_act_ref, decoded_grad_ref, extra_grad_ref,
    loss_ref,
    modulation, tables, extra_rows, pulled,
):
    tables[...] = extra_ref[...].astype(WIDE_TYPE).T
    table_in = tables[0:C].astype(LOW_TYPE)
    table_out = tables[C : 2 * C].astype(LOW_TYPE)

    def bias(index):
        return tables[2 * C + index : 2 * C + index + 1]

    condition = condition_ref[...]
    time_pre = outer_rows(features_ref[...], entry_ref[:, D:]) + bias(1)
    time_act, time_slope = silu_pair(time_pre)
    time_act_ref[...] = time_act
    cond_pre = outer_rows(condition, entry_ref[:, :D]) + bias(0)
    cond_pre = cond_pre + (outer_rows(time_act, square_ref[0]) + bias(2))
    cond_act, cond_slope = silu_pair(cond_pre)
    cond_act_ref[...] = cond_act

    def modulate(part, carry):
        rows = modulate_ref[pl.ds(pl.multiple_of(W * part, W), W)]
        offset = tables[pl.ds(2 * C + 6 + part, 1)]
        modulation[part] = outer_rows(cond_act_ref[...], rows) + offset
        return carry

    lax.fori_loop(0, 5, modulate, 0)
    entry_x = matmul_low(noisy_ref[...], table_in) + bias(3)
    scaled_in, inverse_in = plain_rows(entry_x)
    mod_in = (scaled_in * (1.0 + modulation[1]) + modulation[0]).astype(LOW_TYPE)
    mod_in_ref[...] = mod_in
    hidden_one = outer_rows(mod_in, square_ref[1]) + bias(4)
    hidden_act, hidden_slope = silu_pair(hidden_one)
    hidden_act_ref[...] = hidden_act
    hidden_two = outer_rows(hidden_act, square_ref[2]) + bias(5)
    leaving = entry_x + modulation[2] * hidden_two
    scaled_out, inverse_out = plain_rows(leaving)
    mod_out = (scaled_out * (1.0 + modulation[4]) + modulation[3]).astype(LOW_TYPE)
    error = outer_rows(mod_out, table_out) - noise_ref[...]
    weight = valid_ref[...] * slot_share(tables)
    row_loss = jnp.mean(error * error, axis=1, keepdims=True)
    loss_ref[...] = jnp.full((8, 128), jnp.sum(weight * row_loss))
    pred_grad = (weight * (2.0 / C) * error).astype(LOW_TYPE)
    extra_rows[...] = jnp.zeros_like(extra_rows)
    extra_rows[C : 2 * C] = inner_rows(pred_grad, mod_out)
    mod_out_grad = matmul_low(pred_grad, table_out)
    leaving_grad = plain_pull(mod_out_grad * (1.0 + modulation[4]), scaled_out, inverse_out)

    def give_mod(part, values):
        low = values.astype(LOW_TYPE)
        mod_grad_ref[:, W * part : W * (part + 1)] = low
        row = 2 * C + 6 + part
        extra_rows[row : row + 1] = row_sum(low.astype(WIDE_TYPE))

    def bias_grad(index, low):
        row = 2 * C + index
        extra_rows[row : row + 1] = row_sum(low.astype(WIDE_TYPE))

    give_mod(3, mod_out_grad)
    give_mod(4, mod_out_grad * scaled_out)
    give_mod(2, leaving_grad * hidden_two)
    two_grad = (leaving_grad * modulation[2]).astype(LOW_TYPE)
    two_grad_ref[...] = two_grad
    bias_grad(5, two_grad)
    one_grad = (matmul_low(two_grad, square_ref[2]) * hidden_slope).astype(LOW_TYPE)
    one_grad_ref[...] = one_grad
    bias_grad(4, one_grad)
    mod_in_grad = matmul_low(one_grad, square_ref[1])
    give_mod(0, mod_in_grad)
    give_mod(1, mod_in_grad * scaled_in)
    entry_x_grad = plain_pull(mod_in_grad * (1.0 + modulation[1]), scaled_in, inverse_in)
    entry_x_grad = (entry_x_grad + leaving_grad).astype(LOW_TYPE)
    bias_grad(3, entry_x_grad)
    extra_rows[0:C] = inner_rows(noisy_ref[...], entry_x_grad)
    pulled[...] = jnp.zeros_like(pulled)

    def pull(part, carry):
        start = pl.multiple_of(W * part, W)
        pulled[...] += matmul_low(mod_grad_ref[:, pl.ds(start, W)], modulate_ref[pl.ds(start, W)])
        return carry

    lax.fori_loop(0, 5, pull, 0)
    cond_grad = (pulled[...] * cond_slope).astype(LOW_TYPE)
    cond_grad_ref[...] = cond_grad
    bias_grad(0, cond_grad)
    bias_grad(2, cond_grad)
    decoded_grad = matmul_low(cond_grad, entry_ref[:, :D]).astype(LOW_TYPE)
    decoded_grad_ref[...] = decoded_grad.astype(WIDE_TYPE)
    time_grad = (matmul_low(cond_grad, square_ref[0]) * time_slope).astype(LOW_TYPE)
    time_grad_ref[...] = time_grad
    bias_grad(1, time_grad)
    extra_grad_ref[...] = extra_rows[...].T


def head_grad_kernel(role_ref, *refs):
    mine_of, theirs_of = refs[0:5], refs[5:10]
    time_act, mod_in, hidden_act, cond_act, condition, features = [ref[...] for ref in refs[10:16]]
    mine_out, theirs_out = refs[16:19], refs[19:22]
    for grads, outs, kind in ((mine_of, mine_out, WIDE_TYPE), (theirs_of, theirs_out, LOW_TYPE)):
        cond_grad, time_grad, one_grad, two_grad, mod_grad = [ref[...] for ref in grads]

        def rows(left, right):
            product = inner_rows(left, right)
            return product.reshape(16, product.shape[0] // 16, product.shape[1])

        def put(out, pieces):
            joined = jnp.concatenate(pieces, axis=1).astype(kind)
            out[0] = joined.reshape(4, 4, 24, W)

        put(
            outs[0],
            [rows(cond_grad, time_act), rows(one_grad, mod_in), rows(two_grad, hidden_act)],
        )
        mod_rows = rows(mod_grad, cond_act)
        entry = jnp.concatenate([rows(cond_grad, condition), rows(time_grad, features)], axis=2)
        put(outs[1], [mod_rows[:, :24]])
        put(outs[2], [mod_rows[:, 24:], entry])


HEAD_PARTS = (128, 128, 128, 128, 640)


def head_step(condition, noisy, features, noise_rows, valid, tables, role_array):
    entry, squares, modulate, extras = tables
    rows = condition.shape[0]
    held = pl.BlockSpec(memory_space=pltpu.VMEM)
    outs = pl.pallas_call(
        head_kernel,
        out_shape=(
            narrow(rows, W), narrow(rows, W), narrow(rows, W), narrow(rows, W),
            narrow(rows, 5 * W),
            narrow(rows, W), narrow(rows, W), narrow(rows, W), narrow(rows, W),
            wide(rows, D), wide(W, 128), wide(8, 128),
        ),
        in_specs=[held] * 9,
        out_specs=(held,) * 12,
        scratch_shapes=[
            pltpu.VMEM((5, rows, W), WIDE_TYPE),
            pltpu.VMEM((128, W), WIDE_TYPE),
            pltpu.VMEM((128, W), WIDE_TYPE),
            pltpu.VMEM((rows, W), WIDE_TYPE),
        ],
        compiler_params=pltpu.CompilerParams(vmem_limit_bytes=VMEM_BYTES),
        cost_estimate=cost(4 * rows * W * 9 * W, 20 * W * W),
        name="head_step",
    )(condition, noisy, features, noise_rows, valid, entry, squares, modulate, extras)
    grads, inputs = outs[:5], outs[5:9]
    decoded_grad, extra_grad, loss = outs[9:]

    def half(width, other):
        def index(plane, role_ref):
            return (0, (jnp.abs(role_ref[0] - other)) * 4 + plane)

        return pl.BlockSpec((rows, width), index)

    def full(width):
        return pl.BlockSpec((rows, width), lambda plane, role_ref: (0, 0))

    out_spec = pl.BlockSpec((1, 4, 4, 24, W), lambda plane, role_ref: (plane, 0, 0, 0, 0))
    sums = pl.pallas_call(
        head_grad_kernel,
        grid_spec=pltpu.PrefetchScalarGridSpec(
            num_scalar_prefetch=1,
            grid=(4,),
            in_specs=[half(width, 0) for width in HEAD_PARTS]
            + [half(width, 1) for width in HEAD_PARTS]
            + [full(W)] * 4
            + [full(D), full(FREQ)],
            out_specs=(out_spec,) * 6,
        ),
        out_shape=(wide(4, 4, 4, 24, W),) * 3 + (narrow(4, 4, 4, 24, W),) * 3,
        compiler_params=pltpu.CompilerParams(
            dimension_semantics=("arbitrary",), vmem_limit_bytes=VMEM_BYTES
        ),
        cost_estimate=cost(2 * rows * W * 9 * W, 60 * W * W),
        name="head_gradients",
    )(role_array, *grads, *grads, *inputs, condition, features)
    pairs = list(zip(sums[:3], sums[3:]))
    return loss, pairs, extra_grad, decoded_grad


def adam_kernel(*refs):
    kept_ref, taken_ref, head_ref, ext_ref, small_ref, norm_ref = refs[:6]
    params, firsts, seconds = refs[6:15], refs[15:24], refs[24:33]
    outs = refs[33:]
    role, dp_index = lax.axis_index("role"), lax.axis_index("dp")
    factor = jnp.minimum(1.0, CLIP_NORM / (jnp.sqrt(norm_ref[0:1, 0:1]) + 1e-06))

    def update(index, grad, at=()):
        spot = at if at else (Ellipsis,)
        scaled = factor * grad
        first = BETA_ONE * firsts[index][spot] + (1.0 - BETA_ONE) * scaled
        second = BETA_TWO * seconds[index][spot] + (1.0 - BETA_TWO) * scaled * scaled
        weight = params[index][spot]
        first_hat = first * (1.0 / (1.0 - BETA_ONE**STEP))
        second_hat = second * (1.0 / (1.0 - BETA_TWO**STEP))
        outs[3 * index][spot] = first
        outs[3 * index + 1][spot] = second
        outs[3 * index + 2][spot] = weight - RATE * (
            first_hat / (jnp.sqrt(second_hat) + ADAM_EPS) + DECAY * weight
        )

    first_core = role == 0
    lower = [jnp.where(first_core, kept_ref[part], taken_ref[part]) for part in range(3)]
    upper = [jnp.where(first_core, taken_ref[part], kept_ref[part]) for part in range(3)]
    update(0, small_ref[0 : C + 2])
    for head in range(3):
        spans = [slice(HD * head, HD * (head + 1)), slice(192 + HD * head, 192 + HD * (head + 1))]
        pieces = [upper[0][:, spans[0]], lower[0][:, spans[0]], lower[0][:, spans[1]]]
        update(1, jnp.concatenate(pieces, axis=1), (head,))
    update(2, upper[0][:, 192:])
    update(3, jnp.concatenate([lower[1], upper[1]], axis=1))
    update(4, jnp.concatenate([lower[2], upper[2]], axis=1))
    rows = jnp.where(first_core, small_ref[18:24], small_ref[24:30])
    column = lax.broadcasted_iota(jnp.int32, (D, 48), 0)
    wanted = lax.broadcasted_iota(jnp.int32, (D, 48), 1) + dp_index * 48
    update(5, matmul_high(rows, (column == wanted).astype(WIDE_TYPE)))
    entry = jnp.concatenate([head_ref[2, 16:24], ext_ref[...]], axis=1)
    update(6, entry[:, :HE])
    for part in range(3):
        update(7, head_ref[0, 8 * part : 8 * part + 8], (part,))
    update(8, jnp.concatenate([head_ref[1], head_ref[2, 0:16]], axis=0))


def adam_all(sums, params, firsts, seconds):
    held = pl.BlockSpec(memory_space=pltpu.VMEM)
    return pl.pallas_call(
        adam_kernel,
        out_shape=tuple(wide(*item.shape) for item in params for _ in range(3)),
        in_specs=[held] * 33,
        out_specs=(held,) * 27,
        compiler_params=pltpu.CompilerParams(vmem_limit_bytes=VMEM_BYTES),
        name="adam",
    )(*sums, *params, *firsts, *seconds)


def per_device(
    latents,
    noise_draws,
    timesteps,
    buckets,
    visible_index,
    patch_embed,
    patch_embed_first,
    patch_embed_second,
    attention_in,
    attention_in_first,
    attention_in_second,
    attention_out,
    attention_out_first,
    attention_out_second,
    feedforward_in,
    feedforward_in_first,
    feedforward_in_second,
    feedforward_out,
    feedforward_out_first,
    feedforward_out_second,
    block_affine,
    block_affine_first,
    block_affine_second,
    head_entry,
    head_entry_first,
    head_entry_second,
    head_square,
    head_square_first,
    head_square_second,
    head_modulate,
    head_modulate_first,
    head_modulate_second,
):
    role = lax.axis_index("role")
    mp_index = lax.axis_index("mp")
    facts = jnp.concatenate(
        [
            latents.transpose(0, 2, 1),
            noise_draws.transpose(0, 2, 1),
            jnp.pad(kept_signal(timesteps), ((0, 0), (0, 5), (0, 0))),
        ],
        axis=1,
    )
    shards = (
        attention_in[0].transpose(1, 0, 2),
        attention_out[0].T,
        feedforward_in[0],
        feedforward_out[0].T,
        block_affine[0],
        head_square.transpose(0, 2, 1),
        head_entry.T,
        head_modulate.T,
    )
    blocks, squares_all, entry_all, modulate_all, extras, *rows = gather_weights(
        shards,
        (
            patch_embed, facts, buckets, visible_index[:, :, None], position_table(),
            time_tables(),
        ),
    )
    (
        embedded, embedded_own, enc_keys, enc_ids, dec_rows, dec_rows_own, dec_keys, dec_ids,
        noisy_input, features, noise_rows, valid, enc_left, enc_left_own,
    ) = rows
    blocks = blocks.reshape(2, 4, D, BLOCK_COLS)
    tables = (
        entry_all.reshape(W, SEQ),
        squares_all.reshape(3, W, W),
        modulate_all.reshape(5 * W, W),
        extras.reshape(W, 128),
    )
    role_array = jnp.reshape(role, (1,)).astype(jnp.int32)
    encoded, enc_kept = block_forward(embedded, embedded_own, enc_keys, enc_ids, blocks, 0)
    parity = mp_index % 2
    other = send(encoded, neighbour_pairs())
    pair = jnp.where(parity == 0, jnp.stack([encoded, other]), jnp.stack([other, encoded]))
    across = send(pair, partner_pairs())
    received = jnp.where(role == 0, jnp.stack([pair, across], 1), jnp.stack([across, pair], 1))
    received = received.reshape(VCAP, D).astype(WIDE_TYPE)
    dec_rows = dec_rows.at[MCAP:].add(received)
    condition, dec_kept = block_forward(dec_rows, dec_rows_own, dec_keys, dec_ids, blocks, 1)
    loss_local, head_grads, extra_grad, decoded_grad = head_step(
        condition, noisy_input, features, noise_rows, valid, tables, role_array
    )
    extra_grad = extra_grad.reshape(2, 4, 4, 4, 8, 128)
    is_mask = jnp.arange(24)[None, :] == C + 1
    dec_left = (is_mask & (jnp.arange(MCAP + VCAP)[:, None] < MCAP)).astype(WIDE_TYPE)
    dec_left_own = jnp.broadcast_to(is_mask, (MQP, 24)).astype(WIDE_TYPE)
    visible_grad, dec_grads, dec_small = block_backward(
        decoded_grad, dec_kept, blocks, 1, role_array, dec_left, dec_left_own
    )
    visible_grad = visible_grad.reshape(2, 2, VQ, D)
    summed = pick(visible_grad, role, 1) + send(pick(visible_grad, 1 - role, 1), partner_pairs())
    came = send(pick(summed, 1 - parity, 0).astype(LOW_TYPE), neighbour_pairs())
    returned = pick(summed, parity, 0) + came.astype(WIDE_TYPE)
    returned = returned.astype(LOW_TYPE).astype(WIDE_TYPE)
    _, enc_grads, enc_small = block_backward(
        returned, enc_kept, blocks, 0, role_array, enc_left, enc_left_own
    )
    pairs = enc_grads + dec_grads + head_grads
    *sums, square_total = reduce_gradients(
        [pair[0] for pair in pairs],
        [pair[1] for pair in pairs],
        extra_grad,
        enc_small,
        dec_small,
        loss_local,
    )
    loss_total = sums[4][30, 0]
    grad_norm = jnp.sqrt(square_total[0, 0])

    def flat(arrays):
        patch, joint, branch, up, down, affine, entry, square, modulate = arrays
        return (
            patch,
            joint[0].transpose(1, 0, 2),
            branch[0].T,
            up[0],
            down[0].T,
            affine[0],
            entry.T,
            square.transpose(0, 2, 1),
            modulate.T,
        )

    def restored(arrays):
        patch, joint, branch, up, down, affine, entry, square, modulate = arrays
        return (
            patch,
            joint.transpose(1, 0, 2)[None],
            branch.T[None],
            up[None],
            down.T[None],
            affine[None],
            entry.T,
            square.transpose(0, 2, 1),
            modulate.T,
        )

    params = (
        patch_embed,
        attention_in,
        attention_out,
        feedforward_in,
        feedforward_out,
        block_affine,
        head_entry,
        head_square,
        head_modulate,
    )
    firsts = (
        patch_embed_first,
        attention_in_first,
        attention_out_first,
        feedforward_in_first,
        feedforward_out_first,
        block_affine_first,
        head_entry_first,
        head_square_first,
        head_modulate_first,
    )
    seconds = (
        patch_embed_second,
        attention_in_second,
        attention_out_second,
        feedforward_in_second,
        feedforward_out_second,
        block_affine_second,
        head_entry_second,
        head_square_second,
        head_modulate_second,
    )
    updated = adam_all((*sums, square_total), flat(params), flat(firsts), flat(seconds))
    updated = [restored(updated[part::3]) for part in range(3)]
    news = [updated[part][index] for index in range(9) for part in range(3)]
    return (
        loss_total,
        grad_norm,
        news[0],
        news[1],
        news[2],
        news[3],
        news[4],
        news[5],
        news[6],
        news[7],
        news[8],
        news[9],
        news[10],
        news[11],
        news[12],
        news[13],
        news[14],
        news[15],
        news[16],
        news[17],
        news[18],
        news[19],
        news[20],
        news[21],
        news[22],
        news[23],
        news[24],
        news[25],
        news[26],
    )


def solution(mesh):
    placed = (
        P(None, "dp", None),
        P(None, "dp", None),
        P(None, "dp"),
        P(None, "dp"),
        P(None, "dp"),
        P(),
        P(),
        P(),
        P("role", "dp", "mp", None),
        P("role", "dp", "mp", None),
        P("role", "dp", "mp", None),
        P("role", "mp", "dp"),
        P("role", "mp", "dp"),
        P("role", "mp", "dp"),
        P("role", "dp", "mp"),
        P("role", "dp", "mp"),
        P("role", "dp", "mp"),
        P("role", "mp", "dp"),
        P("role", "mp", "dp"),
        P("role", "mp", "dp"),
        P("role", None, "dp"),
        P("role", None, "dp"),
        P("role", None, "dp"),
        P(None, ("role", "dp", "mp")),
        P(None, ("role", "dp", "mp")),
        P(None, ("role", "dp", "mp")),
        P(None, None, ("role", "dp", "mp")),
        P(None, None, ("role", "dp", "mp")),
        P(None, None, ("role", "dp", "mp")),
        P(None, ("role", "dp", "mp")),
        P(None, ("role", "dp", "mp")),
        P(None, ("role", "dp", "mp")),
    )
    return jax.shard_map(
        per_device,
        mesh=mesh,
        in_specs=placed,
        out_specs=(
            P(),
            P(),
            P(),
            P(),
            P(),
            P("role", "dp", "mp", None),
            P("role", "dp", "mp", None),
            P("role", "dp", "mp", None),
            P("role", "mp", "dp"),
            P("role", "mp", "dp"),
            P("role", "mp", "dp"),
            P("role", "dp", "mp"),
            P("role", "dp", "mp"),
            P("role", "dp", "mp"),
            P("role", "mp", "dp"),
            P("role", "mp", "dp"),
            P("role", "mp", "dp"),
            P("role", None, "dp"),
            P("role", None, "dp"),
            P("role", None, "dp"),
            P(None, ("role", "dp", "mp")),
            P(None, ("role", "dp", "mp")),
            P(None, ("role", "dp", "mp")),
            P(None, None, ("role", "dp", "mp")),
            P(None, None, ("role", "dp", "mp")),
            P(None, None, ("role", "dp", "mp")),
            P(None, ("role", "dp", "mp")),
            P(None, ("role", "dp", "mp")),
            P(None, ("role", "dp", "mp")),
        ),
        check_vma=False,
    )
```

```python
import functools
import math

import jax
import jax.numpy as jnp
from jax import lax
from jax.experimental import pallas as pl
from jax.experimental.pallas import tpu as pltpu
from jax.sharding import PartitionSpec as P

D = 768
HD = 64
C = 16
FREQ = 256
GRID = 32
STEP = 5
SEQ = 1024
VCAP = 320
MCAP = 864


LN_EPS = 1e-06
BETA_ONE = 0.9
BETA_TWO = 0.95
ADAM_EPS = 1e-08
DECAY = 0.02
RATE = 0.02
CLIP_NORM = 0.02
BUCKET_SHARE = (0.6, 0.4)
COSINE_OFFSET = 0.008
HORIZON = 1000.0
LOW_TYPE = jnp.bfloat16
WIDE_TYPE = jnp.float32


def matmul_low(left_side, right_side):
    return jnp.dot(left_side, right_side, preferred_element_type=WIDE_TYPE)


def matmul_high(left_side, right_side):
    return jnp.dot(left_side, right_side, precision=lax.Precision.HIGHEST)


def inner_rows(left_side, right_side):
    return lax.dot_general(
        left_side, right_side, (((0,), (0,)), ((), ())), preferred_element_type=WIDE_TYPE
    )


def outer_rows(left_side, right_side):
    return lax.dot_general(
        left_side, right_side, (((1,), (1,)), ((), ())), preferred_element_type=WIDE_TYPE
    )


def plain_forward(values):
    centered = values - jnp.mean(values, axis=-1, keepdims=True)
    spread = jnp.mean(centered * centered, axis=-1, keepdims=True)
    inverse = lax.rsqrt(spread + LN_EPS)
    scaled = centered * inverse
    return (scaled, (scaled, inverse))


def plain_backward(upstream, saved_norm):
    scaled, inverse = saved_norm
    return inverse * (
        upstream
        - jnp.mean(upstream, axis=-1, keepdims=True)
        - scaled * jnp.mean(upstream * scaled, axis=-1, keepdims=True)
    )


def silu_slope(values):
    sigmoid = jax.nn.sigmoid(values)
    return sigmoid * (1.0 + values * (1.0 - sigmoid))


QUARTER = 4
HE = 1067
MQ = MCAP // QUARTER
VQ = VCAP // QUARTER
HEADS = 12
FF = 3072
W = 1024
ALL = ("role", "dp", "mp")
SCALE = HD ** (-0.5)


def device_order():
    return [(r, x, z, y) for r in range(2) for x in range(4) for z in range(4) for y in range(4)]


def flat_index(r, x, z, y):
    return r * 64 + x * 16 + z * 4 + y


def partner_pairs():
    return [(flat_index(r, x, z, y), flat_index(1 - r, x, z, y)) for r, x, z, y in device_order()]


def neighbour_pairs():
    return [(flat_index(r, x, z, y), flat_index(r, x, z, y ^ 1)) for r, x, z, y in device_order()]


def send(value, pairs):
    return lax.ppermute(value, ALL, pairs)


def pick(value, index, dim):
    return lax.dynamic_index_in_dim(value, index, dim, keepdims=False)


ORDERS = ((1, 2, 3), (2, 3, 1), (3, 1, 2))


def block_position(places, wide_image, table):
    local = jnp.where(wide_image, places, places & 255)
    shift = jnp.where(wide_image, 5, 4)
    rows = lax.shift_right_logical(local, jnp.broadcast_to(shift, local.shape))
    cols = local & jnp.where(wide_image, 31, 15)
    grid = lax.broadcasted_iota(jnp.int32, (places.shape[0], GRID), 1)
    pair = [(side == grid).astype(WIDE_TYPE) for side in (rows, cols)]
    return jnp.concatenate([matmul_high(side, table) for side in pair], axis=1)


def as_row(column):
    return jnp.broadcast_to(column, (column.shape[0], 128)).T[0:1]


def pack_shards(ins, packed):
    joint, branch, up, down, affine, square, entry, modulate = ins
    block, squares, entry_out, modulate_out, extra = packed
    heads = [joint[head] for head in range(3)]

    def kind(index):
        return [head[:, HD * index : HD * (index + 1)] for head in heads]

    block[:, :768] = jnp.concatenate(kind(1) + kind(2) + kind(0) + [branch[...]], axis=1).astype(
        LOW_TYPE
    )
    block[:, 768:1536] = up[...].astype(LOW_TYPE)
    block[:, 1536:2304] = down[...].astype(LOW_TYPE)
    affine_rows = jnp.concatenate([affine[...], jnp.zeros((122, 48), WIDE_TYPE)], axis=0)
    block[:, 2304:] = affine_rows.T.astype(LOW_TYPE)
    squares[...] = square[...].astype(LOW_TYPE)
    entry_out[...] = entry[:, :SEQ].astype(LOW_TYPE)
    modulate_out[...] = modulate[...].astype(LOW_TYPE)
    tail = jnp.concatenate([entry[:, SEQ:], jnp.zeros((8, 85), WIDE_TYPE)], axis=1)
    return tail


def count_codes(buckets, visible):
    lane = lax.broadcasted_iota(jnp.int32, (1, 128), 1)
    row = jnp.zeros((1, 128), WIDE_TYPE)
    for slot in range(2):
        hidden = (visible[slot : slot + 1] >= SEQ).astype(WIDE_TYPE)
        masked = SEQ - VCAP + jnp.sum(hidden, axis=1, keepdims=True)
        high = jnp.floor(masked * (1.0 / 32.0))
        bucket = buckets[0:1, slot : slot + 1].astype(WIDE_TYPE)
        for index, value in enumerate((high, masked - 32.0 * high, bucket)):
            row = row + jnp.where(lane == 64 + 2 * index + slot, value, 0.0)
    return row


def prepare_rows(ins, outs, column_ref):
    patch, latents, noise, signal, buckets, visible, table, trig = ins
    (
        embedded_out, embedded_own_out, enc_keys_out, enc_ids_out, rows_out, rows_own_out,
        dec_keys_out, dec_ids_out, noisy_out, features_out, noise_out, valid_out, left_out,
        left_own_out, enc_inverse_out, dec_inverse_out,
    ) = outs
    role, mp_index = lax.axis_index("role"), lax.axis_index("mp")
    slot = lax.div(mp_index, 2)
    quarter = lax.rem(mp_index, 2) * 2 + role
    first = slot == 0
    wide_image = jnp.where(first, buckets[0:1, 0:1], buckets[0:1, 1:2]) == 1
    table = table[...]
    spare = jnp.zeros((5, SEQ), WIDE_TYPE)
    slot_facts = jnp.concatenate([latents[slot], noise[slot], signal[slot], spare], axis=0)
    shown_row = jnp.where(first, visible[0:1], visible[1:2]).astype(WIDE_TYPE)
    column_ref[...] = jnp.broadcast_to(shown_row, (128, VCAP)).T
    shown_col = column_ref[:, 0:1].astype(jnp.int32)
    lanes = lax.broadcasted_iota(jnp.int32, (1, SEQ), 1)

    def ids_of(places):
        return jnp.where(wide_image, 0, lax.shift_right_logical(places, jnp.full_like(places, 8)))

    def encoder_rows(column):
        places = jnp.minimum(column, SEQ - 1)
        chosen = (places == lanes).astype(WIDE_TYPE)
        picked = lax.dot_general(
            chosen, slot_facts, (((1,), (1,)), ((), ())), precision=lax.Precision.HIGHEST
        )
        place = block_position(places, wide_image, table)
        rows = matmul_high(picked[:, :C], patch[0:C]) + patch[C : C + 1] + place
        ones = jnp.ones((column.shape[0], 1), WIDE_TYPE)
        zeros = jnp.zeros((column.shape[0], 7), WIDE_TYPE)
        return rows, place, ids_of(places), jnp.concatenate([picked[:, :C], ones, zeros], axis=1)

    rows, place, ids, left = encoder_rows(shown_col)
    embedded_out[...], enc_inverse_out[...] = plain_rows(rows)
    left_out[...] = left
    visible_keys = jnp.where(shown_col < SEQ, ids, -1).astype(WIDE_TYPE)
    enc_keys_out[...] = visible_keys
    own_col = column_ref[pl.ds(pl.multiple_of(quarter * VQ, 8), VQ), 0:1].astype(jnp.int32)
    rows, _, ids, left = encoder_rows(own_col)
    embedded_own_out[...] = rows
    left_own_out[...] = left
    enc_ids_out[...] = as_row(ids.astype(WIDE_TYPE))

    shown = jnp.max((shown_col == lanes).astype(WIDE_TYPE), axis=0, keepdims=True)
    masked = 1.0 - shown
    low = lax.broadcasted_iota(jnp.int32, (SEQ, SEQ), 0)
    high = lax.broadcasted_iota(jnp.int32, (SEQ, SEQ), 1)
    before = (low <= high).astype(LOW_TYPE)
    rank = matmul_low(jnp.broadcast_to(masked, (16, SEQ)).astype(LOW_TYPE), before)[0:1] - 1.0
    rank = jnp.where(masked > 0.0, rank, -1.0)
    total = jnp.sum(masked, axis=1, keepdims=True)

    def masked_rows(index):
        valid = index < total
        wanted = jnp.where(valid, index, -2.0)
        hit = jnp.where(valid, (rank == wanted).astype(WIDE_TYPE), (lanes == SEQ - 1).astype(WIDE_TYPE))
        places = jnp.sum(hit * lanes.astype(WIDE_TYPE), axis=1, keepdims=True).astype(jnp.int32)
        return hit, valid, places, patch[C + 1 : C + 2] + block_position(places, wide_image, table)

    index = lax.broadcasted_iota(jnp.int32, (MCAP, 1), 0).astype(WIDE_TYPE)
    _, valid, places, rows = masked_rows(index)
    rows_out[0:MCAP], dec_inverse_out[...] = plain_rows(rows)
    rows_out[MCAP:] = place
    dec_keys_out[0:MCAP] = jnp.where(valid, ids_of(places), -1).astype(WIDE_TYPE)
    dec_keys_out[MCAP:] = visible_keys
    inner = lax.broadcasted_iota(jnp.int32, (MQP, 1), 0)
    index = jnp.where(inner < MQ, inner + quarter * MQ, MCAP).astype(WIDE_TYPE)
    hit, valid, places, rows = masked_rows(index)
    rows_own_out[...] = rows
    ids = jnp.where(inner < MQ, ids_of(places), -2).astype(WIDE_TYPE)
    dec_ids_out[...] = as_row(ids)
    valid_out[...] = valid.astype(WIDE_TYPE)
    picked = lax.dot_general(
        hit, slot_facts, (((1,), (1,)), ((), ())), precision=lax.Precision.HIGHEST
    )
    noise_rows = picked[:, C : 2 * C]
    noise_out[...] = noise_rows
    noisy_out[...] = (picked[:, 33:34] * picked[:, :C] + picked[:, 34:35] * noise_rows).astype(
        LOW_TYPE
    )
    time = picked[:, 32:33].astype(jnp.int32)
    grid = lax.broadcasted_iota(jnp.int32, (MQP, GRID), 1)
    coarse = (lax.shift_right_logical(time, jnp.full_like(time, 5)) == grid).astype(WIDE_TYPE)
    fine = ((time & 31) == grid).astype(WIDE_TYPE)
    coarse = matmul_high(coarse, trig[:, :256])
    fine = matmul_high(fine, trig[:, 256:])
    cos_a, sin_a, cos_b, sin_b = coarse[:, :128], coarse[:, 128:], fine[:, :128], fine[:, 128:]
    features_out[:, :128] = (cos_a * cos_b - sin_a * sin_b).astype(LOW_TYPE)
    features_out[:, 128:] = (sin_a * cos_b + cos_a * sin_b).astype(LOW_TYPE)


BLOCK_COLS = 2432
PIECES = (
    ((0, 0, 0, BLOCK_COLS, 1280), (3, None, 0, 640, 384)),
    ((0, 16, 0, BLOCK_COLS, 1280), (3, None, 640, 384, 256), (2, None, 0, 1024, 512), (4, None, 0, 128, 128)),
    ((0, 32, 0, BLOCK_COLS, 1280), (1, None, 0, 1024, 512)),
)
GATHER_COPIES = 8 + 3 * 8 * 8


def mesh_place():
    dp_index = lax.axis_index("dp")
    role, mp_index = lax.axis_index("role"), lax.axis_index("mp")
    return (role, dp_index // 4, lax.rem(dp_index, 4), mp_index)


def mesh_device(place):
    return (place[0], place[1] * 4 + place[2], place[3])


def moved(place, axis, steps):
    target = list(place)
    count = 2 if axis == 0 else 4
    target[axis] = lax.rem(target[axis] + steps + count, count)
    return tuple(target)


def greet(place, moves):
    barrier = pltpu.get_barrier_semaphore()
    for axis, steps in moves:
        pl.semaphore_signal(
            barrier,
            inc=1,
            device_id=mesh_device(moved(place, axis, steps)),
            device_id_type=pl.DeviceIdType.MESH,
        )
    pl.semaphore_wait(barrier, len(moves))


RING_MOVES = ((0, 1), (1, 1), (1, -1), (2, 1), (2, -1), (3, 1), (3, -1))


def gather_kernel(*refs):
    shard_ins, row_ins, outs, row_outs = refs[:8], refs[8:16], refs[16:21], refs[21:37]
    packed, column_ref, (send_sems, recv_sems, local_sems) = refs[37:42], refs[42], refs[43:]
    ins = packed
    extra_row = count_codes(row_ins[4], row_ins[5])
    first_row = lax.broadcasted_iota(jnp.int32, (8, 128), 0) == 0
    tail = pack_shards(shard_ins, packed)
    packed[4][...] = (tail + jnp.where(first_row, extra_row, 0.0)).astype(LOW_TYPE)
    place = mesh_place()
    used = [0]

    def region(piece, spans, half):
        kind, row, column, width, cut = piece
        if half is not None:
            column, width = (column, cut) if half == 0 else (column + cut, width - cut)
        r = spans[0]
        x, z, y = (slice(None) if spans[axis] is None else spans[axis] for axis in (1, 2, 3))
        columns = pl.ds(column, width)
        if kind == 0:
            return outs[0].at[r, y, x, z, pl.ds(row, 16), columns]
        if kind == 1:
            return outs[1].at[:, r, x, z, y, :, columns]
        return outs[kind].at[r, x, z, y, :, columns]

    def start(unit, spans, half, axis, steps):
        copies = []
        for piece in PIECES[unit[0]]:
            if (piece[0] > 0) != unit[1] or (half == 1 and piece[3] == piece[4]):
                continue
            ref = region(piece, spans, half)
            slot = used[0]
            used[0] += 1
            copy = pltpu.make_async_remote_copy(
                src_ref=ref,
                dst_ref=ref,
                send_sem=send_sems.at[slot],
                recv_sem=recv_sems.at[slot],
                device_id=mesh_device(moved(place, axis, steps)),
                device_id_type=pl.DeviceIdType.MESH,
            )
            copy.start()
            copies.append(copy)
        return copies

    r, x, z, y = place
    own = {0: r, 1: x, 2: z, 3: y}
    targets = (
        outs[0].at[r, y, x, z], outs[1].at[:, r, x, z, y], outs[2].at[r, x, z, y],
        outs[3].at[r, x, z, y], outs[4].at[r, x, z, y],
    )
    placed = [
        pltpu.make_async_copy(source, target, local_sems.at[index])
        for index, (source, target) in enumerate(zip(ins, targets))
    ]
    for copy in placed:
        copy.start()
    greet(place, RING_MOVES)
    for copy in placed:
        copy.wait()
    pending, leaving = [], []
    units = [(third, stream) for stream in (0, 1) for third in range(3)]
    spans = {unit: dict(own) for unit in units}
    first, second = {}, {}

    def step_one(unit, stage):
        axis = ORDERS[unit[0]][stage]
        first[unit] = [start(unit, spans[unit], None, axis, steps) for steps in (1, -1)]

    for unit in units:
        step_one(unit, 0)
    for unit in units:
        pending += start(unit, spans[unit], None, 0, 1)
    for stage in range(3):
        if stage == 2:
            prepare_rows(row_ins, row_outs, column_ref)
        for unit in units:
            axis = ORDERS[unit[0]][stage]
            batch = []
            for which, steps in ((0, 1), (1, -1)):
                came = dict(spans[unit])
                came[axis] = lax.rem(own[axis] - steps + 4, 4)
                for copy in first[unit][which]:
                    copy.wait_recv()
                batch.append(start(unit, came, which, axis, steps))
                pending += start(unit, came, None, 0, 1)
            second[unit] = batch
        for unit in units:
            axis = ORDERS[unit[0]][stage]
            came = dict(spans[unit])
            came[axis] = lax.rem(own[axis] + 2, 4)
            for which in (0, 1):
                for copy in second[unit][which]:
                    copy.wait_recv()
                pending += start(unit, came, which, 0, 1)
            for copies in first[unit] + second[unit]:
                leaving += copies
            spans[unit][axis] = None
            if stage < 2:
                step_one(unit, stage + 1)
    for copy in leaving:
        copy.wait_send()
    for copy in pending:
        copy.wait()


def gather_weights(shards, rows):
    whole_torus = (2, 4, 4, 4)
    held = pl.BlockSpec(memory_space=pltpu.VMEM)
    return pl.pallas_call(
        gather_kernel,
        out_shape=(
            narrow(*whole_torus, 48, BLOCK_COLS),
            narrow(3, *whole_torus, 8, W),
            narrow(*whole_torus, 8, W),
            narrow(*whole_torus, 40, W),
            narrow(*whole_torus, 8, 128),
            wide(VCAP, D), wide(VQ, D), wide(VCAP, 1), wide(1, VQ),
            wide(MCAP + VCAP, D), wide(MQP, D), wide(MCAP + VCAP, 1), wide(1, MQP),
            narrow(MQP, C), narrow(MQP, FREQ), wide(MQP, C), wide(MQP, 1),
            wide(VCAP, 24), wide(VQ, 24), wide(VCAP, 1), wide(MCAP, 1),
        ),
        in_specs=[held] * 16,
        out_specs=(pl.BlockSpec(memory_space=pl.ANY),) * 5 + (held,) * 16,
        scratch_shapes=[
            pltpu.VMEM((48, BLOCK_COLS), LOW_TYPE),
            pltpu.VMEM((3, 8, W), LOW_TYPE),
            pltpu.VMEM((8, W), LOW_TYPE),
            pltpu.VMEM((40, W), LOW_TYPE),
            pltpu.VMEM((8, 128), LOW_TYPE),
            pltpu.VMEM((VCAP, 128), WIDE_TYPE),
            pltpu.SemaphoreType.DMA((GATHER_COPIES,)),
            pltpu.SemaphoreType.DMA((GATHER_COPIES,)),
            pltpu.SemaphoreType.DMA((5,)),
        ],
        compiler_params=pltpu.CompilerParams(
            collective_id=0, has_side_effects=True, vmem_limit_bytes=VMEM_BYTES
        ),
        name="gather_weights",
    )(*shards, *rows)


SUM_MOVES = ((0, 1),) + tuple((axis, steps) for axis in (1, 2, 3) for steps in (1, 2, 3))


def position_table():
    frequency = 1.0 / 10000.0 ** (jnp.arange(D // 4, dtype=WIDE_TYPE) / (D // 4))
    angle = jnp.arange(GRID, dtype=WIDE_TYPE)[:, None] * frequency[None, :]
    return jnp.concatenate([jnp.sin(angle), jnp.cos(angle)], axis=1)


def time_tables():
    half_width = FREQ // 2
    frequency = jnp.exp(-math.log(10000.0) * jnp.arange(half_width, dtype=WIDE_TYPE) / half_width)
    fine = jnp.arange(32, dtype=WIDE_TYPE)[:, None] * frequency[None, :]
    angles = (32.0 * fine, fine)
    return jnp.concatenate([part(angle) for angle in angles for part in (jnp.cos, jnp.sin)], axis=1)


def kept_signal(timesteps):
    times_f = (timesteps + 1).astype(WIDE_TYPE)
    half_turn = math.pi / 2
    angle_now = (times_f / HORIZON + COSINE_OFFSET) / (1.0 + COSINE_OFFSET) * half_turn
    start_cos = math.cos(COSINE_OFFSET / (1.0 + COSINE_OFFSET) * half_turn)
    signal_kept = (jnp.cos(angle_now) / start_cos) ** 2
    return jnp.stack([times_f, jnp.sqrt(signal_kept), jnp.sqrt(1.0 - signal_kept)], axis=1)


def block_position(places, wide_image, table):
    local = jnp.where(wide_image, places, places & 255)
    shift = jnp.where(wide_image, 5, 4)
    rows = lax.shift_right_logical(local, jnp.broadcast_to(shift, local.shape))
    cols = local & jnp.where(wide_image, 31, 15)
    grid = lax.broadcasted_iota(jnp.int32, (places.shape[0], GRID), 1)
    pair = [(side == grid).astype(WIDE_TYPE) for side in (rows, cols)]
    return jnp.concatenate([matmul_high(side, table) for side in pair], axis=1)


def as_row(column):
    return jnp.broadcast_to(column, (column.shape[0], 128)).T[0:1]


def pack_shards(ins, packed):
    joint, branch, up, down, affine, square, entry, modulate = ins
    block, squares, entry_out, modulate_out, extra = packed
    heads = [joint[head] for head in range(3)]

    def kind(index):
        return [head[:, HD * index : HD * (index + 1)] for head in heads]

    block[:, :768] = jnp.concatenate(kind(1) + kind(2) + kind(0) + [branch[...]], axis=1).astype(
        LOW_TYPE
    )
    block[:, 768:1536] = up[...].astype(LOW_TYPE)
    block[:, 1536:2304] = down[...].astype(LOW_TYPE)
    affine_rows = jnp.concatenate([affine[...], jnp.zeros((122, 48), WIDE_TYPE)], axis=0)
    block[:, 2304:] = affine_rows.T.astype(LOW_TYPE)
    squares[...] = square[...].astype(LOW_TYPE)
    entry_out[...] = entry[:, :SEQ].astype(LOW_TYPE)
    modulate_out[...] = modulate[...].astype(LOW_TYPE)
    tail = jnp.concatenate([entry[:, SEQ:], jnp.zeros((8, 85), WIDE_TYPE)], axis=1)
    return tail


def count_codes(buckets, visible):
    lane = lax.broadcasted_iota(jnp.int32, (1, 128), 1)
    row = jnp.zeros((1, 128), WIDE_TYPE)
    for slot in range(2):
        hidden = (visible[slot : slot + 1] >= SEQ).astype(WIDE_TYPE)
        masked = SEQ - VCAP + jnp.sum(hidden, axis=1, keepdims=True)
        high = jnp.floor(masked * (1.0 / 32.0))
        bucket = buckets[0:1, slot : slot + 1].astype(WIDE_TYPE)
        for index, value in enumerate((high, masked - 32.0 * high, bucket)):
            row = row + jnp.where(lane == 64 + 2 * index + slot, value, 0.0)
    return row


def prepare_rows(ins, outs, column_ref):
    patch, latents, noise, signal, buckets, visible, table, trig = ins
    (
        embedded_out, embedded_own_out, enc_keys_out, enc_ids_out, rows_out, rows_own_out,
        dec_keys_out, dec_ids_out, noisy_out, features_out, noise_out, valid_out, left_out,
        left_own_out, enc_inverse_out, dec_inverse_out,
    ) = outs
    role, mp_index = lax.axis_index("role"), lax.axis_index("mp")
    slot = lax.div(mp_index, 2)
    quarter = lax.rem(mp_index, 2) * 2 + role
    first = slot == 0
    wide_image = jnp.where(first, buckets[0:1, 0:1], buckets[0:1, 1:2]) == 1
    table = table[...]
    spare = jnp.zeros((5, SEQ), WIDE_TYPE)
    slot_facts = jnp.concatenate([latents[slot], noise[slot], signal[slot], spare], axis=0)
    shown_row = jnp.where(first, visible[0:1], visible[1:2]).astype(WIDE_TYPE)
    column_ref[...] = jnp.broadcast_to(shown_row, (128, VCAP)).T
    shown_col = column_ref[:, 0:1].astype(jnp.int32)
    lanes = lax.broadcasted_iota(jnp.int32, (1, SEQ), 1)

    def ids_of(places):
        return jnp.where(wide_image, 0, lax.shift_right_logical(places, jnp.full_like(places, 8)))

    def encoder_rows(column):
        places = jnp.minimum(column, SEQ - 1)
        chosen = (places == lanes).astype(WIDE_TYPE)
        picked = lax.dot_general(
            chosen, slot_facts, (((1,), (1,)), ((), ())), precision=lax.Precision.HIGHEST
        )
        place = block_position(places, wide_image, table)
        rows = matmul_high(picked[:, :C], patch[0:C]) + patch[C : C + 1] + place
        ones = jnp.ones((column.shape[0], 1), WIDE_TYPE)
        zeros = jnp.zeros((column.shape[0], 7), WIDE_TYPE)
        return rows, place, ids_of(places), jnp.concatenate([picked[:, :C], ones, zeros], axis=1)

    rows, place, ids, left = encoder_rows(shown_col)
    embedded_out[...], enc_inverse_out[...] = plain_rows(rows)
    left_out[...] = left
    visible_keys = jnp.where(shown_col < SEQ, ids, -1).astype(WIDE_TYPE)
    enc_keys_out[...] = visible_keys
    own_col = column_ref[pl.ds(pl.multiple_of(quarter * VQ, 8), VQ), 0:1].astype(jnp.int32)
    rows, _, ids, left = encoder_rows(own_col)
    embedded_own_out[...] = rows
    left_own_out[...] = left
    enc_ids_out[...] = as_row(ids.astype(WIDE_TYPE))

    shown = jnp.max((shown_col == lanes).astype(WIDE_TYPE), axis=0, keepdims=True)
    masked = 1.0 - shown
    low = lax.broadcasted_iota(jnp.int32, (SEQ, SEQ), 0)
    high = lax.broadcasted_iota(jnp.int32, (SEQ, SEQ), 1)
    before = (low <= high).astype(LOW_TYPE)
    rank = matmul_low(jnp.broadcast_to(masked, (16, SEQ)).astype(LOW_TYPE), before)[0:1] - 1.0
    rank = jnp.where(masked > 0.0, rank, -1.0)
    total = jnp.sum(masked, axis=1, keepdims=True)

    def masked_rows(index):
        valid = index < total
        wanted = jnp.where(valid, index, -2.0)
        hit = jnp.where(valid, (rank == wanted).astype(WIDE_TYPE), (lanes == SEQ - 1).astype(WIDE_TYPE))
        places = jnp.sum(hit * lanes.astype(WIDE_TYPE), axis=1, keepdims=True).astype(jnp.int32)
        return hit, valid, places, patch[C + 1 : C + 2] + block_position(places, wide_image, table)

    index = lax.broadcasted_iota(jnp.int32, (MCAP, 1), 0).astype(WIDE_TYPE)
    _, valid, places, rows = masked_rows(index)
    rows_out[0:MCAP], dec_inverse_out[...] = plain_rows(rows)
    rows_out[MCAP:] = place
    dec_keys_out[0:MCAP] = jnp.where(valid, ids_of(places), -1).astype(WIDE_TYPE)
    dec_keys_out[MCAP:] = visible_keys
    inner = lax.broadcasted_iota(jnp.int32, (MQP, 1), 0)
    index = jnp.where(inner < MQ, inner + quarter * MQ, MCAP).astype(WIDE_TYPE)
    hit, valid, places, rows = masked_rows(index)
    rows_own_out[...] = rows
    ids = jnp.where(inner < MQ, ids_of(places), -2).astype(WIDE_TYPE)
    dec_ids_out[...] = as_row(ids)
    valid_out[...] = valid.astype(WIDE_TYPE)
    picked = lax.dot_general(
        hit, slot_facts, (((1,), (1,)), ((), ())), precision=lax.Precision.HIGHEST
    )
    noise_rows = picked[:, C : 2 * C]
    noise_out[...] = noise_rows
    noisy_out[...] = (picked[:, 33:34] * picked[:, :C] + picked[:, 34:35] * noise_rows).astype(
        LOW_TYPE
    )
    time = picked[:, 32:33].astype(jnp.int32)
    grid = lax.broadcasted_iota(jnp.int32, (MQP, GRID), 1)
    coarse = (lax.shift_right_logical(time, jnp.full_like(time, 5)) == grid).astype(WIDE_TYPE)
    fine = ((time & 31) == grid).astype(WIDE_TYPE)
    coarse = matmul_high(coarse, trig[:, :256])
    fine = matmul_high(fine, trig[:, 256:])
    cos_a, sin_a, cos_b, sin_b = coarse[:, :128], coarse[:, 128:], fine[:, :128], fine[:, 128:]
    features_out[:, :128] = (cos_a * cos_b - sin_a * sin_b).astype(LOW_TYPE)
    features_out[:, 128:] = (sin_a * cos_b + cos_a * sin_b).astype(LOW_TYPE)


BLOCK_COLS = 2432
PIECES = (
    ((0, 0, 0, BLOCK_COLS, 1280), (3, None, 0, 640, 384)),
    ((0, 16, 0, BLOCK_COLS, 1280), (3, None, 640, 384, 256), (2, None, 0, 1024, 512), (4, None, 0, 128, 128)),
    ((0, 32, 0, BLOCK_COLS, 1280), (1, None, 0, 1024, 512)),
)
GATHER_COPIES = 8 + 3 * 8 * 8


def mesh_place():
    dp_index = lax.axis_index("dp")
    role, mp_index = lax.axis_index("role"), lax.axis_index("mp")
    return (role, dp_index // 4, lax.rem(dp_index, 4), mp_index)


def mesh_device(place):
    return (place[0], place[1] * 4 + place[2], place[3])


def moved(place, axis, steps):
    target = list(place)
    count = 2 if axis == 0 else 4
    target[axis] = lax.rem(target[axis] + steps + count, count)
    return tuple(target)


def greet(place, moves):
    barrier = pltpu.get_barrier_semaphore()
    for axis, steps in moves:
        pl.semaphore_signal(
            barrier,
            inc=1,
            device_id=mesh_device(moved(place, axis, steps)),
            device_id_type=pl.DeviceIdType.MESH,
        )
    pl.semaphore_wait(barrier, len(moves))


RING_MOVES = ((0, 1), (1, 1), (1, -1), (2, 1), (2, -1), (3, 1), (3, -1))


def gather_kernel(*refs):
    shard_ins, row_ins, outs, row_outs = refs[:8], refs[8:16], refs[16:21], refs[21:37]
    packed, column_ref, (send_sems, recv_sems, local_sems) = refs[37:42], refs[42], refs[43:]
    ins = packed
    extra_row = count_codes(row_ins[4], row_ins[5])
    first_row = lax.broadcasted_iota(jnp.int32, (8, 128), 0) == 0
    tail = pack_shards(shard_ins, packed)
    packed[4][...] = (tail + jnp.where(first_row, extra_row, 0.0)).astype(LOW_TYPE)
    place = mesh_place()
    used = [0]

    def region(piece, spans, half):
        kind, row, column, width, cut = piece
        if half is not None:
            column, width = (column, cut) if half == 0 else (column + cut, width - cut)
        r = spans[0]
        x, z, y = (slice(None) if spans[axis] is None else spans[axis] for axis in (1, 2, 3))
        columns = pl.ds(column, width)
        if kind == 0:
            return outs[0].at[r, y, x, z, pl.ds(row, 16), columns]
        if kind == 1:
            return outs[1].at[:, r, x, z, y, :, columns]
        return outs[kind].at[r, x, z, y, :, columns]

    def start(unit, spans, half, axis, steps):
        copies = []
        for piece in PIECES[unit[0]]:
            if (piece[0] > 0) != unit[1] or (half == 1 and piece[3] == piece[4]):
                continue
            ref = region(piece, spans, half)
            slot = used[0]
            used[0] += 1
            copy = pltpu.make_async_remote_copy(
                src_ref=ref,
                dst_ref=ref,
                send_sem=send_sems.at[slot],
                recv_sem=recv_sems.at[slot],
                device_id=mesh_device(moved(place, axis, steps)),
                device_id_type=pl.DeviceIdType.MESH,
            )
            copy.start()
            copies.append(copy)
        return copies

    r, x, z, y = place
    own = {0: r, 1: x, 2: z, 3: y}
    targets = (
        outs[0].at[r, y, x, z], outs[1].at[:, r, x, z, y], outs[2].at[r, x, z, y],
        outs[3].at[r, x, z, y], outs[4].at[r, x, z, y],
    )
    placed = [
        pltpu.make_async_copy(source, target, local_sems.at[index])
        for index, (source, target) in enumerate(zip(ins, targets))
    ]
    for copy in placed:
        copy.start()
    greet(place, RING_MOVES)
    for copy in placed:
        copy.wait()
    pending, leaving = [], []
    units = [(third, stream) for stream in (0, 1) for third in range(3)]
    spans = {unit: dict(own) for unit in units}
    first, second = {}, {}

    def step_one(unit, stage):
        axis = ORDERS[unit[0]][stage]
        first[unit] = [start(unit, spans[unit], None, axis, steps) for steps in (1, -1)]

    for unit in units:
        step_one(unit, 0)
    for unit in units:
        pending += start(unit, spans[unit], None, 0, 1)
    for stage in range(3):
        if stage == 2:
            prepare_rows(row_ins, row_outs, column_ref)
        for unit in units:
            axis = ORDERS[unit[0]][stage]
            batch = []
            for which, steps in ((0, 1), (1, -1)):
                came = dict(spans[unit])
                came[axis] = lax.rem(own[axis] - steps + 4, 4)
                for copy in first[unit][which]:
                    copy.wait_recv()
                batch.append(start(unit, came, which, axis, steps))
                pending += start(unit, came, None, 0, 1)
            second[unit] = batch
        for unit in units:
            axis = ORDERS[unit[0]][stage]
            came = dict(spans[unit])
            came[axis] = lax.rem(own[axis] + 2, 4)
            for which in (0, 1):
                for copy in second[unit][which]:
                    copy.wait_recv()
                pending += start(unit, came, which, 0, 1)
            for copies in first[unit] + second[unit]:
                leaving += copies
            spans[unit][axis] = None
            if stage < 2:
                step_one(unit, stage + 1)
    for copy in leaving:
        copy.wait_send()
    for copy in pending:
        copy.wait()


def gather_weights(shards, rows):
    whole_torus = (2, 4, 4, 4)
    held = pl.BlockSpec(memory_space=pltpu.VMEM)
    return pl.pallas_call(
        gather_kernel,
        out_shape=(
            narrow(*whole_torus, 48, BLOCK_COLS),
            narrow(3, *whole_torus, 8, W),
            narrow(*whole_torus, 8, W),
            narrow(*whole_torus, 40, W),
            narrow(*whole_torus, 8, 128),
            wide(VCAP, D), wide(VQ, D), wide(VCAP, 1), wide(1, VQ),
            wide(MCAP + VCAP, D), wide(MQP, D), wide(MCAP + VCAP, 1), wide(1, MQP),
            narrow(MQP, C), narrow(MQP, FREQ), wide(MQP, C), wide(MQP, 1),
            wide(VCAP, 24), wide(VQ, 24), wide(VCAP, 1), wide(MCAP, 1),
        ),
        in_specs=[held] * 16,
        out_specs=(pl.BlockSpec(memory_space=pl.ANY),) * 5 + (held,) * 16,
        scratch_shapes=[
            pltpu.VMEM((48, BLOCK_COLS), LOW_TYPE),
            pltpu.VMEM((3, 8, W), LOW_TYPE),
            pltpu.VMEM((8, W), LOW_TYPE),
            pltpu.VMEM((40, W), LOW_TYPE),
            pltpu.VMEM((8, 128), LOW_TYPE),
            pltpu.VMEM((VCAP, 128), WIDE_TYPE),
            pltpu.SemaphoreType.DMA((GATHER_COPIES,)),
            pltpu.SemaphoreType.DMA((GATHER_COPIES,)),
            pltpu.SemaphoreType.DMA((5,)),
        ],
        compiler_params=pltpu.CompilerParams(
            collective_id=0, has_side_effects=True, vmem_limit_bytes=VMEM_BYTES
        ),
        name="gather_weights",
    )(*shards, *rows)


SUM_MOVES = ((0, 1),) + tuple((axis, steps) for axis in (1, 2, 3) for steps in (1, 2, 3))


MQP = 224
VMEM_BYTES = 60 * 1024 * 1024


def normed_rows(values, gain, offset):
    centered = values - jnp.mean(values, axis=-1, keepdims=True)
    inverse = lax.rsqrt(jnp.mean(centered * centered, axis=-1, keepdims=True) + LN_EPS)
    scaled = centered * inverse
    return scaled * gain + offset, scaled, inverse


def affine_rows(ref):
    return ref[0, 0].astype(WIDE_TYPE).T[0:8]


def norm_pull(upstream, scaled, inverse, gain):
    inner = upstream * gain
    return inverse * (
        inner
        - jnp.mean(inner, axis=-1, keepdims=True)
        - scaled * jnp.mean(inner * scaled, axis=-1, keepdims=True)
    )


def inner_high(left_side, right_side):
    dims = (((0,), (0,)), ((), ()))
    return lax.dot_general(left_side, right_side, dims, precision=lax.Precision.HIGHEST)


def row_sum(values):
    return jnp.sum(values, axis=0, keepdims=True)


def attention_forward_kernel(
    ready, all_ref, own_ref, keys_ref, own_ids_ref, affine_ref, w_ref,
    first_ref, low_all_ref, low_own_ref, joint_ref, query_ref, mass_ref, merged_ref,
    total,
):
    head_set = pl.program_id(0)

    @pl.when(head_set == 0)
    def _():
        affine = affine_rows(affine_ref)
        gain, offset = affine[0:1], affine[1:2]
        low_all_ref[:ready] = (all_ref[:ready] * gain + offset).astype(LOW_TYPE)
        if ready < all_ref.shape[0]:
            low_all_ref[ready:] = normed_rows(all_ref[ready:], gain, offset)[0].astype(LOW_TYPE)
        low_own_ref[...] = normed_rows(own_ref[...], gain, offset)[0].astype(LOW_TYPE)
        total[...] = own_ref[...] + affine[4:5]

    weights = w_ref[0, 0]
    joint = matmul_low(low_all_ref[...], weights[:, :384]).astype(LOW_TYPE)
    query = matmul_low(low_own_ref[...], weights[:, 384:])[:, :192].astype(LOW_TYPE)
    joint_ref[0] = joint
    query_ref[0] = query
    allowed = keys_ref[...] == own_ids_ref[...]
    parts = []
    for head in range(3):
        key = joint[:, HD * head : HD * (head + 1)]
        value = joint[:, 192 + HD * head : 192 + HD * (head + 1)]
        scores = outer_rows(key, query[:, HD * head : HD * (head + 1)]) * SCALE
        scores = jnp.where(allowed, scores, -1e30)
        peak = jnp.max(scores, axis=0, keepdims=True)
        exponent = jnp.exp(scores - peak)
        mass = row_sum(exponent)
        probability = (exponent * (1.0 / mass)).astype(LOW_TYPE)
        mass_ref[0, head : head + 1] = peak + jnp.log(mass)
        parts.append(inner_rows(value, probability))
    merged = jnp.concatenate(parts, axis=0).T.astype(LOW_TYPE)
    merged_ref[0] = merged
    total[...] += outer_rows(merged, weights[:, 576:])

    @pl.when(head_set == 3)
    def _():
        first_ref[...] = total[...]


def attention_backward_kernel(
    ready, role_ref, grad_ref, all_ref, inverse_ref, own_ref, keys_ref, own_ids_ref, affine_ref, w_ref,
    low_all_ref, low_own_ref, joint_ref, query_ref, mass_ref, merged_ref, affine_two_ref,
    left_all_ref, left_own_ref,
    mine_ref, theirs_ref, tail_grad_ref, small_ref,
    branch, all_sum, own_sum,
):
    head_set = pl.program_id(0)

    @pl.when(head_set == 0)
    def _():
        branch[...] = grad_ref[...].astype(LOW_TYPE)
        all_sum[...] = jnp.zeros_like(all_sum)
        own_sum[...] = jnp.zeros_like(own_sum)

    weights = w_ref[0, 0]
    joint = joint_ref[0]
    query = query_ref[0]
    branch_grad = branch[...]
    merged_grad = matmul_low(branch_grad, weights[:, 576:]).astype(LOW_TYPE)
    grad_out = inner_rows(branch_grad, merged_ref[0])
    allowed = keys_ref[...] == own_ids_ref[...]
    key_grads, value_grads, query_grads = [], [], []
    for head in range(3):
        key = joint[:, HD * head : HD * (head + 1)]
        value = joint[:, 192 + HD * head : 192 + HD * (head + 1)]
        one_query = query[:, HD * head : HD * (head + 1)]
        one_merged = merged_grad[:, HD * head : HD * (head + 1)]
        scores = jnp.where(allowed, outer_rows(key, one_query) * SCALE, -1e30)
        probability = jnp.exp(scores - mass_ref[0, head : head + 1])
        value_grads.append(matmul_low(probability.astype(LOW_TYPE), one_merged))
        weighted = probability * outer_rows(value, one_merged)
        score_grad = (weighted - probability * row_sum(weighted)).astype(LOW_TYPE)
        key_grads.append(matmul_low(score_grad, one_query) * SCALE)
        query_grads.append(inner_rows(key, score_grad) * SCALE)
    joint_grad = jnp.concatenate(key_grads + value_grads, axis=1).astype(LOW_TYPE)
    query_grad = jnp.concatenate(query_grads, axis=0).T.astype(LOW_TYPE)
    all_sum[...] += outer_rows(joint_grad, weights[:, :384])
    own_sum[...] += outer_rows(query_grad, weights[:, 384:576])
    grad_joint = inner_rows(low_all_ref[...], joint_grad)
    grad_rest = jnp.concatenate([inner_rows(low_own_ref[...], query_grad), grad_out], axis=1)
    first_core = role_ref[0] == 0
    mine_ref[:, :, 0] = jnp.where(first_core, grad_joint, grad_rest).reshape(4, 4, 48, 384)
    theirs = jnp.where(first_core, grad_rest, grad_joint).astype(LOW_TYPE)
    theirs_ref[:, :, 0] = theirs.reshape(4, 4, 48, 384)

    @pl.when(head_set == 3)
    def _():
        gain = affine_rows(affine_ref)[0:1]
        scaled = all_ref[:ready]
        upstream = all_sum[:ready]
        all_grad = norm_pull(upstream, scaled, inverse_ref[...], gain)
        gain_grad = row_sum(upstream * scaled)
        offset_grad = row_sum(upstream)
        tail_grad = all_grad
        if ready < all_ref.shape[0]:
            upstream = all_sum[ready:]
            _, scaled, inverse = normed_rows(all_ref[ready:], gain, gain)
            tail_grad = norm_pull(upstream, scaled, inverse, gain)
            gain_grad += row_sum(upstream * scaled)
            offset_grad += row_sum(upstream)
        tail_grad_ref[...] = tail_grad
        _, scaled, inverse = normed_rows(own_ref[...], gain, gain)
        own_grad = norm_pull(own_sum[...], scaled, inverse, gain) + grad_ref[...]
        if ready == all_ref.shape[0]:
            small_ref[...] = inner_high(left_all_ref[...], all_grad) + inner_high(
                left_own_ref[...], own_grad
            )
        else:
            small_ref[...] = jnp.zeros_like(small_ref)
            small_ref[17:18] = row_sum(all_grad) + row_sum(own_grad)
        small_ref[18:19] = gain_grad + row_sum(own_sum[...] * scaled)
        small_ref[19:20] = offset_grad + row_sum(own_sum[...])
        small_ref[20:22] = affine_two_ref[0:2]
        small_ref[22:23] = row_sum(grad_ref[...])
        small_ref[23:24] = affine_two_ref[2:3]


def feed_forward_kernel(first_ref, affine_ref, up_ref, down_ref, out_ref, low_ref, before_ref, total):
    part = pl.program_id(0)

    @pl.when(part == 0)
    def _():
        first = first_ref[...]
        affine = affine_rows(affine_ref)
        low_ref[...] = normed_rows(first, affine[2:3], affine[3:4])[0].astype(LOW_TYPE)
        total[...] = first + affine[5:6]

    before = matmul_low(low_ref[...], up_ref[0, 0])
    before_ref[0] = before
    acted = before * (0.5 * (1.0 + lax.erf(before * (1.0 / math.sqrt(2.0)))))
    total[...] += outer_rows(acted.astype(LOW_TYPE), down_ref[0, 0])

    @pl.when(part == 3)
    def _():
        out_ref[...] = total[...].astype(LOW_TYPE)


def feed_backward_kernel(
    role_ref, grad_ref, first_ref, low_ref, before_ref, affine_ref, up_ref, down_ref,
    up_mine_ref, up_theirs_ref, down_mine_ref, down_theirs_ref, first_grad_ref, affine_grad_ref,
    down_grad, total,
):
    part = pl.program_id(0)

    @pl.when(part == 0)
    def _():
        down_grad[...] = grad_ref[...].astype(LOW_TYPE)
        total[...] = jnp.zeros_like(total)

    first_core = role_ref[0] == 0

    def give(values, mine_ref, theirs_ref):
        lower, upper = values[:, :384], values[:, 384:]
        mine_ref[:, :, 0] = jnp.where(first_core, lower, upper).reshape(4, 4, 48, 384)
        theirs = jnp.where(first_core, upper, lower).astype(LOW_TYPE)
        theirs_ref[:, :, 0] = theirs.reshape(4, 4, 48, 384)

    before = before_ref[0]
    half = 0.5 * (1.0 + lax.erf(before * (1.0 / math.sqrt(2.0))))
    acted = (before * half).astype(LOW_TYPE)
    give(inner_rows(down_grad[...], acted), down_mine_ref, down_theirs_ref)
    slope = half + before * jnp.exp(-0.5 * before * before) * (1.0 / math.sqrt(2.0 * math.pi))
    before_grad = (matmul_low(down_grad[...], down_ref[0, 0]) * slope).astype(LOW_TYPE)
    give(inner_rows(low_ref[...], before_grad), up_mine_ref, up_theirs_ref)
    total[...] += outer_rows(before_grad, up_ref[0, 0])

    @pl.when(part == 3)
    def _():
        gain = affine_rows(affine_ref)[2:3]
        _, scaled, inverse = normed_rows(first_ref[...], gain, gain)
        first_grad_ref[...] = grad_ref[...] + norm_pull(total[...], scaled, inverse, gain)
        affine_grad_ref[0:1] = row_sum(total[...] * scaled)
        affine_grad_ref[1:2] = row_sum(total[...])
        affine_grad_ref[2:3] = row_sum(grad_ref[...])
        affine_grad_ref[3:8] = jnp.zeros((5, D), WIDE_TYPE)


def whole(shape):
    return pl.BlockSpec(shape, lambda part: (0,) * len(shape))


def weight_spec(which, column):
    return pl.BlockSpec((1, 1, D, D), lambda part: (which, part, 0, column))


def affine_spec(which):
    return pl.BlockSpec((1, 1, D, 128), lambda part: (which, 0, 0, 18))


def part_spec(*shape):
    return pl.BlockSpec((1,) + shape, lambda part: (part,) + (0,) * len(shape))


GRAD_SPEC = pl.BlockSpec((4, 4, 1, 48, 384), lambda part: (0, 0, part, 0, 0))
GRAD_WIDE = jax.ShapeDtypeStruct((4, 4, 4, 48, 384), WIDE_TYPE)
GRAD_LOW = jax.ShapeDtypeStruct((4, 4, 4, 48, 384), LOW_TYPE)
ROLE_SPEC = pl.BlockSpec(memory_space=pltpu.SMEM)


def cost(flops, moved_bytes):
    return pl.CostEstimate(flops=flops, bytes_accessed=moved_bytes, transcendentals=0)


def wide(*shape):
    return jax.ShapeDtypeStruct(shape, WIDE_TYPE)


def narrow(*shape):
    return jax.ShapeDtypeStruct(shape, LOW_TYPE)


def grid_call(kernel, in_specs, out_specs, out_shape, scratch, price, name):
    return pl.pallas_call(
        kernel,
        grid=(4,),
        in_specs=in_specs,
        out_specs=out_specs,
        out_shape=out_shape,
        scratch_shapes=scratch,
        compiler_params=pltpu.CompilerParams(
            dimension_semantics=("arbitrary",), vmem_limit_bytes=VMEM_BYTES
        ),
        cost_estimate=price,
        name=name,
    )


def block_forward(rows_all, inverse_all, rows_own, keys, own_ids, blocks, which):
    total, count, ready = rows_all.shape[0], rows_own.shape[0], inverse_all.shape[0]
    saved_specs = (
        whole((total, D)), whole((count, D)), part_spec(total, 384), part_spec(count, 192),
        part_spec(3, count), part_spec(count, 192),
    )
    first, *saved = grid_call(
        functools.partial(attention_forward_kernel, ready),
        [
            whole((total, D)), whole((count, D)), whole((total, 1)), whole((1, count)),
            affine_spec(which), weight_spec(which, 0),
        ],
        (whole((count, D)),) + saved_specs,
        (
            wide(count, D), narrow(total, D), narrow(count, D), narrow(4, total, 384),
            narrow(4, count, 192), wide(4, 3, count), narrow(4, count, 192),
        ),
        [pltpu.VMEM((count, D), WIDE_TYPE)],
        cost(2 * total * D * 2 * D + 24 * total * count * 256, 20 * total * D),
        "attention_forward",
    )(rows_all, rows_own, keys, own_ids, blocks, blocks)
    result, low_two, before = grid_call(
        feed_forward_kernel,
        [whole((count, D)), affine_spec(which), weight_spec(which, 1), weight_spec(which, 2)],
        (whole((count, D)), whole((count, D)), part_spec(count, D)),
        (narrow(count, D), narrow(count, D), wide(4, count, D)),
        [pltpu.VMEM((count, D), WIDE_TYPE)],
        cost(4 * count * D * FF, 4 * D * FF),
        "feed_forward",
    )(first, blocks, blocks, blocks)
    return result, (rows_all, inverse_all, rows_own, keys, own_ids, saved, first, low_two, before)


def block_backward(upstream, kept, blocks, which, role_array, left_all, left_own):
    rows_all, inverse_all, rows_own, keys, own_ids, saved, first, low_two, before = kept
    total, count, ready = rows_all.shape[0], rows_own.shape[0], inverse_all.shape[0]
    up_mine, up_theirs, down_mine, down_theirs, first_grad, affine_two = grid_call(
        feed_backward_kernel,
        [
            ROLE_SPEC, whole((count, D)), whole((count, D)), whole((count, D)),
            part_spec(count, D), affine_spec(which), weight_spec(which, 1), weight_spec(which, 2),
        ],
        (GRAD_SPEC,) * 4 + (whole((count, D)), whole((8, D))),
        (GRAD_WIDE, GRAD_LOW, GRAD_WIDE, GRAD_LOW, wide(count, D), wide(8, D)),
        [pltpu.VMEM((count, D), LOW_TYPE), pltpu.VMEM((count, D), WIDE_TYPE)],
        cost(8 * count * D * FF, 16 * D * FF),
        "feed_backward",
    )(role_array, upstream, first, low_two, before, blocks, blocks, blocks)
    mine, theirs, tail_grad, small = grid_call(
        functools.partial(attention_backward_kernel, ready),
        [
            ROLE_SPEC, whole((count, D)), whole((total, D)), whole((ready, 1)), whole((count, D)),
            whole((total, 1)), whole((1, count)), affine_spec(which), weight_spec(which, 0),
            whole((total, D)), whole((count, D)), part_spec(total, 384), part_spec(count, 192),
            part_spec(3, count), part_spec(count, 192), whole((8, D)), whole((VCAP, 24)),
            whole((VQ, 24)),
        ],
        (GRAD_SPEC, GRAD_SPEC, whole((VCAP, D)), whole((24, D))),
        (GRAD_WIDE, GRAD_LOW, wide(VCAP, D), wide(24, D)),
        [
            pltpu.VMEM((count, D), LOW_TYPE),
            pltpu.VMEM((total, D), WIDE_TYPE),
            pltpu.VMEM((count, D), WIDE_TYPE),
        ],
        cost(4 * total * D * 2 * D + 24 * total * count * 640, 30 * total * D),
        "attention_backward",
    )(
        role_array, first_grad, rows_all, inverse_all, rows_own, keys, own_ids, blocks, blocks, *saved,
        affine_two, left_all, left_own,
    )
    mine_all = (mine, up_mine, down_mine)
    theirs_all = (theirs, up_theirs, down_theirs)
    grads = list(zip(mine_all, theirs_all))
    return tail_grad, grads, small


B_FIRST = (True, False, True)
FAMILIES = (("blk", "head"), ("blk", "head"), ("blk", "head", "ext"))
UNITS = tuple((third, stream) for stream in (0, 1) for third in range(3))
NAMES = {
    unit: [name for name in FAMILIES[unit[0]] if (name == "blk") == (unit[1] == 1)] for unit in UNITS
}
TAILS = {"blk": (2, 48, 384), "head": (24, 1024), "ext": (8, 128)}
REDUCE_COPIES = 384
SMALL_ROWS = 32


def reduce_kernel(*refs):
    mine, theirs, ext = refs[0:9], refs[9:18], refs[18]
    enc_small, dec_small, loss = refs[19:22]
    kept_out, taken_out, head_out, ext_out, small_out, norm_out = refs[22:28]
    crossed = refs[28:38]
    scratch = list(refs[38:])
    third_refs = [dict() for _ in range(3)]
    for third in range(3):
        for name in FAMILIES[third]:
            third_refs[third][name] = {
                key: scratch.pop(0)
                for key in ("pool", "give", "rest", "come", "last", "b_come", "b_last", "c_come", "c_last")
            }
    pool_low = [{name: scratch.pop(0) for name in FAMILIES[third]} for third in range(3)]
    hand, small_held, small_slots, norm_held, norm_slots = scratch[:5]
    send_sems, recv_sems, load_sems = scratch[5:]
    place = mesh_place()
    used = [0, 0]
    flying = []

    def push(source, target, axis, steps):
        slot = used[0]
        used[0] += 1
        copy = pltpu.make_async_remote_copy(
            src_ref=source,
            dst_ref=target,
            send_sem=send_sems.at[slot],
            recv_sem=recv_sems.at[slot],
            device_id=mesh_device(moved(place, axis, steps)),
            device_id_type=pl.DeviceIdType.MESH,
        )
        copy.start()
        flying.append(copy)
        return copy

    def sent(copies):
        for copy in copies:
            copy.wait_send()
            flying[:] = [other for other in flying if other is not copy]

    def load(source, target):
        copy = pltpu.make_async_copy(source, target, load_sems.at[used[1]])
        used[1] += 1
        copy.start()
        return copy

    def half_spans(third, steps, half):
        first, second, _ = ORDERS[third]
        spans = [slice(None)] * 3
        spans[first - 1] = lax.rem(place[first] + steps + 4, 4)
        spans[second - 1] = pl.ds(2 * half, 2)
        return spans

    def arrays(unit):
        third, stream = unit
        group, low = third_refs[third], pool_low[third]
        if stream == 1:
            for block in range(2):
                index = 3 * block + third
                pools = group["blk"]["pool"].at[:, :, block], low["blk"].at[:, :, block]
                yield mine[index], theirs[index], crossed[index], *pools
            return
        index = 6 + third
        yield mine[index], theirs[index], crossed[index], group["head"]["pool"], low["head"]
        if third == 2:
            given = ext.at[1 - place[0]]
            yield ext.at[place[0]], given, crossed[9], group["ext"]["pool"], low["ext"]

    def cross(unit, steps, half):
        spans = half_spans(unit[0], steps, half)
        crossing[unit, steps, half] = [
            push(given.at[*spans], landed.at[*spans], 0, 1)
            for _, given, landed, _, _ in arrays(unit)
        ]

    def fetch(unit, steps, half):
        spans = half_spans(unit[0], steps, half)
        spot = lead(unit[0], pl.ds(2 * half, 2), slice(None))
        copies = []
        for crossed_copy, (kept, _, landed, pool, low) in zip(
            crossing[unit, steps, half], arrays(unit)
        ):
            copies.append(load(kept.at[*spans], pool.at[*spot]))
            crossed_copy.wait_recv()
            copies.append(load(landed.at[*spans], low.at[*spot]))
        return copies

    def lead(third, b, c):
        return (b, c) if B_FIRST[third] else (c, b)

    def values(third, name, b, c):
        spot = lead(third, b, c)
        total = third_refs[third][name]["pool"][spot]
        return total + pool_low[third][name][spot].astype(WIDE_TYPE)

    def halves(unit, half, body):
        def step(count, carry):
            inner, c = lax.div(count, 4), lax.rem(count, 4)
            for name in NAMES[unit]:
                body(name, inner, c, 2 * half + inner)
            return carry

        lax.fori_loop(0, 8, step, 0)

    def small_stage(held, slots, stage):
        axis = (0, 3, 1, 2)[stage]
        count = 2 if axis == 0 else 4
        copies = [
            push(held.at[stage], slots.at[stage, place[axis]], axis, steps)
            for steps in range(1, count)
        ]
        slots[stage, place[axis]] = held[stage]

        def finish():
            for copy in copies:
                copy.wait_recv()
            total = slots[stage, 0]
            for index in range(1, count):
                total = total + slots[stage, index]
            held[stage + 1] = total

        return finish

    def arrive(copies):
        for copy in copies:
            copy.wait()

    def received(copies):
        for copy in copies:
            copy.wait_recv()

    def both(unit, *steps):
        return [fetch(unit, step, half) for half, step in enumerate(steps)]

    greet(place, SUM_MOVES)
    crossing = {}
    for pair in ((2, 2), (-1, 1), (1, -1), (0, 0)):
        for unit in UNITS:
            for half in (0, 1):
                cross(unit, pair[half], half)
    loads = {}

    def ahead(low_steps, high_steps):
        loads[UNITS[0]] = both(UNITS[0], low_steps, high_steps)
        for unit, later in zip(UNITS, UNITS[1:] + (None,)):
            if later is not None:
                loads[later] = both(later, low_steps, high_steps)
            yield unit

    small_held[0, 0:24] = enc_small[...]
    small_held[0, 0:18] += dec_small[0:18]
    small_held[0, 24:30] = dec_small[18:24]
    small_held[0, 30:32] = jnp.concatenate([loss[0:2]] * 6, axis=1)
    small = small_stage(small_held, small_slots, 0)

    first, last = ({unit: [] for unit in UNITS} for _ in range(2))
    for unit in ahead(2, 2):
        third = unit[0]
        group = third_refs[third]
        for half in (0, 1):
            arrive(loads[unit][half])

            def give(name, inner, c, b, half=half, third=third, unit=unit, group=group):
                total = values(third, name, b, c).astype(LOW_TYPE)
                group[name]["give"][half, inner, c] = total

            halves(unit, half, give)
            first[unit].append(
                [
                    push(
                        group[name]["give"].at[half],
                        group[name]["come"].at[half],
                        ORDERS[third][0],
                        1 - 2 * half,
                    )
                    for name in NAMES[unit]
                ]
            )
    small()
    small = small_stage(small_held, small_slots, 1)

    for unit in ahead(-1, 1):
        third = unit[0]
        group = third_refs[third]
        for way in (1, 0):
            arrive(loads[unit][1 - way])

            def keep(name, inner, c, b, way=way, third=third, unit=unit, group=group):
                group[name]["rest"][way, inner, c] = values(third, name, b, c).astype(LOW_TYPE)

            halves(unit, 1 - way, keep)
            for name in NAMES[unit]:
                refs_of = group[name]
                source, target = refs_of["rest"].at[way], refs_of["last"].at[way, 1 - way]
                last[unit].append(push(source, target, ORDERS[third][0], 1 - 2 * way))
    small()
    small = small_stage(small_held, small_slots, 2)
    for unit in ahead(1, -1):
        third = unit[0]
        group = third_refs[third]
        for way in (0, 1):
            arrive(loads[unit][way])
            received(first[unit][way])

            def join(name, inner, c, b, way=way, third=third, unit=unit, group=group):
                total = values(third, name, b, c)
                total = total + group[name]["come"][way, inner, c].astype(WIDE_TYPE)
                group[name]["come"][way, inner, c] = total.astype(LOW_TYPE)

            halves(unit, way, join)
            for name in NAMES[unit]:
                refs_of = group[name]
                source, target = refs_of["come"].at[way], refs_of["last"].at[way, way]
                last[unit].append(push(source, target, ORDERS[third][0], 1 - 2 * way))
    small()
    small = small_stage(small_held, small_slots, 3)

    second, ready = ({unit: [] for unit in UNITS} for _ in range(2))
    for unit in ahead(0, 0):
        third = unit[0]
        axis = ORDERS[third][1]
        group = third_refs[third]
        received(last[unit])
        for half in (0, 1):
            arrive(loads[unit][half])

            def total_up(name, inner, c, b, half=half, third=third, unit=unit, group=group):
                total = values(third, name, b, c)
                for way in (0, 1):
                    total = total + group[name]["last"][way, half, inner, c].astype(WIDE_TYPE)
                group[name]["pool"][lead(third, b, c)] = total

            halves(unit, half, total_up)
            sent(first[unit][half])

        def pack(b, spot, start, third=third, unit=unit, group=group):
            for name in NAMES[unit]:
                refs_of = group[name]
                for c in (start, start + 1):
                    total = refs_of["pool"][lead(third, b, c)]
                    refs_of["give"][(*spot, c)] = total.astype(LOW_TYPE)

        opposite = lax.rem(place[axis] + 2, 4)
        for way in (0, 1):
            pack(opposite, (0, 0), 2 * way)
            second[unit].append(
                [
                    push(
                        group[name]["give"].at[0, 0, pl.ds(2 * way, 2)],
                        group[name]["b_come"].at[way],
                        axis,
                        1 - 2 * way,
                    )
                    for name in NAMES[unit]
                ]
            )
        for way, spot in ((0, (0, 1)), (1, (1, 0))):
            steps = 1 - 2 * way
            pack(lax.rem(place[axis] + steps + 4, 4), spot, 2 - 2 * way)
            part = pl.ds(2 - 2 * way, 2)
            for name in NAMES[unit]:
                refs_of = group[name]
                source, target = refs_of["give"].at[*spot, part], refs_of["b_last"].at[way, part]
                ready[unit].append(push(source, target, axis, steps))
    small()
    small_out[...] = small_held[4]
    for unit in UNITS:
        third = unit[0]
        axis = ORDERS[third][1]
        group = third_refs[third]
        for way, spot in ((0, (0, 1)), (1, (1, 0))):
            steps = 1 - 2 * way
            b = lax.rem(place[axis] + steps + 4, 4)
            received(second[unit][way])
            part = pl.ds(2 * way, 2)
            for name in NAMES[unit]:
                refs_of = group[name]
                for inner in range(2):
                    c = 2 * way + inner
                    total = refs_of["pool"][lead(third, b, c)]
                    total = total + refs_of["b_come"][way, inner].astype(WIDE_TYPE)
                    refs_of["give"][(*spot, c)] = total.astype(LOW_TYPE)
                source, target = refs_of["give"].at[*spot, part], refs_of["b_last"].at[way, part]
                ready[unit].append(push(source, target, axis, steps))

    second, last = ({unit: [] for unit in UNITS} for _ in range(2))
    for unit in UNITS:
        third = unit[0]
        axis = ORDERS[third][2]
        own_b = place[ORDERS[third][1]]
        group = third_refs[third]
        received(ready[unit])
        for name in NAMES[unit]:
            refs_of = group[name]
            for c in range(4):
                total = refs_of["pool"][lead(third, own_b, c)]
                for way in (0, 1):
                    total = total + refs_of["b_last"][way, c].astype(WIDE_TYPE)
                refs_of["pool"][lead(third, own_b, c)] = total
        pieces = c_pieces(unit)
        spot = lead(third, own_b, lax.rem(place[axis] + 2, 4))
        for way in (0, 1):
            second[unit].append(
                [
                    push(
                        group[name]["pool"].at[(*spot, *piece)],
                        group[name]["c_come"].at[piece],
                        axis,
                        1 - 2 * way,
                    )
                    for name, piece in pieces[way]
                ]
            )
        for way in (0, 1):
            steps = 1 - 2 * way
            spot = lead(third, own_b, lax.rem(place[axis] + steps + 4, 4))
            for name, piece in pieces[1 - way]:
                source = group[name]["pool"].at[(*spot, *piece)]
                target = group[name]["c_last"].at[(way, *piece)]
                last[unit].append(push(source, target, axis, steps))
    for unit in UNITS:
        third = unit[0]
        axis = ORDERS[third][2]
        own_b = place[ORDERS[third][1]]
        group = third_refs[third]
        pieces = c_pieces(unit)
        for way in (0, 1):
            steps = 1 - 2 * way
            spot = lead(third, own_b, lax.rem(place[axis] + steps + 4, 4))
            received(second[unit][way])
            for name, piece in pieces[way]:
                refs_of = group[name]
                refs_of["pool"][(*spot, *piece)] += refs_of["c_come"][piece]
                source = refs_of["pool"].at[(*spot, *piece)]
                target = refs_of["c_last"].at[(way, *piece)]
                last[unit].append(push(source, target, axis, steps))
    squares_sum = jnp.zeros((), WIDE_TYPE)
    handed = []
    for unit in UNITS:
        third = unit[0]
        axis = ORDERS[third][2]
        spot = lead(third, place[ORDERS[third][1]], place[axis])
        for copy in last[unit]:
            copy.wait_recv()
        for name in NAMES[unit]:
            refs_of = third_refs[third][name]
            total = refs_of["pool"][spot] + (refs_of["c_last"][0] + refs_of["c_last"][1])
            refs_of["pool"][spot] = total
            squares_sum += jnp.sum(total * total)
            if name == "head":
                head_out[third] = total
            if name == "ext":
                ext_out[...] = total
        if unit[1] == 0:
            continue
        blk = third_refs[third]["blk"]["pool"]
        handed.append(push(blk.at[(*spot, 1 - place[0])], hand.at[third], 0, 1))
        kept_out[third] = blk[(*spot, place[0])]
    small_total = small_held[4, 0:30]
    squares_sum += jnp.sum(small_total * small_total) * (1.0 / 128.0)
    norm_held[0] = jnp.full((8, 128), squares_sum)
    for stage in range(4):
        small_stage(norm_held, norm_slots, stage)()
    norm_out[...] = norm_held[4]
    for copy in handed:
        copy.wait_recv()
    taken_out[...] = hand[...]
    for copy in list(flying):
        copy.wait_send()


def c_pieces(unit):
    everything = slice(None)
    if unit[1] == 1:
        return [("blk", (0,))], [("blk", (1,))]
    lower = [("head", (everything, pl.ds(0, 512)))]
    upper = [("head", (everything, pl.ds(512, 512)))]
    if unit[0] == 2:
        lower.append(("ext", (everything, everything)))
    return lower, upper


def reduce_gradients(mine, theirs, ext, enc_small, dec_small, loss):
    scratch = []
    for third in range(3):
        for name in FAMILIES[third]:
            tail = TAILS[name]
            scratch += [
                pltpu.VMEM((4, 4) + tail, WIDE_TYPE),
                pltpu.VMEM((2, 2, 4) + tail, LOW_TYPE),
                pltpu.VMEM((2, 2, 4) + tail, LOW_TYPE),
                pltpu.VMEM((2, 2, 4) + tail, LOW_TYPE),
                pltpu.VMEM((2, 2, 2, 4) + tail, LOW_TYPE),
                pltpu.VMEM((2, 2) + tail, LOW_TYPE),
                pltpu.VMEM((2, 4) + tail, LOW_TYPE),
                pltpu.VMEM(tail, WIDE_TYPE),
                pltpu.VMEM((2,) + tail, WIDE_TYPE),
            ]
    for third in range(3):
        for name in FAMILIES[third]:
            kind = WIDE_TYPE if name == "ext" else LOW_TYPE
            scratch.append(pltpu.VMEM((4, 4) + TAILS[name], kind))
    scratch += [
        pltpu.VMEM((3, 48, 384), WIDE_TYPE),
        pltpu.VMEM((5, SMALL_ROWS, D), WIDE_TYPE),
        pltpu.VMEM((4, 4, SMALL_ROWS, D), WIDE_TYPE),
        pltpu.VMEM((5, 8, 128), WIDE_TYPE),
        pltpu.VMEM((4, 4, 8, 128), WIDE_TYPE),
        pltpu.SemaphoreType.DMA((REDUCE_COPIES,)),
        pltpu.SemaphoreType.DMA((REDUCE_COPIES,)),
        pltpu.SemaphoreType.DMA((256,)),
    ]
    held = pl.BlockSpec(memory_space=pltpu.VMEM)
    return pl.pallas_call(
        reduce_kernel,
        out_shape=(
            wide(3, 48, 384),
            wide(3, 48, 384),
            wide(3, 24, 1024),
            wide(8, 128),
            wide(SMALL_ROWS, D),
            wide(8, 128),
        )
        + (narrow(4, 4, 4, 48, 384),) * 6
        + (narrow(4, 4, 4, 24, W),) * 3
        + (wide(4, 4, 4, 8, 128),),
        in_specs=[pl.BlockSpec(memory_space=pl.ANY)] * 19 + [held] * 3,
        out_specs=(held,) * 6 + (pl.BlockSpec(memory_space=pl.ANY),) * 10,
        scratch_shapes=scratch,
        compiler_params=pltpu.CompilerParams(
            collective_id=1, has_side_effects=True, vmem_limit_bytes=REDUCE_VMEM
        ),
        name="reduce_gradients",
    )(*mine, *theirs, ext, enc_small, dec_small, loss)[:6]


REDUCE_VMEM = 63 * 1024 * 1024


def silu_pair(values):
    gate = lax.logistic(values)
    return (values * gate).astype(LOW_TYPE), gate * (1.0 + values * (1.0 - gate))


def plain_rows(values):
    centered = values - jnp.mean(values, axis=-1, keepdims=True)
    inverse = lax.rsqrt(jnp.mean(centered * centered, axis=-1, keepdims=True) + LN_EPS)
    return centered * inverse, inverse


def plain_pull(upstream, scaled, inverse):
    return inverse * (
        upstream
        - jnp.mean(upstream, axis=-1, keepdims=True)
        - scaled * jnp.mean(upstream * scaled, axis=-1, keepdims=True)
    )


def slot_share(tables):
    lane = lax.broadcasted_iota(jnp.int32, (1, W), 1)
    one_each = ((lane & 31) == 0) & (lane < W // 2)
    counts = [0.0, 0.0]
    for slot in range(2):
        masked = jnp.where(
            one_each, 32.0 * tables[64 + slot : 65 + slot] + tables[66 + slot : 67 + slot], 0.0
        )
        bucket = tables[68 + slot : 69 + slot]
        counts[0] += jnp.sum(masked * (1.0 - bucket), axis=1, keepdims=True)
        counts[1] += jnp.sum(masked * bucket, axis=1, keepdims=True)
    own = lane == lax.axis_index("dp") * 32
    first = lax.axis_index("mp") < 2
    bucket = jnp.sum(
        jnp.where(own, jnp.where(first, tables[68:69], tables[69:70]), 0.0), axis=1, keepdims=True
    )
    return jnp.where(bucket == 1.0, BUCKET_SHARE[1] / counts[1], BUCKET_SHARE[0] / counts[0])


def head_kernel(
    condition_ref, noisy_ref, features_ref, noise_ref, valid_ref, entry_in, square_in,
    modulate_in, extra_ref,
    cond_grad_ref, time_grad_ref, one_grad_ref, two_grad_ref, mod_grad_ref,
    time_act_ref, mod_in_ref, hidden_act_ref, cond_act_ref, decoded_grad_ref, extra_grad_ref,
    loss_ref,
    modulation, tables, extra_rows, pulled, entry_ref, square_ref, modulate_ref, load_sems,
):
    parts = [(entry_in, entry_ref)]
    parts += [(square_in.at[index], square_ref.at[index]) for index in range(3)]
    spans = [pl.ds(W * part, W) for part in range(5)]
    parts += [(modulate_in.at[span], modulate_ref.at[span]) for span in spans]
    loads = [
        pltpu.make_async_copy(source, target, load_sems.at[index])
        for index, (source, target) in enumerate(parts)
    ]
    for index in (0, 1, 4, 5, 6, 7, 8, 2, 3):
        loads[index].start()
    tables[...] = extra_ref[...].astype(WIDE_TYPE).T
    table_in = tables[0:C].astype(LOW_TYPE)
    table_out = tables[C : 2 * C].astype(LOW_TYPE)

    def bias(index):
        return tables[2 * C + index : 2 * C + index + 1]

    condition = condition_ref[...]
    loads[0].wait()
    time_pre = outer_rows(features_ref[...], entry_ref[:, D:]) + bias(1)
    time_act, time_slope = silu_pair(time_pre)
    time_act_ref[...] = time_act
    cond_pre = outer_rows(condition, entry_ref[:, :D]) + bias(0)
    loads[1].wait()
    cond_pre = cond_pre + (outer_rows(time_act, square_ref[0]) + bias(2))
    cond_act, cond_slope = silu_pair(cond_pre)
    cond_act_ref[...] = cond_act

    def modulate(part, carry):
        span = pl.ds(pl.multiple_of(W * part, W), W)
        pltpu.make_async_copy(
            modulate_in.at[span], modulate_ref.at[span], load_sems.at[4 + part]
        ).wait()
        rows = modulate_ref[pl.ds(pl.multiple_of(W * part, W), W)]
        offset = tables[pl.ds(2 * C + 6 + part, 1)]
        modulation[part] = outer_rows(cond_act_ref[...], rows) + offset
        return carry

    lax.fori_loop(0, 5, modulate, 0)
    entry_x = matmul_low(noisy_ref[...], table_in) + bias(3)
    scaled_in, inverse_in = plain_rows(entry_x)
    mod_in = (scaled_in * (1.0 + modulation[1]) + modulation[0]).astype(LOW_TYPE)
    mod_in_ref[...] = mod_in
    loads[2].wait()
    hidden_one = outer_rows(mod_in, square_ref[1]) + bias(4)
    hidden_act, hidden_slope = silu_pair(hidden_one)
    hidden_act_ref[...] = hidden_act
    loads[3].wait()
    hidden_two = outer_rows(hidden_act, square_ref[2]) + bias(5)
    leaving = entry_x + modulation[2] * hidden_two
    scaled_out, inverse_out = plain_rows(leaving)
    mod_out = (scaled_out * (1.0 + modulation[4]) + modulation[3]).astype(LOW_TYPE)
    error = outer_rows(mod_out, table_out) - noise_ref[...]
    weight = valid_ref[...] * slot_share(tables)
    row_loss = jnp.mean(error * error, axis=1, keepdims=True)
    loss_ref[...] = jnp.full((8, 128), jnp.sum(weight * row_loss))
    pred_grad = (weight * (2.0 / C) * error).astype(LOW_TYPE)
    extra_rows[...] = jnp.zeros_like(extra_rows)
    extra_rows[C : 2 * C] = inner_rows(pred_grad, mod_out)
    mod_out_grad = matmul_low(pred_grad, table_out)
    leaving_grad = plain_pull(mod_out_grad * (1.0 + modulation[4]), scaled_out, inverse_out)

    def give_mod(part, values):
        low = values.astype(LOW_TYPE)
        mod_grad_ref[:, W * part : W * (part + 1)] = low
        row = 2 * C + 6 + part
        extra_rows[row : row + 1] = row_sum(low.astype(WIDE_TYPE))

    def bias_grad(index, low):
        row = 2 * C + index
        extra_rows[row : row + 1] = row_sum(low.astype(WIDE_TYPE))

    give_mod(3, mod_out_grad)
    give_mod(4, mod_out_grad * scaled_out)
    give_mod(2, leaving_grad * hidden_two)
    two_grad = (leaving_grad * modulation[2]).astype(LOW_TYPE)
    two_grad_ref[...] = two_grad
    bias_grad(5, two_grad)
    one_grad = (matmul_low(two_grad, square_ref[2]) * hidden_slope).astype(LOW_TYPE)
    one_grad_ref[...] = one_grad
    bias_grad(4, one_grad)
    mod_in_grad = matmul_low(one_grad, square_ref[1])
    give_mod(0, mod_in_grad)
    give_mod(1, mod_in_grad * scaled_in)
    entry_x_grad = plain_pull(mod_in_grad * (1.0 + modulation[1]), scaled_in, inverse_in)
    entry_x_grad = (entry_x_grad + leaving_grad).astype(LOW_TYPE)
    bias_grad(3, entry_x_grad)
    extra_rows[0:C] = inner_rows(noisy_ref[...], entry_x_grad)
    pulled[...] = jnp.zeros_like(pulled)

    def pull(part, carry):
        start = pl.multiple_of(W * part, W)
        pulled[...] += matmul_low(mod_grad_ref[:, pl.ds(start, W)], modulate_ref[pl.ds(start, W)])
        return carry

    lax.fori_loop(0, 5, pull, 0)
    cond_grad = (pulled[...] * cond_slope).astype(LOW_TYPE)
    cond_grad_ref[...] = cond_grad
    bias_grad(0, cond_grad)
    bias_grad(2, cond_grad)
    decoded_grad = matmul_low(cond_grad, entry_ref[:, :D]).astype(LOW_TYPE)
    decoded_grad_ref[...] = decoded_grad.astype(WIDE_TYPE)
    time_grad = (matmul_low(cond_grad, square_ref[0]) * time_slope).astype(LOW_TYPE)
    time_grad_ref[...] = time_grad
    bias_grad(1, time_grad)
    extra_grad_ref[...] = extra_rows[...].T


def head_grad_kernel(role_ref, *refs):
    mine_of, theirs_of = refs[0:5], refs[5:10]
    time_act, mod_in, hidden_act, cond_act, condition, features = [ref[...] for ref in refs[10:16]]
    mine_out, theirs_out = refs[16:19], refs[19:22]
    for grads, outs, kind in ((mine_of, mine_out, WIDE_TYPE), (theirs_of, theirs_out, LOW_TYPE)):
        cond_grad, time_grad, one_grad, two_grad, mod_grad = [ref[...] for ref in grads]

        def rows(left, right):
            product = inner_rows(left, right)
            return product.reshape(16, product.shape[0] // 16, product.shape[1])

        def put(out, pieces):
            joined = jnp.concatenate(pieces, axis=1).astype(kind)
            out[0] = joined.reshape(4, 4, 24, W)

        put(
            outs[0],
            [rows(cond_grad, time_act), rows(one_grad, mod_in), rows(two_grad, hidden_act)],
        )
        mod_rows = rows(mod_grad, cond_act)
        entry = jnp.concatenate([rows(cond_grad, condition), rows(time_grad, features)], axis=2)
        put(outs[1], [mod_rows[:, :24]])
        put(outs[2], [mod_rows[:, 24:], entry])


HEAD_PARTS = (128, 128, 128, 128, 640)


def head_step(condition, noisy, features, noise_rows, valid, tables, role_array):
    entry, squares, modulate, extras = tables
    rows = condition.shape[0]
    held = pl.BlockSpec(memory_space=pltpu.VMEM)
    outs = pl.pallas_call(
        head_kernel,
        out_shape=(
            narrow(rows, W), narrow(rows, W), narrow(rows, W), narrow(rows, W),
            narrow(rows, 5 * W),
            narrow(rows, W), narrow(rows, W), narrow(rows, W), narrow(rows, W),
            wide(rows, D), wide(W, 128), wide(8, 128),
        ),
        in_specs=[held] * 5 + [pl.BlockSpec(memory_space=pl.ANY)] * 3 + [held],
        out_specs=(held,) * 12,
        scratch_shapes=[
            pltpu.VMEM((5, rows, W), WIDE_TYPE),
            pltpu.VMEM((128, W), WIDE_TYPE),
            pltpu.VMEM((128, W), WIDE_TYPE),
            pltpu.VMEM((rows, W), WIDE_TYPE),
            pltpu.VMEM((W, W), LOW_TYPE),
            pltpu.VMEM((3, W, W), LOW_TYPE),
            pltpu.VMEM((5 * W, W), LOW_TYPE),
            pltpu.SemaphoreType.DMA((9,)),
        ],
        compiler_params=pltpu.CompilerParams(vmem_limit_bytes=VMEM_BYTES),
        cost_estimate=cost(4 * rows * W * 9 * W, 20 * W * W),
        name="head_step",
    )(condition, noisy, features, noise_rows, valid, entry, squares, modulate, extras)
    grads, inputs = outs[:5], outs[5:9]
    decoded_grad, extra_grad, loss = outs[9:]

    def half(width, other):
        def index(plane, role_ref):
            return (0, (jnp.abs(role_ref[0] - other)) * 4 + plane)

        return pl.BlockSpec((rows, width), index)

    def full(width):
        return pl.BlockSpec((rows, width), lambda plane, role_ref: (0, 0))

    out_spec = pl.BlockSpec((1, 4, 4, 24, W), lambda plane, role_ref: (plane, 0, 0, 0, 0))
    sums = pl.pallas_call(
        head_grad_kernel,
        grid_spec=pltpu.PrefetchScalarGridSpec(
            num_scalar_prefetch=1,
            grid=(4,),
            in_specs=[half(width, 0) for width in HEAD_PARTS]
            + [half(width, 1) for width in HEAD_PARTS]
            + [full(W)] * 4
            + [full(D), full(FREQ)],
            out_specs=(out_spec,) * 6,
        ),
        out_shape=(wide(4, 4, 4, 24, W),) * 3 + (narrow(4, 4, 4, 24, W),) * 3,
        compiler_params=pltpu.CompilerParams(
            dimension_semantics=("arbitrary",), vmem_limit_bytes=VMEM_BYTES
        ),
        cost_estimate=cost(2 * rows * W * 9 * W, 60 * W * W),
        name="head_gradients",
    )(role_array, *grads, *grads, *inputs, condition, features)
    pairs = list(zip(sums[:3], sums[3:]))
    return loss, pairs, extra_grad, decoded_grad


def adam_kernel(*refs):
    kept_ref, taken_ref, head_ref, ext_ref, small_ref, norm_ref = refs[:6]
    params, firsts, seconds = refs[6:15], refs[15:24], refs[24:33]
    outs, (loss_out, norm_out) = refs[33:60], refs[60:]
    role, dp_index = lax.axis_index("role"), lax.axis_index("dp")
    norm = jnp.sqrt(norm_ref[0:1, 0:1])
    factor = jnp.minimum(1.0, CLIP_NORM / (norm + 1e-06))
    norm_out[0, 0] = jnp.sum(norm)
    loss_out[0, 0] = jnp.sum(small_ref[30:31, 0:1])

    def update(index, grad, at=()):
        spot = at if at else (Ellipsis,)
        scaled = factor * grad
        first = BETA_ONE * firsts[index][spot] + (1.0 - BETA_ONE) * scaled
        second = BETA_TWO * seconds[index][spot] + (1.0 - BETA_TWO) * scaled * scaled
        weight = params[index][spot]
        first_hat = first * (1.0 / (1.0 - BETA_ONE**STEP))
        second_hat = second * (1.0 / (1.0 - BETA_TWO**STEP))
        outs[3 * index][spot] = first
        outs[3 * index + 1][spot] = second
        outs[3 * index + 2][spot] = weight - RATE * (
            first_hat / (jnp.sqrt(second_hat) + ADAM_EPS) + DECAY * weight
        )

    first_core = role == 0
    lower = [jnp.where(first_core, kept_ref[part], taken_ref[part]) for part in range(3)]
    upper = [jnp.where(first_core, taken_ref[part], kept_ref[part]) for part in range(3)]
    update(0, small_ref[0 : C + 2])
    for head in range(3):
        spans = [slice(HD * head, HD * (head + 1)), slice(192 + HD * head, 192 + HD * (head + 1))]
        pieces = [upper[0][:, spans[0]], lower[0][:, spans[0]], lower[0][:, spans[1]]]
        update(1, jnp.concatenate(pieces, axis=1), (head,))
    update(2, upper[0][:, 192:])
    update(3, jnp.concatenate([lower[1], upper[1]], axis=1))
    update(4, jnp.concatenate([lower[2], upper[2]], axis=1))
    rows = jnp.where(first_core, small_ref[18:24], small_ref[24:30])
    column = lax.broadcasted_iota(jnp.int32, (D, 48), 0)
    wanted = lax.broadcasted_iota(jnp.int32, (D, 48), 1) + dp_index * 48
    rows = matmul_high(rows, (column == wanted).astype(WIDE_TYPE))
    for row in range(6):
        update(5, rows[row : row + 1], (row,))
    entry = jnp.concatenate([head_ref[2, 16:24], ext_ref[...]], axis=1)
    update(6, entry[:, :HE])
    for part in range(3):
        update(7, head_ref[0, 8 * part : 8 * part + 8], (part,))
    update(8, jnp.concatenate([head_ref[1], head_ref[2, 0:16]], axis=0))


def adam_all(sums, params, firsts, seconds):
    held = pl.BlockSpec(memory_space=pltpu.VMEM)
    return pl.pallas_call(
        adam_kernel,
        out_shape=tuple(wide(*item.shape) for item in params for _ in range(3)) + (wide(1, 1),) * 2,
        in_specs=[held] * 33,
        out_specs=(held,) * 27 + (pl.BlockSpec(memory_space=pltpu.SMEM),) * 2,
        compiler_params=pltpu.CompilerParams(vmem_limit_bytes=VMEM_BYTES),
        name="adam",
    )(*sums, *params, *firsts, *seconds)


def per_device(
    latents,
    noise_draws,
    timesteps,
    buckets,
    visible_index,
    patch_embed,
    patch_embed_first,
    patch_embed_second,
    attention_in,
    attention_in_first,
    attention_in_second,
    attention_out,
    attention_out_first,
    attention_out_second,
    feedforward_in,
    feedforward_in_first,
    feedforward_in_second,
    feedforward_out,
    feedforward_out_first,
    feedforward_out_second,
    block_affine,
    block_affine_first,
    block_affine_second,
    head_entry,
    head_entry_first,
    head_entry_second,
    head_square,
    head_square_first,
    head_square_second,
    head_modulate,
    head_modulate_first,
    head_modulate_second,
):
    role = lax.axis_index("role")
    mp_index = lax.axis_index("mp")
    shards = (
        attention_in[0].transpose(1, 0, 2),
        attention_out[0].T,
        feedforward_in[0],
        feedforward_out[0].T,
        block_affine[0],
        head_square.transpose(0, 2, 1),
        head_entry.T,
        head_modulate.T,
    )
    blocks, squares_all, entry_all, modulate_all, extras, *rows = gather_weights(
        shards,
        (
            patch_embed,
            latents.transpose(0, 2, 1),
            noise_draws.transpose(0, 2, 1),
            kept_signal(timesteps),
            buckets.T,
            visible_index,
            position_table(),
            time_tables(),
        ),
    )
    (
        embedded, embedded_own, enc_keys, enc_ids, dec_rows, dec_rows_own, dec_keys, dec_ids,
        noisy_input, features, noise_rows, valid, enc_left, enc_left_own, enc_inverse, dec_inverse,
    ) = rows
    blocks = blocks.reshape(2, 4, D, BLOCK_COLS)
    tables = (
        entry_all.reshape(W, SEQ),
        squares_all.reshape(3, W, W),
        modulate_all.reshape(5 * W, W),
        extras.reshape(W, 128),
    )
    role_array = jnp.reshape(role, (1,)).astype(jnp.int32)
    encoded, enc_kept = block_forward(
        embedded, enc_inverse, embedded_own, enc_keys, enc_ids, blocks, 0
    )
    parity = mp_index % 2
    other = send(encoded, neighbour_pairs())
    pair = jnp.where(parity == 0, jnp.stack([encoded, other]), jnp.stack([other, encoded]))
    across = send(pair, partner_pairs())
    received = jnp.where(role == 0, jnp.stack([pair, across], 1), jnp.stack([across, pair], 1))
    received = received.reshape(VCAP, D).astype(WIDE_TYPE)
    dec_rows = dec_rows.at[MCAP:].add(received)
    condition, dec_kept = block_forward(
        dec_rows, dec_inverse, dec_rows_own, dec_keys, dec_ids, blocks, 1
    )
    loss_local, head_grads, extra_grad, decoded_grad = head_step(
        condition, noisy_input, features, noise_rows, valid, tables, role_array
    )
    extra_grad = extra_grad.reshape(2, 4, 4, 4, 8, 128)
    visible_grad, dec_grads, dec_small = block_backward(
        decoded_grad, dec_kept, blocks, 1, role_array, enc_left, enc_left_own
    )
    visible_grad = visible_grad.reshape(2, 2, VQ, D)
    summed = pick(visible_grad, role, 1) + send(pick(visible_grad, 1 - role, 1), partner_pairs())
    came = send(pick(summed, 1 - parity, 0).astype(LOW_TYPE), neighbour_pairs())
    returned = pick(summed, parity, 0) + came.astype(WIDE_TYPE)
    returned = returned.astype(LOW_TYPE).astype(WIDE_TYPE)
    _, enc_grads, enc_small = block_backward(
        returned, enc_kept, blocks, 0, role_array, enc_left, enc_left_own
    )
    pairs = enc_grads + dec_grads + head_grads
    *sums, square_total = reduce_gradients(
        [pair[0] for pair in pairs],
        [pair[1] for pair in pairs],
        extra_grad,
        enc_small,
        dec_small,
        loss_local,
    )

    def flat(arrays):
        patch, joint, branch, up, down, affine, entry, square, modulate = arrays
        return (
            patch,
            joint[0].transpose(1, 0, 2),
            branch[0].T,
            up[0],
            down[0].T,
            affine.transpose(1, 0, 2),
            entry.T,
            square.transpose(0, 2, 1),
            modulate.T,
        )

    def restored(arrays):
        patch, joint, branch, up, down, affine, entry, square, modulate = arrays
        return (
            patch,
            joint.transpose(1, 0, 2)[None],
            branch.T[None],
            up[None],
            down.T[None],
            affine.transpose(1, 0, 2),
            entry.T,
            square.transpose(0, 2, 1),
            modulate.T,
        )

    params = (
        patch_embed,
        attention_in,
        attention_out,
        feedforward_in,
        feedforward_out,
        block_affine,
        head_entry,
        head_square,
        head_modulate,
    )
    firsts = (
        patch_embed_first,
        attention_in_first,
        attention_out_first,
        feedforward_in_first,
        feedforward_out_first,
        block_affine_first,
        head_entry_first,
        head_square_first,
        head_modulate_first,
    )
    seconds = (
        patch_embed_second,
        attention_in_second,
        attention_out_second,
        feedforward_in_second,
        feedforward_out_second,
        block_affine_second,
        head_entry_second,
        head_square_second,
        head_modulate_second,
    )
    *updated, loss_total, grad_norm = adam_all(
        (*sums, square_total), flat(params), flat(firsts), flat(seconds)
    )
    loss_total, grad_norm = loss_total[0, 0], grad_norm[0, 0]
    updated = [restored(updated[part::3]) for part in range(3)]
    news = [updated[part][index] for index in range(9) for part in range(3)]
    return (
        loss_total,
        grad_norm,
        news[0],
        news[1],
        news[2],
        news[3],
        news[4],
        news[5],
        news[6],
        news[7],
        news[8],
        news[9],
        news[10],
        news[11],
        news[12],
        news[13],
        news[14],
        news[15],
        news[16],
        news[17],
        news[18],
        news[19],
        news[20],
        news[21],
        news[22],
        news[23],
        news[24],
        news[25],
        news[26],
    )


def solution(mesh):
    placed = (
        P(None, "dp", None),
        P(None, "dp", None),
        P(None, "dp"),
        P(None, "dp"),
        P(None, "dp"),
        P(),
        P(),
        P(),
        P("role", "dp", "mp", None),
        P("role", "dp", "mp", None),
        P("role", "dp", "mp", None),
        P("role", "mp", "dp"),
        P("role", "mp", "dp"),
        P("role", "mp", "dp"),
        P("role", "dp", "mp"),
        P("role", "dp", "mp"),
        P("role", "dp", "mp"),
        P("role", "mp", "dp"),
        P("role", "mp", "dp"),
        P("role", "mp", "dp"),
        P("role", None, "dp"),
        P("role", None, "dp"),
        P("role", None, "dp"),
        P(None, ("role", "dp", "mp")),
        P(None, ("role", "dp", "mp")),
        P(None, ("role", "dp", "mp")),
        P(None, None, ("role", "dp", "mp")),
        P(None, None, ("role", "dp", "mp")),
        P(None, None, ("role", "dp", "mp")),
        P(None, ("role", "dp", "mp")),
        P(None, ("role", "dp", "mp")),
        P(None, ("role", "dp", "mp")),
    )
    return jax.shard_map(
        per_device,
        mesh=mesh,
        in_specs=placed,
        out_specs=(
            P(),
            P(),
            P(),
            P(),
            P(),
            P("role", "dp", "mp", None),
            P("role", "dp", "mp", None),
            P("role", "dp", "mp", None),
            P("role", "mp", "dp"),
            P("role", "mp", "dp"),
            P("role", "mp", "dp"),
            P("role", "dp", "mp"),
            P("role", "dp", "mp"),
            P("role", "dp", "mp"),
            P("role", "mp", "dp"),
            P("role", "mp", "dp"),
            P("role", "mp", "dp"),
            P("role", None, "dp"),
            P("role", None, "dp"),
            P("role", None, "dp"),
            P(None, ("role", "dp", "mp")),
            P(None, ("role", "dp", "mp")),
            P(None, ("role", "dp", "mp")),
            P(None, None, ("role", "dp", "mp")),
            P(None, None, ("role", "dp", "mp")),
            P(None, None, ("role", "dp", "mp")),
            P(None, ("role", "dp", "mp")),
            P(None, ("role", "dp", "mp")),
            P(None, ("role", "dp", "mp")),
        ),
        check_vma=False,
    )
```

```python
import functools
import math

import jax
import jax.numpy as jnp
from jax import lax
from jax.experimental import pallas as pl
from jax.experimental.pallas import tpu as pltpu
from jax.sharding import PartitionSpec as P

D = 768
HD = 64
C = 16
FREQ = 256
GRID = 32
STEP = 5
SEQ = 1024
VCAP = 320
MCAP = 864


LN_EPS = 1e-06
BETA_ONE = 0.9
BETA_TWO = 0.95
ADAM_EPS = 1e-08
DECAY = 0.02
RATE = 0.02
CLIP_NORM = 0.02
BUCKET_SHARE = (0.6, 0.4)
COSINE_OFFSET = 0.008
HORIZON = 1000.0
LOW_TYPE = jnp.bfloat16
WIDE_TYPE = jnp.float32


def matmul_low(left_side, right_side):
    return jnp.dot(left_side, right_side, preferred_element_type=WIDE_TYPE)


def matmul_high(left_side, right_side):
    return jnp.dot(left_side, right_side, precision=lax.Precision.HIGHEST)


def inner_rows(left_side, right_side):
    return lax.dot_general(
        left_side, right_side, (((0,), (0,)), ((), ())), preferred_element_type=WIDE_TYPE
    )


def outer_rows(left_side, right_side):
    return lax.dot_general(
        left_side, right_side, (((1,), (1,)), ((), ())), preferred_element_type=WIDE_TYPE
    )


def plain_forward(values):
    centered = values - jnp.mean(values, axis=-1, keepdims=True)
    spread = jnp.mean(centered * centered, axis=-1, keepdims=True)
    inverse = lax.rsqrt(spread + LN_EPS)
    scaled = centered * inverse
    return (scaled, (scaled, inverse))


def plain_backward(upstream, saved_norm):
    scaled, inverse = saved_norm
    return inverse * (
        upstream
        - jnp.mean(upstream, axis=-1, keepdims=True)
        - scaled * jnp.mean(upstream * scaled, axis=-1, keepdims=True)
    )


def silu_slope(values):
    sigmoid = jax.nn.sigmoid(values)
    return sigmoid * (1.0 + values * (1.0 - sigmoid))


QUARTER = 4
HE = 1067
MQ = MCAP // QUARTER
VQ = VCAP // QUARTER
HEADS = 12
FF = 3072
W = 1024
ALL = ("role", "dp", "mp")
SCALE = HD ** (-0.5)


def device_order():
    return [(r, x, z, y) for r in range(2) for x in range(4) for z in range(4) for y in range(4)]


def flat_index(r, x, z, y):
    return r * 64 + x * 16 + z * 4 + y


def partner_pairs():
    return [(flat_index(r, x, z, y), flat_index(1 - r, x, z, y)) for r, x, z, y in device_order()]


def neighbour_pairs():
    return [(flat_index(r, x, z, y), flat_index(r, x, z, y ^ 1)) for r, x, z, y in device_order()]


def send(value, pairs):
    return lax.ppermute(value, ALL, pairs)


def pick(value, index, dim):
    return lax.dynamic_index_in_dim(value, index, dim, keepdims=False)


ORDERS = ((1, 2, 3), (2, 3, 1), (3, 1, 2))


def block_position(places, wide_image, table):
    local = jnp.where(wide_image, places, places & 255)
    shift = jnp.where(wide_image, 5, 4)
    rows = lax.shift_right_logical(local, jnp.broadcast_to(shift, local.shape))
    cols = local & jnp.where(wide_image, 31, 15)
    grid = lax.broadcasted_iota(jnp.int32, (places.shape[0], GRID), 1)
    pair = [(side == grid).astype(WIDE_TYPE) for side in (rows, cols)]
    return jnp.concatenate([matmul_high(side, table) for side in pair], axis=1)


def as_row(column):
    return jnp.broadcast_to(column, (column.shape[0], 128)).T[0:1]


def pack_shards(ins, packed):
    joint, branch, up, down, affine, square, entry, modulate = ins
    block, squares, entry_out, modulate_out, extra = packed
    heads = [joint[head] for head in range(3)]

    def kind(index):
        return [head[:, HD * index : HD * (index + 1)] for head in heads]

    block[:, :768] = jnp.concatenate(kind(1) + kind(2) + kind(0) + [branch[...]], axis=1).astype(
        LOW_TYPE
    )
    block[:, 768:1536] = up[...].astype(LOW_TYPE)
    block[:, 1536:2304] = down[...].astype(LOW_TYPE)
    affine_rows = jnp.concatenate([affine[...], jnp.zeros((122, 48), WIDE_TYPE)], axis=0)
    block[:, 2304:] = affine_rows.T.astype(LOW_TYPE)
    squares[...] = square[...].astype(LOW_TYPE)
    entry_out[...] = entry[:, :SEQ].astype(LOW_TYPE)
    modulate_out[...] = modulate[...].astype(LOW_TYPE)
    tail = jnp.concatenate([entry[:, SEQ:], jnp.zeros((8, 85), WIDE_TYPE)], axis=1)
    return tail


def count_codes(buckets, visible):
    lane = lax.broadcasted_iota(jnp.int32, (1, 128), 1)
    row = jnp.zeros((1, 128), WIDE_TYPE)
    for slot in range(2):
        hidden = (visible[slot : slot + 1] >= SEQ).astype(WIDE_TYPE)
        masked = SEQ - VCAP + jnp.sum(hidden, axis=1, keepdims=True)
        high = jnp.floor(masked * (1.0 / 32.0))
        bucket = buckets[0:1, slot : slot + 1].astype(WIDE_TYPE)
        for index, value in enumerate((high, masked - 32.0 * high, bucket)):
            row = row + jnp.where(lane == 64 + 2 * index + slot, value, 0.0)
    return row


def prepare_rows(ins, outs, column_ref):
    patch, latents, noise, signal, buckets, visible, table, trig = ins
    (
        embedded_out, embedded_own_out, enc_keys_out, enc_ids_out, rows_out, rows_own_out,
        dec_keys_out, dec_ids_out, noisy_out, features_out, noise_out, valid_out, left_out,
        left_own_out, enc_inverse_out, dec_inverse_out,
    ) = outs
    role, mp_index = lax.axis_index("role"), lax.axis_index("mp")
    slot = lax.div(mp_index, 2)
    quarter = lax.rem(mp_index, 2) * 2 + role
    first = slot == 0
    wide_image = jnp.where(first, buckets[0:1, 0:1], buckets[0:1, 1:2]) == 1
    table = table[...]
    spare = jnp.zeros((5, SEQ), WIDE_TYPE)
    slot_facts = jnp.concatenate([latents[slot], noise[slot], signal[slot], spare], axis=0)
    shown_row = jnp.where(first, visible[0:1], visible[1:2]).astype(WIDE_TYPE)
    column_ref[...] = jnp.broadcast_to(shown_row, (128, VCAP)).T
    shown_col = column_ref[:, 0:1].astype(jnp.int32)
    lanes = lax.broadcasted_iota(jnp.int32, (1, SEQ), 1)

    def ids_of(places):
        return jnp.where(wide_image, 0, lax.shift_right_logical(places, jnp.full_like(places, 8)))

    def encoder_rows(column):
        places = jnp.minimum(column, SEQ - 1)
        chosen = (places == lanes).astype(WIDE_TYPE)
        picked = lax.dot_general(
            chosen, slot_facts, (((1,), (1,)), ((), ())), precision=lax.Precision.HIGHEST
        )
        place = block_position(places, wide_image, table)
        rows = matmul_high(picked[:, :C], patch[0:C]) + patch[C : C + 1] + place
        ones = jnp.ones((column.shape[0], 1), WIDE_TYPE)
        zeros = jnp.zeros((column.shape[0], 7), WIDE_TYPE)
        return rows, place, ids_of(places), jnp.concatenate([picked[:, :C], ones, zeros], axis=1)

    rows, place, ids, left = encoder_rows(shown_col)
    embedded_out[...], enc_inverse_out[...] = plain_rows(rows)
    left_out[...] = left
    visible_keys = jnp.where(shown_col < SEQ, ids, -1).astype(WIDE_TYPE)
    enc_keys_out[...] = visible_keys
    own_col = column_ref[pl.ds(pl.multiple_of(quarter * VQ, 8), VQ), 0:1].astype(jnp.int32)
    rows, _, ids, left = encoder_rows(own_col)
    embedded_own_out[...] = rows
    left_own_out[...] = left
    enc_ids_out[...] = as_row(ids.astype(WIDE_TYPE))

    shown = jnp.max((shown_col == lanes).astype(WIDE_TYPE), axis=0, keepdims=True)
    masked = 1.0 - shown
    low = lax.broadcasted_iota(jnp.int32, (SEQ, SEQ), 0)
    high = lax.broadcasted_iota(jnp.int32, (SEQ, SEQ), 1)
    before = (low <= high).astype(LOW_TYPE)
    rank = matmul_low(jnp.broadcast_to(masked, (16, SEQ)).astype(LOW_TYPE), before)[0:1] - 1.0
    rank = jnp.where(masked > 0.0, rank, -1.0)
    total = jnp.sum(masked, axis=1, keepdims=True)

    def masked_rows(index):
        valid = index < total
        wanted = jnp.where(valid, index, -2.0)
        hit = jnp.where(valid, (rank == wanted).astype(WIDE_TYPE), (lanes == SEQ - 1).astype(WIDE_TYPE))
        places = jnp.sum(hit * lanes.astype(WIDE_TYPE), axis=1, keepdims=True).astype(jnp.int32)
        return hit, valid, places, patch[C + 1 : C + 2] + block_position(places, wide_image, table)

    index = lax.broadcasted_iota(jnp.int32, (MCAP, 1), 0).astype(WIDE_TYPE)
    _, valid, places, rows = masked_rows(index)
    rows_out[0:MCAP], dec_inverse_out[...] = plain_rows(rows)
    rows_out[MCAP:] = place
    dec_keys_out[0:MCAP] = jnp.where(valid, ids_of(places), -1).astype(WIDE_TYPE)
    dec_keys_out[MCAP:] = visible_keys
    inner = lax.broadcasted_iota(jnp.int32, (MQP, 1), 0)
    index = jnp.where(inner < MQ, inner + quarter * MQ, MCAP).astype(WIDE_TYPE)
    hit, valid, places, rows = masked_rows(index)
    rows_own_out[...] = rows
    ids = jnp.where(inner < MQ, ids_of(places), -2).astype(WIDE_TYPE)
    dec_ids_out[...] = as_row(ids)
    valid_out[...] = valid.astype(WIDE_TYPE)
    picked = lax.dot_general(
        hit, slot_facts, (((1,), (1,)), ((), ())), precision=lax.Precision.HIGHEST
    )
    noise_rows = picked[:, C : 2 * C]
    noise_out[...] = noise_rows
    noisy_out[...] = (picked[:, 33:34] * picked[:, :C] + picked[:, 34:35] * noise_rows).astype(
        LOW_TYPE
    )
    time = picked[:, 32:33].astype(jnp.int32)
    grid = lax.broadcasted_iota(jnp.int32, (MQP, GRID), 1)
    coarse = (lax.shift_right_logical(time, jnp.full_like(time, 5)) == grid).astype(WIDE_TYPE)
    fine = ((time & 31) == grid).astype(WIDE_TYPE)
    coarse = matmul_high(coarse, trig[:, :256])
    fine = matmul_high(fine, trig[:, 256:])
    cos_a, sin_a, cos_b, sin_b = coarse[:, :128], coarse[:, 128:], fine[:, :128], fine[:, 128:]
    features_out[:, :128] = (cos_a * cos_b - sin_a * sin_b).astype(LOW_TYPE)
    features_out[:, 128:] = (sin_a * cos_b + cos_a * sin_b).astype(LOW_TYPE)


BLOCK_COLS = 2432
PIECES = (
    ((0, 0, 0, BLOCK_COLS, 1280), (3, None, 0, 640, 384)),
    ((0, 16, 0, BLOCK_COLS, 1280), (3, None, 640, 384, 256), (2, None, 0, 1024, 512), (4, None, 0, 128, 128)),
    ((0, 32, 0, BLOCK_COLS, 1280), (1, None, 0, 1024, 512)),
)
GATHER_COPIES = 8 + 3 * 8 * 8


def mesh_place():
    dp_index = lax.axis_index("dp")
    role, mp_index = lax.axis_index("role"), lax.axis_index("mp")
    return (role, dp_index // 4, lax.rem(dp_index, 4), mp_index)


def mesh_device(place):
    return (place[0], place[1] * 4 + place[2], place[3])


def moved(place, axis, steps):
    target = list(place)
    count = 2 if axis == 0 else 4
    target[axis] = lax.rem(target[axis] + steps + count, count)
    return tuple(target)


def greet(place, moves):
    barrier = pltpu.get_barrier_semaphore()
    for axis, steps in moves:
        pl.semaphore_signal(
            barrier,
            inc=1,
            device_id=mesh_device(moved(place, axis, steps)),
            device_id_type=pl.DeviceIdType.MESH,
        )
    pl.semaphore_wait(barrier, len(moves))


RING_MOVES = ((0, 1), (1, 1), (1, -1), (2, 1), (2, -1), (3, 1), (3, -1))


def gather_region(outs, piece, spans, half):
    kind, row, column, width, cut = piece
    if half is not None:
        column, width = (column, cut) if half == 0 else (column + cut, width - cut)
    r = spans[0]
    x, z, y = (slice(None) if spans[axis] is None else spans[axis] for axis in (1, 2, 3))
    columns = pl.ds(column, width)
    if kind == 0:
        return outs[0].at[r, y, x, z, pl.ds(row, 16), columns]
    if kind == 1:
        return outs[1].at[:, r, x, z, y, :, columns]
    return outs[kind].at[r, x, z, y, :, columns]


LATE_COPIES = 40
LATE_STEPS = ("first", "second", "cross_first", "cross_second")


def late_copies(outs, send_sems, recv_sems, wanted):
    place = mesh_place()
    slot, copies = 0, []
    for step in LATE_STEPS:
        for third in range(3):
            axis = ORDERS[third][2]
            for which, steps in ((0, 1), (1, -1)):
                spans = {other: None for other in (1, 2, 3)}
                spans[0] = place[0]
                if step == "first":
                    spans[axis], half = place[axis], None
                elif step == "cross_second":
                    spans[axis], half = lax.rem(place[axis] + 2, 4), which
                else:
                    spans[axis] = lax.rem(place[axis] - steps + 4, 4)
                    half = which if step == "second" else None
                target = moved(place, *((axis, steps) if step in LATE_STEPS[:2] else (0, 1)))
                batch = []
                for piece in PIECES[third]:
                    if piece[0] == 0 or (half == 1 and piece[3] == piece[4]):
                        continue
                    if step == wanted:
                        ref = gather_region(outs, piece, spans, half)
                        batch.append(
                            pltpu.make_async_remote_copy(
                                src_ref=ref,
                                dst_ref=ref,
                                send_sem=send_sems.at[slot],
                                recv_sem=recv_sems.at[slot],
                                device_id=mesh_device(target),
                                device_id_type=pl.DeviceIdType.MESH,
                            )
                        )
                    slot += 1
                copies.append(batch)
    return [batch for batch in copies if batch]


def gather_kernel(*refs):
    shard_ins, row_ins, outs, row_outs = refs[:8], refs[8:16], refs[16:21], refs[21:37]
    packed, column_ref, (send_sems, recv_sems, local_sems) = refs[37:42], refs[42], refs[43:]
    ins = packed
    extra_row = count_codes(row_ins[4], row_ins[5])
    first_row = lax.broadcasted_iota(jnp.int32, (8, 128), 0) == 0
    tail = pack_shards(shard_ins, packed)
    packed[4][...] = (tail + jnp.where(first_row, extra_row, 0.0)).astype(LOW_TYPE)
    place = mesh_place()
    used = [0]

    def region(piece, spans, half):
        return gather_region(outs, piece, spans, half)

    def start(unit, spans, half, axis, steps):
        copies = []
        for piece in PIECES[unit[0]]:
            if (piece[0] > 0) != unit[1] or (half == 1 and piece[3] == piece[4]):
                continue
            ref = region(piece, spans, half)
            slot = used[0]
            used[0] += 1
            copy = pltpu.make_async_remote_copy(
                src_ref=ref,
                dst_ref=ref,
                send_sem=send_sems.at[slot],
                recv_sem=recv_sems.at[slot],
                device_id=mesh_device(moved(place, axis, steps)),
                device_id_type=pl.DeviceIdType.MESH,
            )
            copy.start()
            copies.append(copy)
        return copies

    r, x, z, y = place
    own = {0: r, 1: x, 2: z, 3: y}
    targets = (
        outs[0].at[r, y, x, z], outs[1].at[:, r, x, z, y], outs[2].at[r, x, z, y],
        outs[3].at[r, x, z, y], outs[4].at[r, x, z, y],
    )
    placed = [
        pltpu.make_async_copy(source, target, local_sems.at[index])
        for index, (source, target) in enumerate(zip(ins, targets))
    ]
    for copy in placed:
        copy.start()
    greet(place, RING_MOVES)
    for copy in placed:
        copy.wait()
    pending, leaving = [], []
    units = [(third, stream) for stream in (0, 1) for third in range(3)]
    spans = {unit: dict(own) for unit in units}
    first, second = {}, {}

    def step_one(unit, stage):
        axis = ORDERS[unit[0]][stage]
        first[unit] = [start(unit, spans[unit], None, axis, steps) for steps in (1, -1)]

    for unit in units:
        step_one(unit, 0)
    for unit in units:
        pending += start(unit, spans[unit], None, 0, 1)
    for stage in range(3):
        if stage == 2:
            units = units[:3]
            prepare_rows(row_ins, row_outs, column_ref)
        for unit in units:
            axis = ORDERS[unit[0]][stage]
            batch = []
            for which, steps in ((0, 1), (1, -1)):
                came = dict(spans[unit])
                came[axis] = lax.rem(own[axis] - steps + 4, 4)
                for copy in first[unit][which]:
                    copy.wait_recv()
                batch.append(start(unit, came, which, axis, steps))
                pending += start(unit, came, None, 0, 1)
            second[unit] = batch
        for unit in units:
            axis = ORDERS[unit[0]][stage]
            came = dict(spans[unit])
            came[axis] = lax.rem(own[axis] + 2, 4)
            for which in (0, 1):
                for copy in second[unit][which]:
                    copy.wait_recv()
                pending += start(unit, came, which, 0, 1)
            for copies in first[unit] + second[unit]:
                leaving += copies
            spans[unit][axis] = None
            if stage + unit[1] < 2:
                step_one(unit, stage + 1)
    for copy in leaving:
        copy.wait_send()
    for copy in pending:
        copy.wait()


def gather_weights(shards, rows):
    whole_torus = (2, 4, 4, 4)
    held = pl.BlockSpec(memory_space=pltpu.VMEM)
    return pl.pallas_call(
        gather_kernel,
        out_shape=(
            narrow(*whole_torus, 48, BLOCK_COLS),
            narrow(3, *whole_torus, 8, W),
            narrow(*whole_torus, 8, W),
            narrow(*whole_torus, 40, W),
            narrow(*whole_torus, 8, 128),
            wide(VCAP, D), wide(VQ, D), wide(VCAP, 1), wide(1, VQ),
            wide(MCAP + VCAP, D), wide(MQP, D), wide(MCAP + VCAP, 1), wide(1, MQP),
            narrow(MQP, C), narrow(MQP, FREQ), wide(MQP, C), wide(MQP, 1),
            wide(VCAP, 24), wide(VQ, 24), wide(VCAP, 1), wide(MCAP, 1),
        ),
        in_specs=[held] * 16,
        out_specs=(pl.BlockSpec(memory_space=pl.ANY),) * 5 + (held,) * 16,
        scratch_shapes=[
            pltpu.VMEM((48, BLOCK_COLS), LOW_TYPE),
            pltpu.VMEM((3, 8, W), LOW_TYPE),
            pltpu.VMEM((8, W), LOW_TYPE),
            pltpu.VMEM((40, W), LOW_TYPE),
            pltpu.VMEM((8, 128), LOW_TYPE),
            pltpu.VMEM((VCAP, 128), WIDE_TYPE),
            pltpu.SemaphoreType.DMA((GATHER_COPIES,)),
            pltpu.SemaphoreType.DMA((GATHER_COPIES,)),
            pltpu.SemaphoreType.DMA((5,)),
        ],
        compiler_params=pltpu.CompilerParams(
            collective_id=0, has_side_effects=True, vmem_limit_bytes=VMEM_BYTES
        ),
        name="gather_weights",
    )(*shards, *rows)


SUM_MOVES = ((0, 1),) + tuple((axis, steps) for axis in (1, 2, 3) for steps in (1, 2, 3))


def position_table():
    frequency = 1.0 / 10000.0 ** (jnp.arange(D // 4, dtype=WIDE_TYPE) / (D // 4))
    angle = jnp.arange(GRID, dtype=WIDE_TYPE)[:, None] * frequency[None, :]
    return jnp.concatenate([jnp.sin(angle), jnp.cos(angle)], axis=1)


def time_tables():
    half_width = FREQ // 2
    frequency = jnp.exp(-math.log(10000.0) * jnp.arange(half_width, dtype=WIDE_TYPE) / half_width)
    fine = jnp.arange(32, dtype=WIDE_TYPE)[:, None] * frequency[None, :]
    angles = (32.0 * fine, fine)
    return jnp.concatenate([part(angle) for angle in angles for part in (jnp.cos, jnp.sin)], axis=1)


def kept_signal(timesteps):
    times_f = (timesteps + 1).astype(WIDE_TYPE)
    half_turn = math.pi / 2
    angle_now = (times_f / HORIZON + COSINE_OFFSET) / (1.0 + COSINE_OFFSET) * half_turn
    start_cos = math.cos(COSINE_OFFSET / (1.0 + COSINE_OFFSET) * half_turn)
    signal_kept = (jnp.cos(angle_now) / start_cos) ** 2
    return jnp.stack([times_f, jnp.sqrt(signal_kept), jnp.sqrt(1.0 - signal_kept)], axis=1)


def block_position(places, wide_image, table):
    local = jnp.where(wide_image, places, places & 255)
    shift = jnp.where(wide_image, 5, 4)
    rows = lax.shift_right_logical(local, jnp.broadcast_to(shift, local.shape))
    cols = local & jnp.where(wide_image, 31, 15)
    grid = lax.broadcasted_iota(jnp.int32, (places.shape[0], GRID), 1)
    pair = [(side == grid).astype(WIDE_TYPE) for side in (rows, cols)]
    return jnp.concatenate([matmul_high(side, table) for side in pair], axis=1)


def as_row(column):
    return jnp.broadcast_to(column, (column.shape[0], 128)).T[0:1]


def pack_shards(ins, packed):
    joint, branch, up, down, affine, square, entry, modulate = ins
    block, squares, entry_out, modulate_out, extra = packed
    heads = [joint[head] for head in range(3)]

    def kind(index):
        return [head[:, HD * index : HD * (index + 1)] for head in heads]

    block[:, :768] = jnp.concatenate(kind(1) + kind(2) + kind(0) + [branch[...]], axis=1).astype(
        LOW_TYPE
    )
    block[:, 768:1536] = up[...].astype(LOW_TYPE)
    block[:, 1536:2304] = down[...].astype(LOW_TYPE)
    affine_rows = jnp.concatenate([affine[...], jnp.zeros((122, 48), WIDE_TYPE)], axis=0)
    block[:, 2304:] = affine_rows.T.astype(LOW_TYPE)
    squares[...] = square[...].astype(LOW_TYPE)
    entry_out[...] = entry[:, :SEQ].astype(LOW_TYPE)
    modulate_out[...] = modulate[...].astype(LOW_TYPE)
    tail = jnp.concatenate([entry[:, SEQ:], jnp.zeros((8, 85), WIDE_TYPE)], axis=1)
    return tail


def count_codes(buckets, visible):
    lane = lax.broadcasted_iota(jnp.int32, (1, 128), 1)
    row = jnp.zeros((1, 128), WIDE_TYPE)
    for slot in range(2):
        hidden = (visible[slot : slot + 1] >= SEQ).astype(WIDE_TYPE)
        masked = SEQ - VCAP + jnp.sum(hidden, axis=1, keepdims=True)
        high = jnp.floor(masked * (1.0 / 32.0))
        bucket = buckets[0:1, slot : slot + 1].astype(WIDE_TYPE)
        for index, value in enumerate((high, masked - 32.0 * high, bucket)):
            row = row + jnp.where(lane == 64 + 2 * index + slot, value, 0.0)
    return row


def prepare_rows(ins, outs, column_ref):
    patch, latents, noise, signal, buckets, visible, table, trig = ins
    (
        embedded_out, embedded_own_out, enc_keys_out, enc_ids_out, rows_out, rows_own_out,
        dec_keys_out, dec_ids_out, noisy_out, features_out, noise_out, valid_out, left_out,
        left_own_out, enc_inverse_out, dec_inverse_out,
    ) = outs
    role, mp_index = lax.axis_index("role"), lax.axis_index("mp")
    slot = lax.div(mp_index, 2)
    quarter = lax.rem(mp_index, 2) * 2 + role
    first = slot == 0
    wide_image = jnp.where(first, buckets[0:1, 0:1], buckets[0:1, 1:2]) == 1
    table = table[...]
    spare = jnp.zeros((5, SEQ), WIDE_TYPE)
    slot_facts = jnp.concatenate([latents[slot], noise[slot], signal[slot], spare], axis=0)
    shown_row = jnp.where(first, visible[0:1], visible[1:2]).astype(WIDE_TYPE)
    column_ref[...] = jnp.broadcast_to(shown_row, (128, VCAP)).T
    shown_col = column_ref[:, 0:1].astype(jnp.int32)
    lanes = lax.broadcasted_iota(jnp.int32, (1, SEQ), 1)

    def ids_of(places):
        return jnp.where(wide_image, 0, lax.shift_right_logical(places, jnp.full_like(places, 8)))

    def encoder_rows(column):
        places = jnp.minimum(column, SEQ - 1)
        chosen = (places == lanes).astype(WIDE_TYPE)
        picked = lax.dot_general(
            chosen, slot_facts, (((1,), (1,)), ((), ())), precision=lax.Precision.HIGHEST
        )
        place = block_position(places, wide_image, table)
        rows = matmul_high(picked[:, :C], patch[0:C]) + patch[C : C + 1] + place
        ones = jnp.ones((column.shape[0], 1), WIDE_TYPE)
        zeros = jnp.zeros((column.shape[0], 7), WIDE_TYPE)
        return rows, place, ids_of(places), jnp.concatenate([picked[:, :C], ones, zeros], axis=1)

    rows, place, ids, left = encoder_rows(shown_col)
    embedded_out[...], enc_inverse_out[...] = plain_rows(rows)
    left_out[...] = left
    visible_keys = jnp.where(shown_col < SEQ, ids, -1).astype(WIDE_TYPE)
    enc_keys_out[...] = visible_keys
    own_col = column_ref[pl.ds(pl.multiple_of(quarter * VQ, 8), VQ), 0:1].astype(jnp.int32)
    rows, _, ids, left = encoder_rows(own_col)
    embedded_own_out[...] = rows
    left_own_out[...] = left
    enc_ids_out[...] = as_row(ids.astype(WIDE_TYPE))

    shown = jnp.max((shown_col == lanes).astype(WIDE_TYPE), axis=0, keepdims=True)
    masked = 1.0 - shown
    low = lax.broadcasted_iota(jnp.int32, (SEQ, SEQ), 0)
    high = lax.broadcasted_iota(jnp.int32, (SEQ, SEQ), 1)
    before = (low <= high).astype(LOW_TYPE)
    rank = matmul_low(jnp.broadcast_to(masked, (16, SEQ)).astype(LOW_TYPE), before)[0:1] - 1.0
    rank = jnp.where(masked > 0.0, rank, -1.0)
    total = jnp.sum(masked, axis=1, keepdims=True)

    def masked_rows(index):
        valid = index < total
        wanted = jnp.where(valid, index, -2.0)
        hit = jnp.where(valid, (rank == wanted).astype(WIDE_TYPE), (lanes == SEQ - 1).astype(WIDE_TYPE))
        places = jnp.sum(hit * lanes.astype(WIDE_TYPE), axis=1, keepdims=True).astype(jnp.int32)
        return hit, valid, places, patch[C + 1 : C + 2] + block_position(places, wide_image, table)

    index = lax.broadcasted_iota(jnp.int32, (MCAP, 1), 0).astype(WIDE_TYPE)
    _, valid, places, rows = masked_rows(index)
    rows_out[0:MCAP], dec_inverse_out[...] = plain_rows(rows)
    rows_out[MCAP:] = place
    dec_keys_out[0:MCAP] = jnp.where(valid, ids_of(places), -1).astype(WIDE_TYPE)
    dec_keys_out[MCAP:] = visible_keys
    inner = lax.broadcasted_iota(jnp.int32, (MQP, 1), 0)
    index = jnp.where(inner < MQ, inner + quarter * MQ, MCAP).astype(WIDE_TYPE)
    hit, valid, places, rows = masked_rows(index)
    rows_own_out[...] = rows
    ids = jnp.where(inner < MQ, ids_of(places), -2).astype(WIDE_TYPE)
    dec_ids_out[...] = as_row(ids)
    valid_out[...] = valid.astype(WIDE_TYPE)
    picked = lax.dot_general(
        hit, slot_facts, (((1,), (1,)), ((), ())), precision=lax.Precision.HIGHEST
    )
    noise_rows = picked[:, C : 2 * C]
    noise_out[...] = noise_rows
    noisy_out[...] = (picked[:, 33:34] * picked[:, :C] + picked[:, 34:35] * noise_rows).astype(
        LOW_TYPE
    )
    time = picked[:, 32:33].astype(jnp.int32)
    grid = lax.broadcasted_iota(jnp.int32, (MQP, GRID), 1)
    coarse = (lax.shift_right_logical(time, jnp.full_like(time, 5)) == grid).astype(WIDE_TYPE)
    fine = ((time & 31) == grid).astype(WIDE_TYPE)
    coarse = matmul_high(coarse, trig[:, :256])
    fine = matmul_high(fine, trig[:, 256:])
    cos_a, sin_a, cos_b, sin_b = coarse[:, :128], coarse[:, 128:], fine[:, :128], fine[:, 128:]
    features_out[:, :128] = (cos_a * cos_b - sin_a * sin_b).astype(LOW_TYPE)
    features_out[:, 128:] = (sin_a * cos_b + cos_a * sin_b).astype(LOW_TYPE)


BLOCK_COLS = 2432
PIECES = (
    ((0, 0, 0, BLOCK_COLS, 1280), (3, None, 0, 640, 384)),
    ((0, 16, 0, BLOCK_COLS, 1280), (3, None, 640, 384, 256), (2, None, 0, 1024, 512), (4, None, 0, 128, 128)),
    ((0, 32, 0, BLOCK_COLS, 1280), (1, None, 0, 1024, 512)),
)
GATHER_COPIES = 8 + 3 * 8 * 8


def mesh_place():
    dp_index = lax.axis_index("dp")
    role, mp_index = lax.axis_index("role"), lax.axis_index("mp")
    return (role, dp_index // 4, lax.rem(dp_index, 4), mp_index)


def mesh_device(place):
    return (place[0], place[1] * 4 + place[2], place[3])


def moved(place, axis, steps):
    target = list(place)
    count = 2 if axis == 0 else 4
    target[axis] = lax.rem(target[axis] + steps + count, count)
    return tuple(target)


def greet(place, moves):
    barrier = pltpu.get_barrier_semaphore()
    for axis, steps in moves:
        pl.semaphore_signal(
            barrier,
            inc=1,
            device_id=mesh_device(moved(place, axis, steps)),
            device_id_type=pl.DeviceIdType.MESH,
        )
    pl.semaphore_wait(barrier, len(moves))


RING_MOVES = ((0, 1), (1, 1), (1, -1), (2, 1), (2, -1), (3, 1), (3, -1))


def gather_region(outs, piece, spans, half):
    kind, row, column, width, cut = piece
    if half is not None:
        column, width = (column, cut) if half == 0 else (column + cut, width - cut)
    r = spans[0]
    x, z, y = (slice(None) if spans[axis] is None else spans[axis] for axis in (1, 2, 3))
    columns = pl.ds(column, width)
    if kind == 0:
        return outs[0].at[r, y, x, z, pl.ds(row, 16), columns]
    if kind == 1:
        return outs[1].at[:, r, x, z, y, :, columns]
    return outs[kind].at[r, x, z, y, :, columns]


LATE_COPIES = 40
LATE_STEPS = ("first", "second", "cross_first", "cross_second")


def late_copies(outs, send_sems, recv_sems, wanted):
    place = mesh_place()
    slot, copies = 0, []
    for step in LATE_STEPS:
        for third in range(3):
            axis = ORDERS[third][2]
            for which, steps in ((0, 1), (1, -1)):
                spans = {other: None for other in (1, 2, 3)}
                spans[0] = place[0]
                if step == "first":
                    spans[axis], half = place[axis], None
                elif step == "cross_second":
                    spans[axis], half = lax.rem(place[axis] + 2, 4), which
                else:
                    spans[axis] = lax.rem(place[axis] - steps + 4, 4)
                    half = which if step == "second" else None
                target = moved(place, *((axis, steps) if step in LATE_STEPS[:2] else (0, 1)))
                batch = []
                for piece in PIECES[third]:
                    if piece[0] == 0 or (half == 1 and piece[3] == piece[4]):
                        continue
                    if step == wanted:
                        ref = gather_region(outs, piece, spans, half)
                        batch.append(
                            pltpu.make_async_remote_copy(
                                src_ref=ref,
                                dst_ref=ref,
                                send_sem=send_sems.at[slot],
                                recv_sem=recv_sems.at[slot],
                                device_id=mesh_device(target),
                                device_id_type=pl.DeviceIdType.MESH,
                            )
                        )
                    slot += 1
                copies.append(batch)
    return [batch for batch in copies if batch]


def gather_kernel(*refs):
    shard_ins, row_ins, outs, row_outs = refs[:8], refs[8:16], refs[16:21], refs[21:37]
    packed, column_ref, (send_sems, recv_sems, local_sems) = refs[37:42], refs[42], refs[43:]
    ins = packed
    extra_row = count_codes(row_ins[4], row_ins[5])
    first_row = lax.broadcasted_iota(jnp.int32, (8, 128), 0) == 0
    tail = pack_shards(shard_ins, packed)
    packed[4][...] = (tail + jnp.where(first_row, extra_row, 0.0)).astype(LOW_TYPE)
    place = mesh_place()
    used = [0]

    def region(piece, spans, half):
        return gather_region(outs, piece, spans, half)

    def start(unit, spans, half, axis, steps):
        copies = []
        for piece in PIECES[unit[0]]:
            if (piece[0] > 0) != unit[1] or (half == 1 and piece[3] == piece[4]):
                continue
            ref = region(piece, spans, half)
            slot = used[0]
            used[0] += 1
            copy = pltpu.make_async_remote_copy(
                src_ref=ref,
                dst_ref=ref,
                send_sem=send_sems.at[slot],
                recv_sem=recv_sems.at[slot],
                device_id=mesh_device(moved(place, axis, steps)),
                device_id_type=pl.DeviceIdType.MESH,
            )
            copy.start()
            copies.append(copy)
        return copies

    r, x, z, y = place
    own = {0: r, 1: x, 2: z, 3: y}
    targets = (
        outs[0].at[r, y, x, z], outs[1].at[:, r, x, z, y], outs[2].at[r, x, z, y],
        outs[3].at[r, x, z, y], outs[4].at[r, x, z, y],
    )
    placed = [
        pltpu.make_async_copy(source, target, local_sems.at[index])
        for index, (source, target) in enumerate(zip(ins, targets))
    ]
    for copy in placed:
        copy.start()
    greet(place, RING_MOVES)
    for copy in placed:
        copy.wait()
    pending, leaving = [], []
    units = [(third, stream) for stream in (0, 1) for third in range(3)]
    spans = {unit: dict(own) for unit in units}
    first, second = {}, {}

    def step_one(unit, stage):
        axis = ORDERS[unit[0]][stage]
        first[unit] = [start(unit, spans[unit], None, axis, steps) for steps in (1, -1)]

    for unit in units:
        step_one(unit, 0)
    for unit in units:
        pending += start(unit, spans[unit], None, 0, 1)
    for stage in range(3):
        if stage == 2:
            units = units[:3]
            prepare_rows(row_ins, row_outs, column_ref)
        for unit in units:
            axis = ORDERS[unit[0]][stage]
            batch = []
            for which, steps in ((0, 1), (1, -1)):
                came = dict(spans[unit])
                came[axis] = lax.rem(own[axis] - steps + 4, 4)
                for copy in first[unit][which]:
                    copy.wait_recv()
                batch.append(start(unit, came, which, axis, steps))
                pending += start(unit, came, None, 0, 1)
            second[unit] = batch
        for unit in units:
            axis = ORDERS[unit[0]][stage]
            came = dict(spans[unit])
            came[axis] = lax.rem(own[axis] + 2, 4)
            for which in (0, 1):
                for copy in second[unit][which]:
                    copy.wait_recv()
                pending += start(unit, came, which, 0, 1)
            for copies in first[unit] + second[unit]:
                leaving += copies
            spans[unit][axis] = None
            if stage + unit[1] < 2:
                step_one(unit, stage + 1)
    for copy in leaving:
        copy.wait_send()
    for copy in pending:
        copy.wait()


def gather_weights(shards, rows):
    whole_torus = (2, 4, 4, 4)
    held = pl.BlockSpec(memory_space=pltpu.VMEM)
    return pl.pallas_call(
        gather_kernel,
        out_shape=(
            narrow(*whole_torus, 48, BLOCK_COLS),
            narrow(3, *whole_torus, 8, W),
            narrow(*whole_torus, 8, W),
            narrow(*whole_torus, 40, W),
            narrow(*whole_torus, 8, 128),
            wide(VCAP, D), wide(VQ, D), wide(VCAP, 1), wide(1, VQ),
            wide(MCAP + VCAP, D), wide(MQP, D), wide(MCAP + VCAP, 1), wide(1, MQP),
            narrow(MQP, C), narrow(MQP, FREQ), wide(MQP, C), wide(MQP, 1),
            wide(VCAP, 24), wide(VQ, 24), wide(VCAP, 1), wide(MCAP, 1),
        ),
        in_specs=[held] * 16,
        out_specs=(pl.BlockSpec(memory_space=pl.ANY),) * 5 + (held,) * 16,
        scratch_shapes=[
            pltpu.VMEM((48, BLOCK_COLS), LOW_TYPE),
            pltpu.VMEM((3, 8, W), LOW_TYPE),
            pltpu.VMEM((8, W), LOW_TYPE),
            pltpu.VMEM((40, W), LOW_TYPE),
            pltpu.VMEM((8, 128), LOW_TYPE),
            pltpu.VMEM((VCAP, 128), WIDE_TYPE),
            pltpu.SemaphoreType.DMA((GATHER_COPIES,)),
            pltpu.SemaphoreType.DMA((GATHER_COPIES,)),
            pltpu.SemaphoreType.DMA((5,)),
        ],
        compiler_params=pltpu.CompilerParams(
            collective_id=0, has_side_effects=True, vmem_limit_bytes=VMEM_BYTES
        ),
        name="gather_weights",
    )(*shards, *rows)


SUM_MOVES = ((0, 1),) + tuple((axis, steps) for axis in (1, 2, 3) for steps in (1, 2, 3))


MQP = 224
VMEM_BYTES = 60 * 1024 * 1024


def normed_rows(values, gain, offset):
    centered = values - jnp.mean(values, axis=-1, keepdims=True)
    inverse = lax.rsqrt(jnp.mean(centered * centered, axis=-1, keepdims=True) + LN_EPS)
    scaled = centered * inverse
    return scaled * gain + offset, scaled, inverse


def affine_rows(ref):
    return ref[0, 0].astype(WIDE_TYPE).T[0:8]


def norm_pull(upstream, scaled, inverse, gain):
    inner = upstream * gain
    return inverse * (
        inner
        - jnp.mean(inner, axis=-1, keepdims=True)
        - scaled * jnp.mean(inner * scaled, axis=-1, keepdims=True)
    )


def inner_high(left_side, right_side):
    dims = (((0,), (0,)), ((), ()))
    return lax.dot_general(left_side, right_side, dims, precision=lax.Precision.HIGHEST)


def row_sum(values):
    return jnp.sum(values, axis=0, keepdims=True)


def attention_forward_kernel(
    ready, all_ref, own_ref, keys_ref, own_ids_ref, affine_ref, w_ref,
    first_ref, low_all_ref, low_own_ref, joint_ref, query_ref, mass_ref, merged_ref,
    total,
):
    head_set = pl.program_id(0)

    @pl.when(head_set == 0)
    def _():
        affine = affine_rows(affine_ref)
        gain, offset = affine[0:1], affine[1:2]
        low_all_ref[:ready] = (all_ref[:ready] * gain + offset).astype(LOW_TYPE)
        if ready < all_ref.shape[0]:
            low_all_ref[ready:] = normed_rows(all_ref[ready:], gain, offset)[0].astype(LOW_TYPE)
        low_own_ref[...] = normed_rows(own_ref[...], gain, offset)[0].astype(LOW_TYPE)
        total[...] = own_ref[...] + affine[4:5]

    weights = w_ref[0, 0]
    joint = matmul_low(low_all_ref[...], weights[:, :384]).astype(LOW_TYPE)
    query = matmul_low(low_own_ref[...], weights[:, 384:])[:, :192].astype(LOW_TYPE)
    joint_ref[0] = joint
    query_ref[0] = query
    allowed = keys_ref[...] == own_ids_ref[...]
    parts = []
    for head in range(3):
        key = joint[:, HD * head : HD * (head + 1)]
        value = joint[:, 192 + HD * head : 192 + HD * (head + 1)]
        scores = outer_rows(key, query[:, HD * head : HD * (head + 1)]) * SCALE
        scores = jnp.where(allowed, scores, -1e30)
        peak = jnp.max(scores, axis=0, keepdims=True)
        exponent = jnp.exp(scores - peak)
        mass = row_sum(exponent)
        probability = (exponent * (1.0 / mass)).astype(LOW_TYPE)
        mass_ref[0, head : head + 1] = peak + jnp.log(mass)
        parts.append(inner_rows(value, probability))
    merged = jnp.concatenate(parts, axis=0).T.astype(LOW_TYPE)
    merged_ref[0] = merged
    total[...] += outer_rows(merged, weights[:, 576:])

    @pl.when(head_set == 3)
    def _():
        first_ref[...] = total[...]


def attention_forward_late_kernel(ready, *refs):
    tables = (None, *refs[17:21])
    total, send_sems, recv_sems = refs[21:]
    head_set = pl.program_id(0)

    def step(name):
        return late_copies(tables, send_sems, recv_sems, name)

    @pl.when(head_set == 0)
    def _():
        greet(mesh_place(), RING_MOVES)
        for batch in step("first"):
            for copy in batch:
                copy.start()

    @pl.when(head_set == 3)
    def _():
        for came, onward, across in zip(step("first"), step("second"), step("cross_first")):
            for copy in came:
                copy.wait_recv()
            for copy in onward + across:
                copy.start()

    attention_forward_kernel(ready, *refs[:6], *refs[10:17], total)

    @pl.when(head_set == 3)
    def _():
        second = step("second")
        for came, across in zip(second, step("cross_second")):
            for copy in came:
                copy.wait_recv()
            for copy in across:
                copy.start()
        for batch in step("first") + second:
            for copy in batch:
                copy.wait_send()
        for batch in step("cross_first") + step("cross_second"):
            for copy in batch:
                copy.wait()


def attention_backward_kernel(
    ready, role_ref, grad_ref, all_ref, inverse_ref, own_ref, keys_ref, own_ids_ref, affine_ref, w_ref,
    low_all_ref, low_own_ref, joint_ref, query_ref, mass_ref, merged_ref, affine_two_ref,
    left_all_ref, left_own_ref,
    mine_ref, theirs_ref, tail_grad_ref, small_ref,
    branch, all_sum, own_sum,
):
    head_set = pl.program_id(0)

    @pl.when(head_set == 0)
    def _():
        branch[...] = grad_ref[...].astype(LOW_TYPE)
        all_sum[...] = jnp.zeros_like(all_sum)
        own_sum[...] = jnp.zeros_like(own_sum)

    weights = w_ref[0, 0]
    joint = joint_ref[0]
    query = query_ref[0]
    branch_grad = branch[...]
    merged_grad = matmul_low(branch_grad, weights[:, 576:]).astype(LOW_TYPE)
    grad_out = inner_rows(branch_grad, merged_ref[0])
    allowed = keys_ref[...] == own_ids_ref[...]
    key_grads, value_grads, query_grads = [], [], []
    for head in range(3):
        key = joint[:, HD * head : HD * (head + 1)]
        value = joint[:, 192 + HD * head : 192 + HD * (head + 1)]
        one_query = query[:, HD * head : HD * (head + 1)]
        one_merged = merged_grad[:, HD * head : HD * (head + 1)]
        scores = jnp.where(allowed, outer_rows(key, one_query) * SCALE, -1e30)
        probability = jnp.exp(scores - mass_ref[0, head : head + 1])
        value_grads.append(matmul_low(probability.astype(LOW_TYPE), one_merged))
        weighted = probability * outer_rows(value, one_merged)
        score_grad = (weighted - probability * row_sum(weighted)).astype(LOW_TYPE)
        key_grads.append(matmul_low(score_grad, one_query) * SCALE)
        query_grads.append(inner_rows(key, score_grad) * SCALE)
    joint_grad = jnp.concatenate(key_grads + value_grads, axis=1).astype(LOW_TYPE)
    query_grad = jnp.concatenate(query_grads, axis=0).T.astype(LOW_TYPE)
    all_sum[...] += outer_rows(joint_grad, weights[:, :384])
    own_sum[...] += outer_rows(query_grad, weights[:, 384:576])
    grad_joint = inner_rows(low_all_ref[...], joint_grad)
    grad_rest = jnp.concatenate([inner_rows(low_own_ref[...], query_grad), grad_out], axis=1)
    first_core = role_ref[0] == 0
    mine_ref[:, :, 0] = jnp.where(first_core, grad_joint, grad_rest).reshape(4, 4, 48, 384)
    theirs = jnp.where(first_core, grad_rest, grad_joint).astype(LOW_TYPE)
    theirs_ref[:, :, 0] = theirs.reshape(4, 4, 48, 384)

    @pl.when(head_set == 3)
    def _():
        gain = affine_rows(affine_ref)[0:1]
        scaled = all_ref[:ready]
        upstream = all_sum[:ready]
        all_grad = norm_pull(upstream, scaled, inverse_ref[...], gain)
        gain_grad = row_sum(upstream * scaled)
        offset_grad = row_sum(upstream)
        tail_grad = all_grad
        if ready < all_ref.shape[0]:
            upstream = all_sum[ready:]
            _, scaled, inverse = normed_rows(all_ref[ready:], gain, gain)
            tail_grad = norm_pull(upstream, scaled, inverse, gain)
            gain_grad += row_sum(upstream * scaled)
            offset_grad += row_sum(upstream)
        tail_grad_ref[...] = tail_grad
        _, scaled, inverse = normed_rows(own_ref[...], gain, gain)
        own_grad = norm_pull(own_sum[...], scaled, inverse, gain) + grad_ref[...]
        if ready == all_ref.shape[0]:
            small_ref[...] = inner_high(left_all_ref[...], all_grad) + inner_high(
                left_own_ref[...], own_grad
            )
        else:
            small_ref[...] = jnp.zeros_like(small_ref)
            small_ref[17:18] = row_sum(all_grad) + row_sum(own_grad)
        small_ref[18:19] = gain_grad + row_sum(own_sum[...] * scaled)
        small_ref[19:20] = offset_grad + row_sum(own_sum[...])
        small_ref[20:22] = affine_two_ref[0:2]
        small_ref[22:23] = row_sum(grad_ref[...])
        small_ref[23:24] = affine_two_ref[2:3]


def feed_forward_kernel(first_ref, affine_ref, up_ref, down_ref, out_ref, low_ref, before_ref, total):
    part = pl.program_id(0)

    @pl.when(part == 0)
    def _():
        first = first_ref[...]
        affine = affine_rows(affine_ref)
        low_ref[...] = normed_rows(first, affine[2:3], affine[3:4])[0].astype(LOW_TYPE)
        total[...] = first + affine[5:6]

    before = matmul_low(low_ref[...], up_ref[0, 0])
    before_ref[0] = before
    acted = before * (0.5 * (1.0 + lax.erf(before * (1.0 / math.sqrt(2.0)))))
    total[...] += outer_rows(acted.astype(LOW_TYPE), down_ref[0, 0])

    @pl.when(part == 3)
    def _():
        out_ref[...] = total[...].astype(LOW_TYPE)


def feed_backward_kernel(
    role_ref, grad_ref, first_ref, low_ref, before_ref, affine_ref, up_ref, down_ref,
    up_mine_ref, up_theirs_ref, down_mine_ref, down_theirs_ref, first_grad_ref, affine_grad_ref,
    down_grad, total,
):
    part = pl.program_id(0)

    @pl.when(part == 0)
    def _():
        down_grad[...] = grad_ref[...].astype(LOW_TYPE)
        total[...] = jnp.zeros_like(total)

    first_core = role_ref[0] == 0

    def give(values, mine_ref, theirs_ref):
        lower, upper = values[:, :384], values[:, 384:]
        mine_ref[:, :, 0] = jnp.where(first_core, lower, upper).reshape(4, 4, 48, 384)
        theirs = jnp.where(first_core, upper, lower).astype(LOW_TYPE)
        theirs_ref[:, :, 0] = theirs.reshape(4, 4, 48, 384)

    before = before_ref[0]
    half = 0.5 * (1.0 + lax.erf(before * (1.0 / math.sqrt(2.0))))
    acted = (before * half).astype(LOW_TYPE)
    give(inner_rows(down_grad[...], acted), down_mine_ref, down_theirs_ref)
    slope = half + before * jnp.exp(-0.5 * before * before) * (1.0 / math.sqrt(2.0 * math.pi))
    before_grad = (matmul_low(down_grad[...], down_ref[0, 0]) * slope).astype(LOW_TYPE)
    give(inner_rows(low_ref[...], before_grad), up_mine_ref, up_theirs_ref)
    total[...] += outer_rows(before_grad, up_ref[0, 0])

    @pl.when(part == 3)
    def _():
        gain = affine_rows(affine_ref)[2:3]
        _, scaled, inverse = normed_rows(first_ref[...], gain, gain)
        first_grad_ref[...] = grad_ref[...] + norm_pull(total[...], scaled, inverse, gain)
        affine_grad_ref[0:1] = row_sum(total[...] * scaled)
        affine_grad_ref[1:2] = row_sum(total[...])
        affine_grad_ref[2:3] = row_sum(grad_ref[...])
        affine_grad_ref[3:8] = jnp.zeros((5, D), WIDE_TYPE)


def whole(shape):
    return pl.BlockSpec(shape, lambda part: (0,) * len(shape))


def weight_spec(which, column):
    return pl.BlockSpec((1, 1, D, D), lambda part: (which, part, 0, column))


def affine_spec(which):
    return pl.BlockSpec((1, 1, D, 128), lambda part: (which, 0, 0, 18))


def part_spec(*shape):
    return pl.BlockSpec((1,) + shape, lambda part: (part,) + (0,) * len(shape))


GRAD_SPEC = pl.BlockSpec((4, 4, 1, 48, 384), lambda part: (0, 0, part, 0, 0))
GRAD_WIDE = jax.ShapeDtypeStruct((4, 4, 4, 48, 384), WIDE_TYPE)
GRAD_LOW = jax.ShapeDtypeStruct((4, 4, 4, 48, 384), LOW_TYPE)
ROLE_SPEC = pl.BlockSpec(memory_space=pltpu.SMEM)


def cost(flops, moved_bytes):
    return pl.CostEstimate(flops=flops, bytes_accessed=moved_bytes, transcendentals=0)


def wide(*shape):
    return jax.ShapeDtypeStruct(shape, WIDE_TYPE)


def narrow(*shape):
    return jax.ShapeDtypeStruct(shape, LOW_TYPE)


def grid_call(kernel, in_specs, out_specs, out_shape, scratch, price, name):
    return pl.pallas_call(
        kernel,
        grid=(4,),
        in_specs=in_specs,
        out_specs=out_specs,
        out_shape=out_shape,
        scratch_shapes=scratch,
        compiler_params=pltpu.CompilerParams(
            dimension_semantics=("arbitrary",), vmem_limit_bytes=VMEM_BYTES
        ),
        cost_estimate=price,
        name=name,
    )


def block_forward(rows_all, inverse_all, rows_own, keys, own_ids, blocks, which, tables=None):
    total, count, ready = rows_all.shape[0], rows_own.shape[0], inverse_all.shape[0]
    saved_specs = (
        whole((total, D)), whole((count, D)), part_spec(total, 384), part_spec(count, 192),
        part_spec(3, count), part_spec(count, 192),
    )
    in_specs = [
        whole((total, D)), whole((count, D)), whole((total, 1)), whole((1, count)),
        affine_spec(which), weight_spec(which, 0),
    ]
    out_specs = (whole((count, D)),) + saved_specs
    out_shape = (
        wide(count, D), narrow(total, D), narrow(count, D), narrow(4, total, 384),
        narrow(4, count, 192), wide(4, 3, count), narrow(4, count, 192),
    )
    price = cost(2 * total * D * 2 * D + 24 * total * count * 256, 20 * total * D)
    operands = (rows_all, rows_own, keys, own_ids, blocks, blocks)
    if tables is None:
        first, *saved = grid_call(
            functools.partial(attention_forward_kernel, ready), in_specs, out_specs, out_shape,
            [pltpu.VMEM((count, D), WIDE_TYPE)], price, "attention_forward",
        )(*operands)
    else:
        late = pl.BlockSpec(memory_space=pl.ANY)
        first, *saved = pl.pallas_call(
            functools.partial(attention_forward_late_kernel, ready),
            grid=(4,),
            in_specs=in_specs + [late] * 4,
            out_specs=out_specs + (late,) * 4,
            out_shape=out_shape + tuple(narrow(*item.shape) for item in tables),
            input_output_aliases={6 + index: 7 + index for index in range(4)},
            scratch_shapes=[
                pltpu.VMEM((count, D), WIDE_TYPE),
                pltpu.SemaphoreType.DMA((LATE_COPIES,)),
                pltpu.SemaphoreType.DMA((LATE_COPIES,)),
            ],
            compiler_params=pltpu.CompilerParams(
                dimension_semantics=("arbitrary",),
                vmem_limit_bytes=VMEM_BYTES,
                collective_id=2,
                has_side_effects=True,
            ),
            cost_estimate=price,
            name="attention_and_gather",
        )(*operands, *tables)
        saved, tables = saved[:6], saved[6:]
    result, low_two, before = grid_call(
        feed_forward_kernel,
        [whole((count, D)), affine_spec(which), weight_spec(which, 1), weight_spec(which, 2)],
        (whole((count, D)), whole((count, D)), part_spec(count, D)),
        (narrow(count, D), narrow(count, D), wide(4, count, D)),
        [pltpu.VMEM((count, D), WIDE_TYPE)],
        cost(4 * count * D * FF, 4 * D * FF),
        "feed_forward",
    )(first, blocks, blocks, blocks)
    kept = (rows_all, inverse_all, rows_own, keys, own_ids, saved, first, low_two, before)
    return result, kept, tables


def block_backward(upstream, kept, blocks, which, role_array, left_all, left_own):
    rows_all, inverse_all, rows_own, keys, own_ids, saved, first, low_two, before = kept
    total, count, ready = rows_all.shape[0], rows_own.shape[0], inverse_all.shape[0]
    up_mine, up_theirs, down_mine, down_theirs, first_grad, affine_two = grid_call(
        feed_backward_kernel,
        [
            ROLE_SPEC, whole((count, D)), whole((count, D)), whole((count, D)),
            part_spec(count, D), affine_spec(which), weight_spec(which, 1), weight_spec(which, 2),
        ],
        (GRAD_SPEC,) * 4 + (whole((count, D)), whole((8, D))),
        (GRAD_WIDE, GRAD_LOW, GRAD_WIDE, GRAD_LOW, wide(count, D), wide(8, D)),
        [pltpu.VMEM((count, D), LOW_TYPE), pltpu.VMEM((count, D), WIDE_TYPE)],
        cost(8 * count * D * FF, 16 * D * FF),
        "feed_backward",
    )(role_array, upstream, first, low_two, before, blocks, blocks, blocks)
    mine, theirs, tail_grad, small = grid_call(
        functools.partial(attention_backward_kernel, ready),
        [
            ROLE_SPEC, whole((count, D)), whole((total, D)), whole((ready, 1)), whole((count, D)),
            whole((total, 1)), whole((1, count)), affine_spec(which), weight_spec(which, 0),
            whole((total, D)), whole((count, D)), part_spec(total, 384), part_spec(count, 192),
            part_spec(3, count), part_spec(count, 192), whole((8, D)), whole((VCAP, 24)),
            whole((VQ, 24)),
        ],
        (GRAD_SPEC, GRAD_SPEC, whole((VCAP, D)), whole((24, D))),
        (GRAD_WIDE, GRAD_LOW, wide(VCAP, D), wide(24, D)),
        [
            pltpu.VMEM((count, D), LOW_TYPE),
            pltpu.VMEM((total, D), WIDE_TYPE),
            pltpu.VMEM((count, D), WIDE_TYPE),
        ],
        cost(4 * total * D * 2 * D + 24 * total * count * 640, 30 * total * D),
        "attention_backward",
    )(
        role_array, first_grad, rows_all, inverse_all, rows_own, keys, own_ids, blocks, blocks, *saved,
        affine_two, left_all, left_own,
    )
    mine_all = (mine, up_mine, down_mine)
    theirs_all = (theirs, up_theirs, down_theirs)
    grads = list(zip(mine_all, theirs_all))
    return tail_grad, grads, small


B_FIRST = (True, False, True)
FAMILIES = (("blk", "head"), ("blk", "head"), ("blk", "head", "ext"))
UNITS = tuple((third, stream) for stream in (0, 1) for third in range(3))
NAMES = {
    unit: [name for name in FAMILIES[unit[0]] if (name == "blk") == (unit[1] == 1)] for unit in UNITS
}
TAILS = {"blk": (2, 48, 384), "head": (24, 1024), "ext": (8, 128)}
REDUCE_COPIES = 384
SMALL_ROWS = 32


def reduce_kernel(*refs):
    mine, theirs, ext = refs[0:9], refs[9:18], refs[18]
    enc_small, dec_small, loss = refs[19:22]
    kept_out, taken_out, head_out, ext_out, small_out, norm_out = refs[22:28]
    crossed = refs[28:38]
    scratch = list(refs[38:])
    third_refs = [dict() for _ in range(3)]
    for third in range(3):
        for name in FAMILIES[third]:
            third_refs[third][name] = {
                key: scratch.pop(0)
                for key in ("pool", "give", "rest", "come", "last", "b_come", "b_last", "c_come", "c_last")
            }
    pool_low = [{name: scratch.pop(0) for name in FAMILIES[third]} for third in range(3)]
    hand, small_held, small_slots, norm_held, norm_slots = scratch[:5]
    send_sems, recv_sems, load_sems = scratch[5:]
    place = mesh_place()
    used = [0, 0]
    flying = []

    def push(source, target, axis, steps):
        slot = used[0]
        used[0] += 1
        copy = pltpu.make_async_remote_copy(
            src_ref=source,
            dst_ref=target,
            send_sem=send_sems.at[slot],
            recv_sem=recv_sems.at[slot],
            device_id=mesh_device(moved(place, axis, steps)),
            device_id_type=pl.DeviceIdType.MESH,
        )
        copy.start()
        flying.append(copy)
        return copy

    def sent(copies):
        for copy in copies:
            copy.wait_send()
            flying[:] = [other for other in flying if other is not copy]

    def load(source, target):
        copy = pltpu.make_async_copy(source, target, load_sems.at[used[1]])
        used[1] += 1
        copy.start()
        return copy

    def half_spans(third, steps, half):
        first, second, _ = ORDERS[third]
        spans = [slice(None)] * 3
        spans[first - 1] = lax.rem(place[first] + steps + 4, 4)
        spans[second - 1] = pl.ds(2 * half, 2)
        return spans

    def arrays(unit):
        third, stream = unit
        group, low = third_refs[third], pool_low[third]
        if stream == 1:
            for block in range(2):
                index = 3 * block + third
                pools = group["blk"]["pool"].at[:, :, block], low["blk"].at[:, :, block]
                yield mine[index], theirs[index], crossed[index], *pools
            return
        index = 6 + third
        yield mine[index], theirs[index], crossed[index], group["head"]["pool"], low["head"]
        if third == 2:
            given = ext.at[1 - place[0]]
            yield ext.at[place[0]], given, crossed[9], group["ext"]["pool"], low["ext"]

    def cross(unit, steps, half):
        spans = half_spans(unit[0], steps, half)
        crossing[unit, steps, half] = [
            push(given.at[*spans], landed.at[*spans], 0, 1)
            for _, given, landed, _, _ in arrays(unit)
        ]

    def fetch(unit, steps, half):
        spans = half_spans(unit[0], steps, half)
        spot = lead(unit[0], pl.ds(2 * half, 2), slice(None))
        copies = []
        for crossed_copy, (kept, _, landed, pool, low) in zip(
            crossing[unit, steps, half], arrays(unit)
        ):
            copies.append(load(kept.at[*spans], pool.at[*spot]))
            crossed_copy.wait_recv()
            copies.append(load(landed.at[*spans], low.at[*spot]))
        return copies

    def lead(third, b, c):
        return (b, c) if B_FIRST[third] else (c, b)

    def values(third, name, b, c):
        spot = lead(third, b, c)
        total = third_refs[third][name]["pool"][spot]
        return total + pool_low[third][name][spot].astype(WIDE_TYPE)

    def halves(unit, half, body):
        def step(count, carry):
            inner, c = lax.div(count, 4), lax.rem(count, 4)
            for name in NAMES[unit]:
                body(name, inner, c, 2 * half + inner)
            return carry

        lax.fori_loop(0, 8, step, 0)

    def small_stage(held, slots, stage):
        axis = (0, 3, 1, 2)[stage]
        count = 2 if axis == 0 else 4
        copies = [
            push(held.at[stage], slots.at[stage, place[axis]], axis, steps)
            for steps in range(1, count)
        ]
        slots[stage, place[axis]] = held[stage]

        def finish():
            for copy in copies:
                copy.wait_recv()
            total = slots[stage, 0]
            for index in range(1, count):
                total = total + slots[stage, index]
            held[stage + 1] = total

        return finish

    def arrive(copies):
        for copy in copies:
            copy.wait()

    def received(copies):
        for copy in copies:
            copy.wait_recv()

    def both(unit, *steps):
        return [fetch(unit, step, half) for half, step in enumerate(steps)]

    greet(place, SUM_MOVES)
    crossing = {}
    for pair in ((2, 2), (-1, 1), (1, -1), (0, 0)):
        for unit in UNITS:
            for half in (0, 1):
                cross(unit, pair[half], half)
    loads = {}

    def ahead(low_steps, high_steps):
        loads[UNITS[0]] = both(UNITS[0], low_steps, high_steps)
        for unit, later in zip(UNITS, UNITS[1:] + (None,)):
            if later is not None:
                loads[later] = both(later, low_steps, high_steps)
            yield unit

    small_held[0, 0:24] = enc_small[...]
    small_held[0, 0:18] += dec_small[0:18]
    small_held[0, 24:30] = dec_small[18:24]
    small_held[0, 30:32] = jnp.concatenate([loss[0:2]] * 6, axis=1)
    small = small_stage(small_held, small_slots, 0)

    first, last = ({unit: [] for unit in UNITS} for _ in range(2))
    for unit in ahead(2, 2):
        third = unit[0]
        group = third_refs[third]
        for half in (0, 1):
            arrive(loads[unit][half])

            def give(name, inner, c, b, half=half, third=third, unit=unit, group=group):
                total = values(third, name, b, c).astype(LOW_TYPE)
                group[name]["give"][half, inner, c] = total

            halves(unit, half, give)
            first[unit].append(
                [
                    push(
                        group[name]["give"].at[half],
                        group[name]["come"].at[half],
                        ORDERS[third][0],
                        1 - 2 * half,
                    )
                    for name in NAMES[unit]
                ]
            )
    small()
    small = small_stage(small_held, small_slots, 1)

    for unit in ahead(-1, 1):
        third = unit[0]
        group = third_refs[third]
        for way in (1, 0):
            arrive(loads[unit][1 - way])

            def keep(name, inner, c, b, way=way, third=third, unit=unit, group=group):
                group[name]["rest"][way, inner, c] = values(third, name, b, c).astype(LOW_TYPE)

            halves(unit, 1 - way, keep)
            for name in NAMES[unit]:
                refs_of = group[name]
                source, target = refs_of["rest"].at[way], refs_of["last"].at[way, 1 - way]
                last[unit].append(push(source, target, ORDERS[third][0], 1 - 2 * way))
    small()
    small = small_stage(small_held, small_slots, 2)
    for unit in ahead(1, -1):
        third = unit[0]
        group = third_refs[third]
        for way in (0, 1):
            arrive(loads[unit][way])
            received(first[unit][way])

            def join(name, inner, c, b, way=way, third=third, unit=unit, group=group):
                total = values(third, name, b, c)
                total = total + group[name]["come"][way, inner, c].astype(WIDE_TYPE)
                group[name]["come"][way, inner, c] = total.astype(LOW_TYPE)

            halves(unit, way, join)
            for name in NAMES[unit]:
                refs_of = group[name]
                source, target = refs_of["come"].at[way], refs_of["last"].at[way, way]
                last[unit].append(push(source, target, ORDERS[third][0], 1 - 2 * way))
    small()
    small = small_stage(small_held, small_slots, 3)

    second, ready = ({unit: [] for unit in UNITS} for _ in range(2))
    for unit in ahead(0, 0):
        third = unit[0]
        axis = ORDERS[third][1]
        group = third_refs[third]
        received(last[unit])
        for half in (0, 1):
            arrive(loads[unit][half])

            def total_up(name, inner, c, b, half=half, third=third, unit=unit, group=group):
                total = values(third, name, b, c)
                for way in (0, 1):
                    total = total + group[name]["last"][way, half, inner, c].astype(WIDE_TYPE)
                group[name]["pool"][lead(third, b, c)] = total

            halves(unit, half, total_up)
            sent(first[unit][half])

        def pack(b, spot, start, third=third, unit=unit, group=group):
            for name in NAMES[unit]:
                refs_of = group[name]
                for c in (start, start + 1):
                    total = refs_of["pool"][lead(third, b, c)]
                    refs_of["give"][(*spot, c)] = total.astype(LOW_TYPE)

        opposite = lax.rem(place[axis] + 2, 4)
        for way in (0, 1):
            pack(opposite, (0, 0), 2 * way)
            second[unit].append(
                [
                    push(
                        group[name]["give"].at[0, 0, pl.ds(2 * way, 2)],
                        group[name]["b_come"].at[way],
                        axis,
                        1 - 2 * way,
                    )
                    for name in NAMES[unit]
                ]
            )
        for way, spot in ((0, (0, 1)), (1, (1, 0))):
            steps = 1 - 2 * way
            pack(lax.rem(place[axis] + steps + 4, 4), spot, 2 - 2 * way)
            part = pl.ds(2 - 2 * way, 2)
            for name in NAMES[unit]:
                refs_of = group[name]
                source, target = refs_of["give"].at[*spot, part], refs_of["b_last"].at[way, part]
                ready[unit].append(push(source, target, axis, steps))
    small()
    small_out[...] = small_held[4]
    for unit in UNITS:
        third = unit[0]
        axis = ORDERS[third][1]
        group = third_refs[third]
        for way, spot in ((0, (0, 1)), (1, (1, 0))):
            steps = 1 - 2 * way
            b = lax.rem(place[axis] + steps + 4, 4)
            received(second[unit][way])
            part = pl.ds(2 * way, 2)
            for name in NAMES[unit]:
                refs_of = group[name]
                for inner in range(2):
                    c = 2 * way + inner
                    total = refs_of["pool"][lead(third, b, c)]
                    total = total + refs_of["b_come"][way, inner].astype(WIDE_TYPE)
                    refs_of["give"][(*spot, c)] = total.astype(LOW_TYPE)
                source, target = refs_of["give"].at[*spot, part], refs_of["b_last"].at[way, part]
                ready[unit].append(push(source, target, axis, steps))

    second, last = ({unit: [] for unit in UNITS} for _ in range(2))
    for unit in UNITS:
        third = unit[0]
        axis = ORDERS[third][2]
        own_b = place[ORDERS[third][1]]
        group = third_refs[third]
        received(ready[unit])
        for name in NAMES[unit]:
            refs_of = group[name]
            for c in range(4):
                total = refs_of["pool"][lead(third, own_b, c)]
                for way in (0, 1):
                    total = total + refs_of["b_last"][way, c].astype(WIDE_TYPE)
                refs_of["pool"][lead(third, own_b, c)] = total
        pieces = c_pieces(unit)
        spot = lead(third, own_b, lax.rem(place[axis] + 2, 4))
        for way in (0, 1):
            second[unit].append(
                [
                    push(
                        group[name]["pool"].at[(*spot, *piece)],
                        group[name]["c_come"].at[piece],
                        axis,
                        1 - 2 * way,
                    )
                    for name, piece in pieces[way]
                ]
            )
        for way in (0, 1):
            steps = 1 - 2 * way
            spot = lead(third, own_b, lax.rem(place[axis] + steps + 4, 4))
            for name, piece in pieces[1 - way]:
                source = group[name]["pool"].at[(*spot, *piece)]
                target = group[name]["c_last"].at[(way, *piece)]
                last[unit].append(push(source, target, axis, steps))
    for unit in UNITS:
        third = unit[0]
        axis = ORDERS[third][2]
        own_b = place[ORDERS[third][1]]
        group = third_refs[third]
        pieces = c_pieces(unit)
        for way in (0, 1):
            steps = 1 - 2 * way
            spot = lead(third, own_b, lax.rem(place[axis] + steps + 4, 4))
            received(second[unit][way])
            for name, piece in pieces[way]:
                refs_of = group[name]
                refs_of["pool"][(*spot, *piece)] += refs_of["c_come"][piece]
                source = refs_of["pool"].at[(*spot, *piece)]
                target = refs_of["c_last"].at[(way, *piece)]
                last[unit].append(push(source, target, axis, steps))
    squares_sum = jnp.zeros((), WIDE_TYPE)
    handed = []
    for unit in UNITS:
        third = unit[0]
        axis = ORDERS[third][2]
        spot = lead(third, place[ORDERS[third][1]], place[axis])
        for copy in last[unit]:
            copy.wait_recv()
        for name in NAMES[unit]:
            refs_of = third_refs[third][name]
            total = refs_of["pool"][spot] + (refs_of["c_last"][0] + refs_of["c_last"][1])
            refs_of["pool"][spot] = total
            squares_sum += jnp.sum(total * total)
            if name == "head":
                head_out[third] = total
            if name == "ext":
                ext_out[...] = total
        if unit[1] == 0:
            continue
        blk = third_refs[third]["blk"]["pool"]
        handed.append(push(blk.at[(*spot, 1 - place[0])], hand.at[third], 0, 1))
        kept_out[third] = blk[(*spot, place[0])]
    small_total = small_held[4, 0:30]
    squares_sum += jnp.sum(small_total * small_total) * (1.0 / 128.0)
    norm_held[0] = jnp.full((8, 128), squares_sum)
    for stage in range(4):
        small_stage(norm_held, norm_slots, stage)()
    norm_out[...] = norm_held[4]
    for copy in handed:
        copy.wait_recv()
    taken_out[...] = hand[...]
    for copy in list(flying):
        copy.wait_send()


def c_pieces(unit):
    everything = slice(None)
    if unit[1] == 1:
        return [("blk", (0,))], [("blk", (1,))]
    lower = [("head", (everything, pl.ds(0, 512)))]
    upper = [("head", (everything, pl.ds(512, 512)))]
    if unit[0] == 2:
        lower.append(("ext", (everything, everything)))
    return lower, upper


def reduce_gradients(mine, theirs, ext, enc_small, dec_small, loss):
    scratch = []
    for third in range(3):
        for name in FAMILIES[third]:
            tail = TAILS[name]
            scratch += [
                pltpu.VMEM((4, 4) + tail, WIDE_TYPE),
                pltpu.VMEM((2, 2, 4) + tail, LOW_TYPE),
                pltpu.VMEM((2, 2, 4) + tail, LOW_TYPE),
                pltpu.VMEM((2, 2, 4) + tail, LOW_TYPE),
                pltpu.VMEM((2, 2, 2, 4) + tail, LOW_TYPE),
                pltpu.VMEM((2, 2) + tail, LOW_TYPE),
                pltpu.VMEM((2, 4) + tail, LOW_TYPE),
                pltpu.VMEM(tail, WIDE_TYPE),
                pltpu.VMEM((2,) + tail, WIDE_TYPE),
            ]
    for third in range(3):
        for name in FAMILIES[third]:
            kind = WIDE_TYPE if name == "ext" else LOW_TYPE
            scratch.append(pltpu.VMEM((4, 4) + TAILS[name], kind))
    scratch += [
        pltpu.VMEM((3, 48, 384), WIDE_TYPE),
        pltpu.VMEM((5, SMALL_ROWS, D), WIDE_TYPE),
        pltpu.VMEM((4, 4, SMALL_ROWS, D), WIDE_TYPE),
        pltpu.VMEM((5, 8, 128), WIDE_TYPE),
        pltpu.VMEM((4, 4, 8, 128), WIDE_TYPE),
        pltpu.SemaphoreType.DMA((REDUCE_COPIES,)),
        pltpu.SemaphoreType.DMA((REDUCE_COPIES,)),
        pltpu.SemaphoreType.DMA((256,)),
    ]
    held = pl.BlockSpec(memory_space=pltpu.VMEM)
    return pl.pallas_call(
        reduce_kernel,
        out_shape=(
            wide(3, 48, 384),
            wide(3, 48, 384),
            wide(3, 24, 1024),
            wide(8, 128),
            wide(SMALL_ROWS, D),
            wide(8, 128),
        )
        + (narrow(4, 4, 4, 48, 384),) * 6
        + (narrow(4, 4, 4, 24, W),) * 3
        + (wide(4, 4, 4, 8, 128),),
        in_specs=[pl.BlockSpec(memory_space=pl.ANY)] * 19 + [held] * 3,
        out_specs=(held,) * 6 + (pl.BlockSpec(memory_space=pl.ANY),) * 10,
        scratch_shapes=scratch,
        compiler_params=pltpu.CompilerParams(
            collective_id=1, has_side_effects=True, vmem_limit_bytes=REDUCE_VMEM
        ),
        name="reduce_gradients",
    )(*mine, *theirs, ext, enc_small, dec_small, loss)[:6]


REDUCE_VMEM = 63 * 1024 * 1024


def silu_pair(values):
    gate = lax.logistic(values)
    return (values * gate).astype(LOW_TYPE), gate * (1.0 + values * (1.0 - gate))


def plain_rows(values):
    centered = values - jnp.mean(values, axis=-1, keepdims=True)
    inverse = lax.rsqrt(jnp.mean(centered * centered, axis=-1, keepdims=True) + LN_EPS)
    return centered * inverse, inverse


def plain_pull(upstream, scaled, inverse):
    return inverse * (
        upstream
        - jnp.mean(upstream, axis=-1, keepdims=True)
        - scaled * jnp.mean(upstream * scaled, axis=-1, keepdims=True)
    )


def slot_share(tables):
    lane = lax.broadcasted_iota(jnp.int32, (1, W), 1)
    one_each = ((lane & 31) == 0) & (lane < W // 2)
    counts = [0.0, 0.0]
    for slot in range(2):
        masked = jnp.where(
            one_each, 32.0 * tables[64 + slot : 65 + slot] + tables[66 + slot : 67 + slot], 0.0
        )
        bucket = tables[68 + slot : 69 + slot]
        counts[0] += jnp.sum(masked * (1.0 - bucket), axis=1, keepdims=True)
        counts[1] += jnp.sum(masked * bucket, axis=1, keepdims=True)
    own = lane == lax.axis_index("dp") * 32
    first = lax.axis_index("mp") < 2
    bucket = jnp.sum(
        jnp.where(own, jnp.where(first, tables[68:69], tables[69:70]), 0.0), axis=1, keepdims=True
    )
    return jnp.where(bucket == 1.0, BUCKET_SHARE[1] / counts[1], BUCKET_SHARE[0] / counts[0])


def head_kernel(
    condition_ref, noisy_ref, features_ref, noise_ref, valid_ref, entry_in, square_in,
    modulate_in, extra_ref,
    cond_grad_ref, time_grad_ref, one_grad_ref, two_grad_ref, mod_grad_ref,
    time_act_ref, mod_in_ref, hidden_act_ref, cond_act_ref, decoded_grad_ref, extra_grad_ref,
    loss_ref,
    modulation, tables, extra_rows, pulled, entry_ref, square_ref, modulate_ref, load_sems,
):
    parts = [(entry_in, entry_ref)]
    parts += [(square_in.at[index], square_ref.at[index]) for index in range(3)]
    spans = [pl.ds(W * part, W) for part in range(5)]
    parts += [(modulate_in.at[span], modulate_ref.at[span]) for span in spans]
    loads = [
        pltpu.make_async_copy(source, target, load_sems.at[index])
        for index, (source, target) in enumerate(parts)
    ]
    for index in (0, 1, 4, 5, 6, 7, 8, 2, 3):
        loads[index].start()
    tables[...] = extra_ref[...].astype(WIDE_TYPE).T
    table_in = tables[0:C].astype(LOW_TYPE)
    table_out = tables[C : 2 * C].astype(LOW_TYPE)

    def bias(index):
        return tables[2 * C + index : 2 * C + index + 1]

    condition = condition_ref[...]
    loads[0].wait()
    time_pre = outer_rows(features_ref[...], entry_ref[:, D:]) + bias(1)
    time_act, time_slope = silu_pair(time_pre)
    time_act_ref[...] = time_act
    cond_pre = outer_rows(condition, entry_ref[:, :D]) + bias(0)
    loads[1].wait()
    cond_pre = cond_pre + (outer_rows(time_act, square_ref[0]) + bias(2))
    cond_act, cond_slope = silu_pair(cond_pre)
    cond_act_ref[...] = cond_act

    def modulate(part, carry):
        span = pl.ds(pl.multiple_of(W * part, W), W)
        pltpu.make_async_copy(
            modulate_in.at[span], modulate_ref.at[span], load_sems.at[4 + part]
        ).wait()
        rows = modulate_ref[pl.ds(pl.multiple_of(W * part, W), W)]
        offset = tables[pl.ds(2 * C + 6 + part, 1)]
        modulation[part] = outer_rows(cond_act_ref[...], rows) + offset
        return carry

    lax.fori_loop(0, 5, modulate, 0)
    entry_x = matmul_low(noisy_ref[...], table_in) + bias(3)
    scaled_in, inverse_in = plain_rows(entry_x)
    mod_in = (scaled_in * (1.0 + modulation[1]) + modulation[0]).astype(LOW_TYPE)
    mod_in_ref[...] = mod_in
    loads[2].wait()
    hidden_one = outer_rows(mod_in, square_ref[1]) + bias(4)
    hidden_act, hidden_slope = silu_pair(hidden_one)
    hidden_act_ref[...] = hidden_act
    loads[3].wait()
    hidden_two = outer_rows(hidden_act, square_ref[2]) + bias(5)
    leaving = entry_x + modulation[2] * hidden_two
    scaled_out, inverse_out = plain_rows(leaving)
    mod_out = (scaled_out * (1.0 + modulation[4]) + modulation[3]).astype(LOW_TYPE)
    error = outer_rows(mod_out, table_out) - noise_ref[...]
    weight = valid_ref[...] * slot_share(tables)
    row_loss = jnp.mean(error * error, axis=1, keepdims=True)
    loss_ref[...] = jnp.full((8, 128), jnp.sum(weight * row_loss))
    pred_grad = (weight * (2.0 / C) * error).astype(LOW_TYPE)
    extra_rows[...] = jnp.zeros_like(extra_rows)
    extra_rows[C : 2 * C] = inner_rows(pred_grad, mod_out)
    mod_out_grad = matmul_low(pred_grad, table_out)
    leaving_grad = plain_pull(mod_out_grad * (1.0 + modulation[4]), scaled_out, inverse_out)

    def give_mod(part, values):
        low = values.astype(LOW_TYPE)
        mod_grad_ref[:, W * part : W * (part + 1)] = low
        row = 2 * C + 6 + part
        extra_rows[row : row + 1] = row_sum(low.astype(WIDE_TYPE))

    def bias_grad(index, low):
        row = 2 * C + index
        extra_rows[row : row + 1] = row_sum(low.astype(WIDE_TYPE))

    give_mod(3, mod_out_grad)
    give_mod(4, mod_out_grad * scaled_out)
    give_mod(2, leaving_grad * hidden_two)
    two_grad = (leaving_grad * modulation[2]).astype(LOW_TYPE)
    two_grad_ref[...] = two_grad
    bias_grad(5, two_grad)
    one_grad = (matmul_low(two_grad, square_ref[2]) * hidden_slope).astype(LOW_TYPE)
    one_grad_ref[...] = one_grad
    bias_grad(4, one_grad)
    mod_in_grad = matmul_low(one_grad, square_ref[1])
    give_mod(0, mod_in_grad)
    give_mod(1, mod_in_grad * scaled_in)
    entry_x_grad = plain_pull(mod_in_grad * (1.0 + modulation[1]), scaled_in, inverse_in)
    entry_x_grad = (entry_x_grad + leaving_grad).astype(LOW_TYPE)
    bias_grad(3, entry_x_grad)
    extra_rows[0:C] = inner_rows(noisy_ref[...], entry_x_grad)
    pulled[...] = jnp.zeros_like(pulled)

    def pull(part, carry):
        start = pl.multiple_of(W * part, W)
        pulled[...] += matmul_low(mod_grad_ref[:, pl.ds(start, W)], modulate_ref[pl.ds(start, W)])
        return carry

    lax.fori_loop(0, 5, pull, 0)
    cond_grad = (pulled[...] * cond_slope).astype(LOW_TYPE)
    cond_grad_ref[...] = cond_grad
    bias_grad(0, cond_grad)
    bias_grad(2, cond_grad)
    decoded_grad = matmul_low(cond_grad, entry_ref[:, :D]).astype(LOW_TYPE)
    decoded_grad_ref[...] = decoded_grad.astype(WIDE_TYPE)
    time_grad = (matmul_low(cond_grad, square_ref[0]) * time_slope).astype(LOW_TYPE)
    time_grad_ref[...] = time_grad
    bias_grad(1, time_grad)
    extra_grad_ref[...] = extra_rows[...].T


def head_grad_kernel(role_ref, *refs):
    mine_of, theirs_of = refs[0:5], refs[5:10]
    time_act, mod_in, hidden_act, cond_act, condition, features = [ref[...] for ref in refs[10:16]]
    mine_out, theirs_out = refs[16:19], refs[19:22]
    for grads, outs, kind in ((mine_of, mine_out, WIDE_TYPE), (theirs_of, theirs_out, LOW_TYPE)):
        cond_grad, time_grad, one_grad, two_grad, mod_grad = [ref[...] for ref in grads]

        def rows(left, right):
            product = inner_rows(left, right)
            return product.reshape(16, product.shape[0] // 16, product.shape[1])

        def put(out, pieces):
            joined = jnp.concatenate(pieces, axis=1).astype(kind)
            out[0] = joined.reshape(4, 4, 24, W)

        put(
            outs[0],
            [rows(cond_grad, time_act), rows(one_grad, mod_in), rows(two_grad, hidden_act)],
        )
        mod_rows = rows(mod_grad, cond_act)
        entry = jnp.concatenate([rows(cond_grad, condition), rows(time_grad, features)], axis=2)
        put(outs[1], [mod_rows[:, :24]])
        put(outs[2], [mod_rows[:, 24:], entry])


HEAD_PARTS = (128, 128, 128, 128, 640)


def head_step(condition, noisy, features, noise_rows, valid, tables, role_array):
    entry, squares, modulate, extras = tables
    rows = condition.shape[0]
    held = pl.BlockSpec(memory_space=pltpu.VMEM)
    outs = pl.pallas_call(
        head_kernel,
        out_shape=(
            narrow(rows, W), narrow(rows, W), narrow(rows, W), narrow(rows, W),
            narrow(rows, 5 * W),
            narrow(rows, W), narrow(rows, W), narrow(rows, W), narrow(rows, W),
            wide(rows, D), wide(W, 128), wide(8, 128),
        ),
        in_specs=[held] * 5 + [pl.BlockSpec(memory_space=pl.ANY)] * 3 + [held],
        out_specs=(held,) * 12,
        scratch_shapes=[
            pltpu.VMEM((5, rows, W), WIDE_TYPE),
            pltpu.VMEM((128, W), WIDE_TYPE),
            pltpu.VMEM((128, W), WIDE_TYPE),
            pltpu.VMEM((rows, W), WIDE_TYPE),
            pltpu.VMEM((W, W), LOW_TYPE),
            pltpu.VMEM((3, W, W), LOW_TYPE),
            pltpu.VMEM((5 * W, W), LOW_TYPE),
            pltpu.SemaphoreType.DMA((9,)),
        ],
        compiler_params=pltpu.CompilerParams(vmem_limit_bytes=VMEM_BYTES),
        cost_estimate=cost(4 * rows * W * 9 * W, 20 * W * W),
        name="head_step",
    )(condition, noisy, features, noise_rows, valid, entry, squares, modulate, extras)
    grads, inputs = outs[:5], outs[5:9]
    decoded_grad, extra_grad, loss = outs[9:]

    def half(width, other):
        def index(plane, role_ref):
            return (0, (jnp.abs(role_ref[0] - other)) * 4 + plane)

        return pl.BlockSpec((rows, width), index)

    def full(width):
        return pl.BlockSpec((rows, width), lambda plane, role_ref: (0, 0))

    out_spec = pl.BlockSpec((1, 4, 4, 24, W), lambda plane, role_ref: (plane, 0, 0, 0, 0))
    sums = pl.pallas_call(
        head_grad_kernel,
        grid_spec=pltpu.PrefetchScalarGridSpec(
            num_scalar_prefetch=1,
            grid=(4,),
            in_specs=[half(width, 0) for width in HEAD_PARTS]
            + [half(width, 1) for width in HEAD_PARTS]
            + [full(W)] * 4
            + [full(D), full(FREQ)],
            out_specs=(out_spec,) * 6,
        ),
        out_shape=(wide(4, 4, 4, 24, W),) * 3 + (narrow(4, 4, 4, 24, W),) * 3,
        compiler_params=pltpu.CompilerParams(
            dimension_semantics=("arbitrary",), vmem_limit_bytes=VMEM_BYTES
        ),
        cost_estimate=cost(2 * rows * W * 9 * W, 60 * W * W),
        name="head_gradients",
    )(role_array, *grads, *grads, *inputs, condition, features)
    pairs = list(zip(sums[:3], sums[3:]))
    return loss, pairs, extra_grad, decoded_grad


def adam_kernel(*refs):
    kept_ref, taken_ref, head_ref, ext_ref, small_ref, norm_ref = refs[:6]
    params, firsts, seconds = refs[6:15], refs[15:24], refs[24:33]
    outs, (loss_out, norm_out) = refs[33:60], refs[60:]
    role, dp_index = lax.axis_index("role"), lax.axis_index("dp")
    norm = jnp.sqrt(norm_ref[0:1, 0:1])
    factor = jnp.minimum(1.0, CLIP_NORM / (norm + 1e-06))
    norm_out[0, 0] = jnp.sum(norm)
    loss_out[0, 0] = jnp.sum(small_ref[30:31, 0:1])

    def update(index, grad, at=()):
        spot = at if at else (Ellipsis,)
        scaled = factor * grad
        first = BETA_ONE * firsts[index][spot] + (1.0 - BETA_ONE) * scaled
        second = BETA_TWO * seconds[index][spot] + (1.0 - BETA_TWO) * scaled * scaled
        weight = params[index][spot]
        first_hat = first * (1.0 / (1.0 - BETA_ONE**STEP))
        second_hat = second * (1.0 / (1.0 - BETA_TWO**STEP))
        outs[3 * index][spot] = first
        outs[3 * index + 1][spot] = second
        outs[3 * index + 2][spot] = weight - RATE * (
            first_hat / (jnp.sqrt(second_hat) + ADAM_EPS) + DECAY * weight
        )

    first_core = role == 0
    lower = [jnp.where(first_core, kept_ref[part], taken_ref[part]) for part in range(3)]
    upper = [jnp.where(first_core, taken_ref[part], kept_ref[part]) for part in range(3)]
    update(0, small_ref[0 : C + 2])
    for head in range(3):
        spans = [slice(HD * head, HD * (head + 1)), slice(192 + HD * head, 192 + HD * (head + 1))]
        pieces = [upper[0][:, spans[0]], lower[0][:, spans[0]], lower[0][:, spans[1]]]
        update(1, jnp.concatenate(pieces, axis=1), (head,))
    update(2, upper[0][:, 192:])
    update(3, jnp.concatenate([lower[1], upper[1]], axis=1))
    update(4, jnp.concatenate([lower[2], upper[2]], axis=1))
    rows = jnp.where(first_core, small_ref[18:24], small_ref[24:30])
    column = lax.broadcasted_iota(jnp.int32, (D, 48), 0)
    wanted = lax.broadcasted_iota(jnp.int32, (D, 48), 1) + dp_index * 48
    rows = matmul_high(rows, (column == wanted).astype(WIDE_TYPE))
    for row in range(6):
        update(5, rows[row : row + 1], (row,))
    entry = jnp.concatenate([head_ref[2, 16:24], ext_ref[...]], axis=1)
    update(6, entry[:, :HE])
    for part in range(3):
        update(7, head_ref[0, 8 * part : 8 * part + 8], (part,))
    update(8, jnp.concatenate([head_ref[1], head_ref[2, 0:16]], axis=0))


def adam_all(sums, params, firsts, seconds):
    held = pl.BlockSpec(memory_space=pltpu.VMEM)
    return pl.pallas_call(
        adam_kernel,
        out_shape=tuple(wide(*item.shape) for item in params for _ in range(3)) + (wide(1, 1),) * 2,
        in_specs=[held] * 33,
        out_specs=(held,) * 27 + (pl.BlockSpec(memory_space=pltpu.SMEM),) * 2,
        compiler_params=pltpu.CompilerParams(vmem_limit_bytes=VMEM_BYTES),
        name="adam",
    )(*sums, *params, *firsts, *seconds)


def per_device(
    latents,
    noise_draws,
    timesteps,
    buckets,
    visible_index,
    patch_embed,
    patch_embed_first,
    patch_embed_second,
    attention_in,
    attention_in_first,
    attention_in_second,
    attention_out,
    attention_out_first,
    attention_out_second,
    feedforward_in,
    feedforward_in_first,
    feedforward_in_second,
    feedforward_out,
    feedforward_out_first,
    feedforward_out_second,
    block_affine,
    block_affine_first,
    block_affine_second,
    head_entry,
    head_entry_first,
    head_entry_second,
    head_square,
    head_square_first,
    head_square_second,
    head_modulate,
    head_modulate_first,
    head_modulate_second,
):
    role = lax.axis_index("role")
    mp_index = lax.axis_index("mp")
    shards = (
        attention_in[0].transpose(1, 0, 2),
        attention_out[0].T,
        feedforward_in[0],
        feedforward_out[0].T,
        block_affine[0],
        head_square.transpose(0, 2, 1),
        head_entry.T,
        head_modulate.T,
    )
    blocks, squares_all, entry_all, modulate_all, extras, *rows = gather_weights(
        shards,
        (
            patch_embed,
            latents.transpose(0, 2, 1),
            noise_draws.transpose(0, 2, 1),
            kept_signal(timesteps),
            buckets.T,
            visible_index,
            position_table(),
            time_tables(),
        ),
    )
    (
        embedded, embedded_own, enc_keys, enc_ids, dec_rows, dec_rows_own, dec_keys, dec_ids,
        noisy_input, features, noise_rows, valid, enc_left, enc_left_own, enc_inverse, dec_inverse,
    ) = rows
    blocks = blocks.reshape(2, 4, D, BLOCK_COLS)
    role_array = jnp.reshape(role, (1,)).astype(jnp.int32)
    encoded, enc_kept, _ = block_forward(
        embedded, enc_inverse, embedded_own, enc_keys, enc_ids, blocks, 0
    )
    parity = mp_index % 2
    other = send(encoded, neighbour_pairs())
    pair = jnp.where(parity == 0, jnp.stack([encoded, other]), jnp.stack([other, encoded]))
    across = send(pair, partner_pairs())
    received = jnp.where(role == 0, jnp.stack([pair, across], 1), jnp.stack([across, pair], 1))
    received = received.reshape(VCAP, D).astype(WIDE_TYPE)
    dec_rows = dec_rows.at[MCAP:].add(received)
    condition, dec_kept, tables = block_forward(
        dec_rows, dec_inverse, dec_rows_own, dec_keys, dec_ids, blocks, 1,
        (squares_all, entry_all, modulate_all, extras),
    )
    squares_all, entry_all, modulate_all, extras = tables
    tables = (
        entry_all.reshape(W, SEQ),
        squares_all.reshape(3, W, W),
        modulate_all.reshape(5 * W, W),
        extras.reshape(W, 128),
    )
    loss_local, head_grads, extra_grad, decoded_grad = head_step(
        condition, noisy_input, features, noise_rows, valid, tables, role_array
    )
    extra_grad = extra_grad.reshape(2, 4, 4, 4, 8, 128)
    visible_grad, dec_grads, dec_small = block_backward(
        decoded_grad, dec_kept, blocks, 1, role_array, enc_left, enc_left_own
    )
    visible_grad = visible_grad.reshape(2, 2, VQ, D)
    summed = pick(visible_grad, role, 1) + send(pick(visible_grad, 1 - role, 1), partner_pairs())
    came = send(pick(summed, 1 - parity, 0).astype(LOW_TYPE), neighbour_pairs())
    returned = pick(summed, parity, 0) + came.astype(WIDE_TYPE)
    returned = returned.astype(LOW_TYPE).astype(WIDE_TYPE)
    _, enc_grads, enc_small = block_backward(
        returned, enc_kept, blocks, 0, role_array, enc_left, enc_left_own
    )
    pairs = enc_grads + dec_grads + head_grads
    *sums, square_total = reduce_gradients(
        [pair[0] for pair in pairs],
        [pair[1] for pair in pairs],
        extra_grad,
        enc_small,
        dec_small,
        loss_local,
    )

    def flat(arrays):
        patch, joint, branch, up, down, affine, entry, square, modulate = arrays
        return (
            patch,
            joint[0].transpose(1, 0, 2),
            branch[0].T,
            up[0],
            down[0].T,
            affine.transpose(1, 0, 2),
            entry.T,
            square.transpose(0, 2, 1),
            modulate.T,
        )

    def restored(arrays):
        patch, joint, branch, up, down, affine, entry, square, modulate = arrays
        return (
            patch,
            joint.transpose(1, 0, 2)[None],
            branch.T[None],
            up[None],
            down.T[None],
            affine.transpose(1, 0, 2),
            entry.T,
            square.transpose(0, 2, 1),
            modulate.T,
        )

    params = (
        patch_embed,
        attention_in,
        attention_out,
        feedforward_in,
        feedforward_out,
        block_affine,
        head_entry,
        head_square,
        head_modulate,
    )
    firsts = (
        patch_embed_first,
        attention_in_first,
        attention_out_first,
        feedforward_in_first,
        feedforward_out_first,
        block_affine_first,
        head_entry_first,
        head_square_first,
        head_modulate_first,
    )
    seconds = (
        patch_embed_second,
        attention_in_second,
        attention_out_second,
        feedforward_in_second,
        feedforward_out_second,
        block_affine_second,
        head_entry_second,
        head_square_second,
        head_modulate_second,
    )
    *updated, loss_total, grad_norm = adam_all(
        (*sums, square_total), flat(params), flat(firsts), flat(seconds)
    )
    loss_total, grad_norm = loss_total[0, 0], grad_norm[0, 0]
    updated = [restored(updated[part::3]) for part in range(3)]
    news = [updated[part][index] for index in range(9) for part in range(3)]
    return (
        loss_total,
        grad_norm,
        news[0],
        news[1],
        news[2],
        news[3],
        news[4],
        news[5],
        news[6],
        news[7],
        news[8],
        news[9],
        news[10],
        news[11],
        news[12],
        news[13],
        news[14],
        news[15],
        news[16],
        news[17],
        news[18],
        news[19],
        news[20],
        news[21],
        news[22],
        news[23],
        news[24],
        news[25],
        news[26],
    )


def solution(mesh):
    placed = (
        P(None, "dp", None),
        P(None, "dp", None),
        P(None, "dp"),
        P(None, "dp"),
        P(None, "dp"),
        P(),
        P(),
        P(),
        P("role", "dp", "mp", None),
        P("role", "dp", "mp", None),
        P("role", "dp", "mp", None),
        P("role", "mp", "dp"),
        P("role", "mp", "dp"),
        P("role", "mp", "dp"),
        P("role", "dp", "mp"),
        P("role", "dp", "mp"),
        P("role", "dp", "mp"),
        P("role", "mp", "dp"),
        P("role", "mp", "dp"),
        P("role", "mp", "dp"),
        P("role", None, "dp"),
        P("role", None, "dp"),
        P("role", None, "dp"),
        P(None, ("role", "dp", "mp")),
        P(None, ("role", "dp", "mp")),
        P(None, ("role", "dp", "mp")),
        P(None, None, ("role", "dp", "mp")),
        P(None, None, ("role", "dp", "mp")),
        P(None, None, ("role", "dp", "mp")),
        P(None, ("role", "dp", "mp")),
        P(None, ("role", "dp", "mp")),
        P(None, ("role", "dp", "mp")),
    )
    return jax.shard_map(
        per_device,
        mesh=mesh,
        in_specs=placed,
        out_specs=(
            P(),
            P(),
            P(),
            P(),
            P(),
            P("role", "dp", "mp", None),
            P("role", "dp", "mp", None),
            P("role", "dp", "mp", None),
            P("role", "mp", "dp"),
            P("role", "mp", "dp"),
            P("role", "mp", "dp"),
            P("role", "dp", "mp"),
            P("role", "dp", "mp"),
            P("role", "dp", "mp"),
            P("role", "mp", "dp"),
            P("role", "mp", "dp"),
            P("role", "mp", "dp"),
            P("role", None, "dp"),
            P("role", None, "dp"),
            P("role", None, "dp"),
            P(None, ("role", "dp", "mp")),
            P(None, ("role", "dp", "mp")),
            P(None, ("role", "dp", "mp")),
            P(None, None, ("role", "dp", "mp")),
            P(None, None, ("role", "dp", "mp")),
            P(None, None, ("role", "dp", "mp")),
            P(None, ("role", "dp", "mp")),
            P(None, ("role", "dp", "mp")),
            P(None, ("role", "dp", "mp")),
        ),
        check_vma=False,
    )
```
